32 devices in a mesh: dp: 16 (over z, y, core), tensor: 2 (over x).
Axes of the slice: x: 2, y: 2, z: 4, core: 2. Of those that a mesh axis runs over, the one named last changes fastest.
Arguments:
- target: bfloat16 [32768, 1024], P(('dp', 'tensor')), may hold values from -6 to 6
- memory: bfloat16 [32768, 1024], P(('dp', 'tensor')), may hold values from -6 to 6
- mem_len: int32 [32], P('dp'), may hold values from 512 to 1024, as said below
- grad_out: bfloat16 [32768, 1024], P(('dp', 'tensor')), may hold values from -6 to 6
- self_qkv: bfloat16 [3, 1024, 1024], P(None, None, 'tensor'), may hold values from -0.3125 to 0.3125
- self_out: bfloat16 [1024, 1024], P('tensor'), may hold values from -3 to 3
- cross_query: bfloat16 [1024, 1024], P(None, 'tensor'), may hold values from -0.3125 to 0.3125
- cross_kv: bfloat16 [2, 1024, 1024], P(None, None, 'tensor'), may hold values from -0.3125 to 0.3125
- cross_out: bfloat16 [1024, 1024], P('tensor'), may hold values from -3 to 3
- ffn_up: bfloat16 [1024, 4096], P(None, 'tensor'), may hold values from -0.1875 to 0.1875
- ffn_down: bfloat16 [4096, 1024], P('tensor'), may hold values from -0.75 to 0.75
- ln_gain: float32 [3, 1024], replicated, may hold values from 0.5 to 1.5
- ln_bias: float32 [3, 1024], replicated, may hold values from -3 to 3
Outputs:
- output: bfloat16 [32768, 1024], P(('dp', 'tensor'))
- grad_target: bfloat16 [32768, 1024], P(('dp', 'tensor'))
- grad_memory: bfloat16 [32768, 1024], P(('dp', 'tensor'))
- grad_self_qkv: float32 [3, 1024, 1024], P(None, None, 'tensor')
- grad_self_out: float32 [1024, 1024], P('tensor')
- grad_cross_query: float32 [1024, 1024], P(None, 'tensor')
- grad_cross_kv: float32 [2, 1024, 1024], P(None, None, 'tensor')
- grad_cross_out: float32 [1024, 1024], P('tensor')
- grad_ffn_up: float32 [1024, 4096], P(None, 'tensor')
- grad_ffn_down: float32 [4096, 1024], P('tensor')
- grad_ln_gain: float32 [3, 1024], replicated
- grad_ln_bias: float32 [3, 1024], replicated
The draws below stay inside these ranges and needn't reach their ends.
Inputs may be any that keep to these rules, and one draw needn't show every extreme that they name: Queries of pair p read memory rows 0 to mem_len[p] - 1 of that pair; some pair reads all 1024 and some pair exactly half.
All inputs are finite; a program needn't handle non-finite values.
Results may differ from the reference program's by a relative error of at most 0.038.
The reference program's roundings to bfloat16 on the way count: a program that leaves them out, or rounds other values in their place, can miss the bound.
Values may be sent and summed in bfloat16 or wider, within the bound.
A program may use at most 320 MiB of HBM per device.

```python
import math
from functools import partial
import jax
import jax.numpy as jnp
from jax import lax

D = 1024
HEADS = 16
HD = 64
FF = 4096
SEQ = 1024
PAIRS = 32
TOKENS = 32768


def draw_mem_len(key, part):
    key = jax.random.fold_in(key, 11)
    key_len, key_pick = jax.random.split(key)
    lengths = jax.random.randint(key_len, (PAIRS,), SEQ // 2, SEQ + 1)
    shuffled = jax.random.permutation(key_pick, PAIRS)
    lengths = lengths.at[shuffled[0]].set(SEQ)
    lengths = lengths.at[shuffled[1]].set(SEQ // 2)
    return lengths.astype(jnp.int32)


def block_scale(own_key, shape, pieces, smallest, top_value):
    gain, own = 1.0, jax.random.fold_in(own_key, 6)
    for position, shards_of in pieces:
        heights = jnp.exp(jax.random.uniform(jax.random.fold_in(own, position), (shards_of,), jnp.float32, smallest / len(pieces), top_value / len(pieces)))
        gain = gain * jnp.repeat(heights, shape[position] // shards_of).reshape([-1 if axis == position else 1 for axis in range(len(shape))])
    return gain


def noise(stream_key, shape, width, most, cuts=(), held_as=jnp.bfloat16):
    level = block_scale(stream_key, shape, cuts, -0.22, 0.18) if cuts else 1.0
    drawn = jax.random.normal(stream_key, shape, jnp.float32) * width * level
    return jnp.minimum(jnp.maximum(drawn, -most), most).astype(held_as)


def setup_inputs(seed: int = 0) -> dict:
    keys = jax.random.split(jax.random.key(seed), 14)
    return {
        "target": noise(keys[0], (TOKENS, D), 1.0, 6.0, ((0, 32),)),
        "memory": noise(keys[1], (TOKENS, D), 1.0, 6.0, ((0, 32),)),
        "mem_len": draw_mem_len(jax.random.fold_in(keys[13], 71), 0),
        "grad_out": noise(keys[3], (TOKENS, D), 1.0, 6.0, ((0, 32),)),
        "self_qkv": noise(keys[4], (3, D, D), (D // 3) ** -0.5, 0.3125, ((2, 2),)),
        "self_out": noise(keys[5], (D, D), (max(4, D // 256)) ** -0.5, 3.0, ((0, 2),)),
        "cross_query": noise(keys[6], (D, D), (D // 3) ** -0.5, 0.3125, ((1, 2),)),
        "cross_kv": noise(keys[7], (2, D, D), (D // 3) ** -0.5, 0.3125, ((2, 2),)),
        "cross_out": noise(keys[8], (D, D), (max(4, D // 256)) ** -0.5, 3.0, ((0, 2),)),
        "ffn_up": noise(keys[9], (D, FF), D ** -0.5, 0.1875, ((1, 2),)),
        "ffn_down": noise(keys[10], (FF, D), (max(1, FF // 64)) ** -0.5, 0.75, ((0, 2),)),
        "ln_gain": jnp.clip(1.0 + 0.1 * jax.random.normal(keys[11], (3, D), jnp.float32), 0.5, 1.5),
        "ln_bias": noise(keys[12], (3, D), 0.5, 3.0, (), jnp.float32),
    }


@jax.custom_vjp
def low(v):
    return lax.optimization_barrier(v.astype(jnp.bfloat16)).astype(jnp.float32)

@jax.custom_vjp
def low_back(v):
    return v

def low_keep(v):
    return (low(v), None)

def low_pass(kept, grad):
    return (grad,)

def back_keep(v):
    return (v, None)

def back_low(kept, grad):
    return (low(grad),)
low.defvjp(low_keep, low_pass)
low_back.defvjp(back_keep, back_low)
alpha_res = 300.0 ** 0.25
norm_eps = 1e-05
highest = lax.Precision.HIGHEST

def matmul_hi(left_mat, right_mat):
    return jnp.dot(left_mat, right_mat, precision=highest)

def norm_rows(resid, gain_vec, bias_vec):
    average = lax.optimization_barrier(jnp.mean(resid, axis=-1, keepdims=True))
    centered = resid - average
    variance = lax.optimization_barrier(jnp.mean(centered * centered, axis=-1, keepdims=True))
    return centered * lax.rsqrt(variance + norm_eps) * gain_vec + bias_vec

def attend_pair(packed, causal):
    queries, key_rows, value_rows, key_len = packed
    queries = queries.reshape(SEQ, HEADS, HD)
    key_rows = key_rows.reshape(SEQ, HEADS, HD)
    value_rows = value_rows.reshape(SEQ, HEADS, HD)
    scores = low_back(jnp.einsum('qhd,khd->hqk', queries, key_rows, precision=highest) * HD ** (-0.5))
    key_pos = jnp.arange(SEQ, dtype=jnp.int32)[None, :]
    query_pos = jnp.arange(SEQ, dtype=jnp.int32)[:, None]
    allowed = key_pos < key_len
    if causal:
        allowed = allowed & (key_pos <= query_pos)
    scores = jnp.where(allowed[None], scores, -1e+30)
    attn_prob = low(jax.nn.softmax(scores, axis=-1))
    context = low_back(low(jnp.einsum('hqk,khd->qhd', attn_prob, value_rows, precision=highest)))
    return context.reshape(SEQ, D)

def attention(queries, key_rows, value_rows, key_lens, causal):
    pair_count = key_lens.shape[0]
    shaped = [tensor_in.reshape(pair_count, SEQ, D) for tensor_in in (queries, key_rows, value_rows)]
    pair_fn = jax.checkpoint(partial(attend_pair, causal=causal))
    context = lax.map(pair_fn, (shaped[0], shaped[1], shaped[2], key_lens))
    return context.reshape(pair_count * SEQ, D)

def decoder_layer(target_rows, memory_rows, key_lens, self_qkv, self_out, cross_query, cross_kv, cross_out, ffn_up, ffn_down, ln_gain, ln_bias):
    full_lens = jnp.full(key_lens.shape, SEQ, jnp.int32)
    projected = [low_back(low(matmul_hi(target_rows, self_qkv[member]))) for member in range(3)]
    context_one = attention(projected[0], projected[1], projected[2], full_lens, True)
    branch_one = low_back(matmul_hi(context_one, self_out))
    normed_one = norm_rows(alpha_res * target_rows + branch_one, ln_gain[0], ln_bias[0])
    query_two = low_back(low(matmul_hi(low(normed_one), cross_query)))
    key_two = low_back(low(matmul_hi(memory_rows, cross_kv[0])))
    value_two = low_back(low(matmul_hi(memory_rows, cross_kv[1])))
    context_two = attention(query_two, key_two, value_two, key_lens, False)
    branch_two = low_back(matmul_hi(context_two, cross_out))
    normed_two = norm_rows(alpha_res * normed_one + branch_two, ln_gain[1], ln_bias[1])
    hidden = low_back(matmul_hi(low(normed_two), ffn_up))
    activated = low(jax.nn.gelu(hidden, approximate=False))
    branch_three = low_back(matmul_hi(activated, ffn_down))
    return norm_rows(alpha_res * normed_two + branch_three, ln_gain[2], ln_bias[2])

def reference(target, memory, mem_len, grad_out, self_qkv, self_out, cross_query, cross_kv, cross_out, ffn_up, ffn_down, ln_gain, ln_bias):
    weights = tuple((tensor_in.astype(jnp.float32) for tensor_in in (self_qkv, self_out, cross_query, cross_kv, cross_out, ffn_up, ffn_down, ln_gain, ln_bias)))
    group_size = math.gcd(PAIRS, max(1, 4096 // SEQ))
    step_count = PAIRS // group_size

    def split_rows(array_in):
        return array_in.astype(jnp.float32).reshape(step_count, group_size * SEQ, D)

    def group_step(summed, packed):
        target_rows, memory_rows, key_lens, cotangent = packed

        def forward(target_in, memory_in, *params):
            return decoder_layer(target_in, memory_in, key_lens, *params)
        result, pullback = jax.vjp(forward, target_rows, memory_rows, *weights)
        gradients = pullback(cotangent)
        summed = tuple((before + added for before, added in zip(summed, gradients[2:])))
        return (summed, (result.astype(jnp.bfloat16), gradients[0].astype(jnp.bfloat16), gradients[1].astype(jnp.bfloat16)))
    initial = tuple((jnp.zeros(tensor_in.shape, jnp.float32) for tensor_in in weights))
    summed, (results, target_grads, memory_grads) = lax.scan(group_step, initial, (split_rows(target), split_rows(memory), mem_len.reshape(step_count, group_size), split_rows(grad_out)))
    return (results.reshape(TOKENS, D), target_grads.reshape(TOKENS, D), memory_grads.reshape(TOKENS, D), summed[0], summed[1], summed[2], summed[3], summed[4], summed[5], summed[6], summed[7], summed[8])
```

```python
import functools

import jax
import jax.numpy as jnp
from jax import lax
from jax.experimental import pallas as pl
from jax.experimental.pallas import tpu as pltpu
from jax.sharding import PartitionSpec as P

HD = 64


alpha_res = 300.0**0.25
norm_eps = 1e-05
mask_fill = -1e30
contract_rows = (((0,), (0,)), ((), ()))
contract_cols = (((1,), (1,)), ((), ()))


def norm_rows(resid, gain_vec, bias_vec):
    average = jnp.mean(resid, axis=-1, keepdims=True)
    centered = resid - average
    variance = jnp.mean(centered * centered, axis=-1, keepdims=True)
    return centered * lax.rsqrt(variance + norm_eps) * gain_vec + bias_vec


def exact_gelu(values_in):
    return jax.nn.gelu(values_in, approximate=False)


def gather_rows(local_rows):
    return lax.all_gather(local_rows, "tensor", axis=0, tiled=True)


def gather_grads(local_rows):
    return lax.all_gather(local_rows, "tensor", axis=0, tiled=True)


def scatter_branch(left_mat, right_mat, row_count):

    def partial_term(offset, num_rows):
        return jnp.dot(left_mat, right_mat, preferred_element_type=jnp.float32)

    return lax.psum_scatter(
        partial_term(jnp.int32(0), row_count * lax.axis_size("tensor")),
        "tensor",
        scatter_dimension=0,
        tiled=True,
    )


def project_context(context, weight_local, row_count):
    return scatter_branch(context, weight_local, row_count)


def scatter_inputs(factor_pairs, row_count):

    def partial_term(offset, num_rows):
        terms = [
            lax.dot_general(grad_mat, weight_mat, contract_cols, preferred_element_type=jnp.float32)
            for grad_mat, weight_mat in factor_pairs
        ]
        return sum(terms)

    return lax.psum_scatter(
        partial_term(jnp.int32(0), row_count * lax.axis_size("tensor")).astype(jnp.bfloat16),
        "tensor",
        scatter_dimension=0,
        tiled=True,
    ).astype(jnp.float32)


def block_view(flat, pair_count, block_rows):
    tok_count, col_count = flat.shape
    seq_len = tok_count // pair_count
    return flat.reshape(pair_count, seq_len // block_rows, block_rows, col_count // HD, HD)


def pair_view(flat, pair_count):
    tok_count, col_count = flat.shape
    return flat.reshape(pair_count, tok_count // pair_count, col_count // HD, HD)


def block_scores(query_blk, key_pair, start_row, key_len, causal):
    block_rows = query_blk.shape[0]
    seq_len = key_pair.shape[0]
    products = jnp.einsum(
        "qhd,khd->hqk", query_blk, key_pair, preferred_element_type=jnp.float32
    ) * HD ** (-0.5)
    key_pos = lax.broadcasted_iota(jnp.int32, (block_rows, seq_len), 1)
    query_pos = start_row + lax.broadcasted_iota(jnp.int32, (block_rows, seq_len), 0)
    allowed = key_pos < key_len
    if causal:
        allowed = allowed & (key_pos <= query_pos)
    return jnp.where(allowed[None], products, mask_fill)


def attend_forward(queries, key_rows, value_rows, key_lens, causal):
    pair_count = key_lens.shape[0]
    seq_len = queries.shape[0] // pair_count
    block_rows = min(512, seq_len)
    starts = lax.iota(jnp.int32, seq_len // block_rows) * block_rows

    def one_pair(packed):
        query_pair, key_pair, value_pair, key_len = packed

        def one_block(inner):
            query_blk, start_row = inner
            scores = block_scores(query_blk, key_pair, start_row, key_len, causal)
            row_max = jnp.max(scores, axis=-1, keepdims=True)
            shifted = jnp.exp(scores - row_max)
            row_total = jnp.sum(shifted, axis=-1, keepdims=True)
            attn_prob = (shifted / row_total).astype(jnp.bfloat16)
            context = jnp.einsum(
                "hqk,khd->qhd", attn_prob, value_pair, preferred_element_type=jnp.float32
            )
            return (context.astype(jnp.bfloat16), (row_max + jnp.log(row_total))[..., 0])

        return lax.map(one_block, (query_pair, starts))

    context, log_total = lax.map(
        one_pair,
        (
            block_view(queries, pair_count, block_rows),
            pair_view(key_rows, pair_count),
            pair_view(value_rows, pair_count),
            key_lens,
        ),
    )
    return (context.reshape(queries.shape), log_total)


def attend_backward(queries, key_rows, value_rows, key_lens, causal, log_total, grad_context):
    pair_count = key_lens.shape[0]
    seq_len = queries.shape[0] // pair_count
    block_rows = min(512, seq_len)
    starts = lax.iota(jnp.int32, seq_len // block_rows) * block_rows
    score_scale = HD ** (-0.5)

    def one_pair(packed):
        query_pair, key_pair, value_pair, key_len, total_pair, grad_pair = packed

        def one_block(carry, inner):
            key_grad, value_grad = carry
            query_blk, start_row, total_blk, grad_blk = inner
            scores = block_scores(query_blk, key_pair, start_row, key_len, causal)
            attn_prob = jnp.exp(scores - total_blk[..., None])
            value_grad = value_grad + jnp.einsum(
                "hqk,qhd->khd",
                attn_prob.astype(jnp.bfloat16),
                grad_blk,
                preferred_element_type=jnp.float32,
            )
            prob_grad = jnp.einsum(
                "qhd,khd->hqk", grad_blk, value_pair, preferred_element_type=jnp.float32
            )
            score_grad = (
                attn_prob * (prob_grad - jnp.sum(attn_prob * prob_grad, axis=-1, keepdims=True))
            ).astype(jnp.bfloat16)
            query_grad = (
                jnp.einsum("hqk,khd->qhd", score_grad, key_pair, preferred_element_type=jnp.float32)
                * score_scale
            )
            key_grad = (
                key_grad
                + jnp.einsum(
                    "hqk,qhd->khd", score_grad, query_blk, preferred_element_type=jnp.float32
                )
                * score_scale
            )
            return ((key_grad, value_grad), query_grad.astype(jnp.bfloat16))

        zeros = jnp.zeros(key_pair.shape, jnp.float32)
        (key_grad, value_grad), query_grad = lax.scan(
            one_block, (zeros, zeros), (query_pair, starts, total_pair, grad_pair)
        )
        return (query_grad, key_grad.astype(jnp.bfloat16), value_grad.astype(jnp.bfloat16))

    query_grad, key_grad, value_grad = lax.map(
        one_pair,
        (
            block_view(queries, pair_count, block_rows),
            pair_view(key_rows, pair_count),
            pair_view(value_rows, pair_count),
            key_lens,
            log_total,
            block_view(grad_context, pair_count, block_rows),
        ),
    )
    return (
        query_grad.reshape(queries.shape),
        key_grad.reshape(queries.shape),
        value_grad.reshape(queries.shape),
    )


def on_device(
    target,
    memory,
    mem_len,
    grad_out,
    self_qkv,
    self_out,
    cross_query,
    cross_kv,
    cross_out,
    ffn_up,
    ffn_down,
    ln_gain,
    ln_bias,
):
    row_count = target.shape[0]
    pair_count = mem_len.shape[0]
    seq_len = row_count * lax.axis_size("tensor") // pair_count
    full_lens = jnp.full((pair_count,), seq_len, jnp.int32)
    target_all = gather_rows(target)
    qkv_rows = jnp.einsum(
        "td,ide->ite", target_all, self_qkv, preferred_element_type=jnp.float32
    ).astype(jnp.bfloat16)
    context_one, total_one = attend_forward(qkv_rows[0], qkv_rows[1], qkv_rows[2], full_lens, True)
    branch_one = project_context(context_one, self_out, row_count)
    normed_one, norm_back_one = jax.vjp(
        norm_rows, alpha_res * target.astype(jnp.float32) + branch_one, ln_gain[0], ln_bias[0]
    )
    normed_one_all = gather_rows(normed_one.astype(jnp.bfloat16))
    memory_all = gather_rows(memory)
    query_two = jnp.dot(normed_one_all, cross_query, preferred_element_type=jnp.float32).astype(
        jnp.bfloat16
    )
    kv_two = jnp.einsum(
        "td,ide->ite", memory_all, cross_kv, preferred_element_type=jnp.float32
    ).astype(jnp.bfloat16)
    context_two, total_two = attend_forward(query_two, kv_two[0], kv_two[1], mem_len, False)
    branch_two = project_context(context_two, cross_out, row_count)
    normed_two, norm_back_two = jax.vjp(
        norm_rows, alpha_res * normed_one + branch_two, ln_gain[1], ln_bias[1]
    )
    normed_two_low = normed_two.astype(jnp.bfloat16)
    normed_two_all = gather_rows(normed_two_low)
    hidden = jnp.dot(normed_two_all, ffn_up, preferred_element_type=jnp.float32)
    activated, gelu_back = jax.vjp(exact_gelu, hidden)
    activated_low = activated.astype(jnp.bfloat16)
    branch_three = scatter_branch(activated_low, ffn_down, row_count)
    result, norm_back_three = jax.vjp(
        norm_rows, alpha_res * normed_two + branch_three, ln_gain[2], ln_bias[2]
    )
    grad_sum_three, gain_three, bias_three = norm_back_three(grad_out.astype(jnp.float32))
    branch_grad_three = gather_grads(grad_sum_three.astype(jnp.bfloat16))
    down_grad = lax.dot_general(
        activated_low, branch_grad_three, contract_rows, preferred_element_type=jnp.float32
    )
    act_grad = lax.dot_general(
        branch_grad_three, ffn_down, contract_cols, preferred_element_type=jnp.float32
    )
    hidden_grad = gelu_back(act_grad)[0].astype(jnp.bfloat16)
    up_grad = lax.dot_general(
        normed_two_all, hidden_grad, contract_rows, preferred_element_type=jnp.float32
    )
    normed_two_grad = alpha_res * grad_sum_three + scatter_inputs(
        ((hidden_grad, ffn_up),), row_count
    )
    grad_sum_two, gain_two, bias_two = norm_back_two(normed_two_grad)
    branch_grad_two = gather_grads(grad_sum_two.astype(jnp.bfloat16))
    cross_out_grad = lax.dot_general(
        context_two, branch_grad_two, contract_rows, preferred_element_type=jnp.float32
    )
    context_grad_two = lax.dot_general(
        branch_grad_two, cross_out, contract_cols, preferred_element_type=jnp.float32
    ).astype(jnp.bfloat16)
    query_grad_two, key_grad_two, value_grad_two = attend_backward(
        query_two, kv_two[0], kv_two[1], mem_len, False, total_two, context_grad_two
    )
    cross_query_grad = lax.dot_general(
        normed_one_all, query_grad_two, contract_rows, preferred_element_type=jnp.float32
    )
    cross_kv_grad = jnp.einsum(
        "td,ite->ide",
        memory_all,
        jnp.stack([key_grad_two, value_grad_two]),
        preferred_element_type=jnp.float32,
    )
    memory_grad = scatter_inputs(
        ((key_grad_two, cross_kv[0]), (value_grad_two, cross_kv[1])), row_count
    )
    normed_one_grad = alpha_res * grad_sum_two + scatter_inputs(
        ((query_grad_two, cross_query),), row_count
    )
    grad_sum_one, gain_one, bias_one = norm_back_one(normed_one_grad)
    branch_grad_one = gather_grads(grad_sum_one.astype(jnp.bfloat16))
    self_out_grad = lax.dot_general(
        context_one, branch_grad_one, contract_rows, preferred_element_type=jnp.float32
    )
    context_grad_one = lax.dot_general(
        branch_grad_one, self_out, contract_cols, preferred_element_type=jnp.float32
    ).astype(jnp.bfloat16)
    query_grad_one, key_grad_one, value_grad_one = attend_backward(
        qkv_rows[0], qkv_rows[1], qkv_rows[2], full_lens, True, total_one, context_grad_one
    )
    self_qkv_grad = jnp.einsum(
        "td,ite->ide",
        target_all,
        jnp.stack([query_grad_one, key_grad_one, value_grad_one]),
        preferred_element_type=jnp.float32,
    )
    target_grad = alpha_res * grad_sum_one + scatter_inputs(
        ((query_grad_one, self_qkv[0]), (key_grad_one, self_qkv[1]), (value_grad_one, self_qkv[2])),
        row_count,
    )
    (
        self_qkv_total,
        self_out_total,
        cross_query_total,
        cross_kv_total,
        cross_out_total,
        up_total,
        down_total,
    ) = (
        lax.psum(self_qkv_grad.astype(jnp.bfloat16), "dp").astype(jnp.float32),
        lax.psum(self_out_grad.astype(jnp.bfloat16), "dp").astype(jnp.float32),
        lax.psum(cross_query_grad.astype(jnp.bfloat16), "dp").astype(jnp.float32),
        lax.psum(cross_kv_grad.astype(jnp.bfloat16), "dp").astype(jnp.float32),
        lax.psum(cross_out_grad.astype(jnp.bfloat16), "dp").astype(jnp.float32),
        lax.psum(up_grad.astype(jnp.bfloat16), "dp").astype(jnp.float32),
        lax.psum(down_grad.astype(jnp.bfloat16), "dp").astype(jnp.float32),
    )
    gain_total, bias_total = lax.psum(
        (jnp.stack([gain_one, gain_two, gain_three]), jnp.stack([bias_one, bias_two, bias_three])),
        ("dp", "tensor"),
    )
    return (
        result.astype(jnp.bfloat16),
        target_grad.astype(jnp.bfloat16),
        memory_grad.astype(jnp.bfloat16),
        self_qkv_total,
        self_out_total,
        cross_query_total,
        cross_kv_total,
        cross_out_total,
        up_total,
        down_total,
        gain_total,
        bias_total,
    )


BLK = 256
f32 = jnp.float32
bf16 = jnp.bfloat16
NN = (((1,), (0,)), ((), ()))
NT = (((1,), (1,)), ((), ()))
TN = (((0,), (0,)), ((), ()))


def dot(a, b, dims=NN):
    return lax.dot_general(a, b, dims, preferred_element_type=f32)


def lanes(rows):
    return lax.broadcasted_iota(jnp.int32, (rows, 128), 1)


def place3(x, rows):
    hi = x.astype(bf16)
    rest = x - hi.astype(f32)
    mid = rest.astype(bf16)
    lo = (rest - mid.astype(f32)).astype(bf16)
    at = lanes(rows) % 64
    return jnp.where(at == 0, hi, jnp.where(at == 1, mid, jnp.where(at == 2, lo, jnp.zeros_like(hi))))


def fwd_kernel(causal, len_ref, *refs):
    if causal:
        qkv_ref, c_ref, lse_ref, kaug, vaug = refs
        q_ref, k2, v2 = qkv_ref.at[:, :128], qkv_ref[:, 128:256], qkv_ref[:, 256:]
    else:
        q_ref, kv_ref, c_ref, lse_ref, kaug, vaug = refs
        k2, v2 = kv_ref[:, :128], kv_ref[:, 128:]
    seq = k2.shape[0]
    lane = lanes(seq)
    zero = jnp.zeros_like(k2)
    if not causal:
        pos = lax.broadcasted_iota(jnp.int32, (seq, 128), 0)
        bias = jnp.where((pos >= len_ref[0]) & (lane == 0), -1e30, 0.0).astype(bf16)
    for h in range(2):
        own = (lane // 64) == h
        kaug[h, :, :128] = jnp.where(own, k2, zero)
        if not causal:
            kaug[h, :, 128:] = bias
        vaug[h, :, :128] = jnp.where(own, v2, zero)
        vaug[h, :, 128:] = jnp.where(own, jnp.ones_like(v2), zero)
    lb = lanes(BLK)
    for i in range(seq // BLK):
        rows = slice(i * BLK, (i + 1) * BLK)
        q = q_ref[rows, :] * jnp.asarray(HD**-0.5, bf16)
        if not causal:
            q = jnp.concatenate([q, jnp.where(lb == 0, 1.0, 0.0).astype(bf16)], axis=1)
        nk = (i + 1) * BLK if causal else seq
        acc = None
        ms = []
        for h in range(2):
            s = dot(q, kaug[h, :nk, :128] if causal else kaug[h], NT)
            if causal:
                a = lax.broadcasted_iota(jnp.int32, (BLK, BLK), 0)
                b = lax.broadcasted_iota(jnp.int32, (BLK, BLK), 1)
                d = jnp.where(b <= a, s[:, nk - BLK :], mask_fill)
                s = d if nk == BLK else jnp.concatenate([s[:, : nk - BLK], d], axis=1)
            m = jnp.max(s, axis=1, keepdims=True)
            p = jnp.exp(s - m).astype(bf16)
            o = dot(p, vaug[h, :nk])
            acc = o if acc is None else acc + o
            ms.append(m)
        total = acc[:, 128:]
        c_ref[rows, :] = (acc[:, :128] / total).astype(bf16)
        lse_ref[rows, :] = place3(-(jnp.where(lb < 64, ms[0], ms[1]) + jnp.log(total)), BLK)


def cost(matmuls, blocks, seq, causal):
    area = seq * seq * blocks * 2 * (0.625 if causal else 1)
    return pl.CostEstimate(
        flops=int(matmuls * area * 2 * 256), bytes_accessed=16 * seq * 128 * blocks, transcendentals=int(area)
    )


def columns(seq, width, first=0):
    return pl.BlockSpec((seq, width), lambda i: (0, i + first))


def attend_fwd(arrays, length, causal):
    seq = arrays[0].shape[0]
    widths = (384,) if causal else (128, 256)
    blocks = arrays[0].shape[1] // widths[0]
    return pl.pallas_call(
        functools.partial(fwd_kernel, causal),
        grid=(blocks,),
        in_specs=[pl.BlockSpec(memory_space=pltpu.SMEM)] + [columns(seq, w) for w in widths],
        out_specs=[columns(seq, 128)] * 2,
        out_shape=[jax.ShapeDtypeStruct((seq, 128 * blocks), bf16)] * 2,
        scratch_shapes=[pltpu.VMEM((2, seq, 256), bf16)] * 2,
        compiler_params=pltpu.CompilerParams(vmem_limit_bytes=48 * 2**20),
        cost_estimate=cost(2, blocks, seq, causal),
        name="attend_causal" if causal else "attend_memory",
    )(length, *arrays)


def bwd_kernel(causal, len_ref, *refs):
    if causal:
        qkv_ref, c_ref, lse_ref, g_ref, d_ref, qs, qm, ka, gs, gm, va, dqa = refs
        q2, k2, v2 = qkv_ref[:, :128], qkv_ref[:, 128:256], qkv_ref[:, 256:]
        dq_ref, dk_ref, dv_ref = d_ref.at[:, :128], d_ref.at[:, 128:256], d_ref.at[:, 256:]
    else:
        q_ref, kv_ref, c_ref, lse_ref, g_ref, dq_ref, dkv_ref, qs, qm, ka, gs, gm, va, dqa = refs
        q2, k2, v2 = q_ref[...], kv_ref[:, :128], kv_ref[:, 128:]
        dk_ref, dv_ref = dkv_ref.at[:, :128], dkv_ref.at[:, 128:]
    g2 = g_ref[...]
    seq = k2.shape[0]
    lane = lanes(seq)
    l64 = lane % 64
    zero = jnp.zeros_like(k2)
    one = jnp.ones_like(k2)
    scale = jnp.asarray(HD**-0.5, bf16)
    prod = c_ref[...].astype(f32) * g2.astype(f32)
    d0 = jnp.sum(jnp.where(lane < 64, prod, 0.0), axis=1, keepdims=True)
    d1 = jnp.sum(jnp.where(lane < 64, 0.0, prod), axis=1, keepdims=True)
    qs[:, :128] = q2 * scale
    aug = lse_ref[...]
    if not causal:
        aug = jnp.where(l64 == 3, one, aug)
        pos = lax.broadcasted_iota(jnp.int32, (seq, 128), 0)
        bias = jnp.where(pos >= len_ref[0], -1e30, 0.0).astype(bf16)
    qs[:, 128:] = aug
    gs[:, :128] = g2
    gs[:, 128:] = place3(-jnp.where(lane < 64, d0, d1), seq)
    for h in range(2):
        own = (lane // 64) == h
        sel = own & (l64 < 3)
        qm[h] = jnp.where(own, q2 * scale, zero)
        gm[h] = jnp.where(own, g2, zero)
        ka[h, :, :128] = jnp.where(own, k2, zero)
        ko = jnp.where(sel, one, zero)
        if not causal:
            ko = jnp.where(own & (l64 == 3), bias, ko)
        ka[h, :, 128:] = ko
        va[h, :, :128] = jnp.where(own, v2, zero)
        va[h, :, 128:] = jnp.where(sel, one, zero)
    dqa[...] = jnp.zeros_like(dqa)

    def block(j):
        rows = slice(j * BLK, (j + 1) * BLK)
        q0 = j * BLK if causal else 0
        dk = None
        dv = None
        for h in range(2):
            p = jnp.exp(dot(ka[h, rows, :], qs[q0:, :], NT))
            if causal:
                a = lax.broadcasted_iota(jnp.int32, (BLK, BLK), 0)
                b = lax.broadcasted_iota(jnp.int32, (BLK, BLK), 1)
                d = jnp.where(a <= b, p[:, :BLK], 0.0)
                p = d if q0 + BLK == seq else jnp.concatenate([d, p[:, BLK:]], axis=1)
            dp = dot(va[h, rows, :], gs[q0:, :], NT)
            ds = (p * dp).astype(bf16)
            p = p.astype(bf16)
            a = dot(p, gm[h, q0:, :])
            b = dot(ds, qm[h, q0:, :])
            dv = a if dv is None else dv + a
            dk = b if dk is None else dk + b
            dqa[q0:, :] += dot(ds, ka[h, rows, :128], TN)
        dk_ref[rows, :] = dk.astype(bf16)
        dv_ref[rows, :] = dv.astype(bf16)

    for j in range(seq // BLK):
        if causal:
            block(j)
        else:
            pl.when(j * BLK < len_ref[0])(functools.partial(block, j))

            def clear(j=j):
                rows = slice(j * BLK, (j + 1) * BLK)
                dk_ref[rows, :] = jnp.zeros((BLK, 128), bf16)
                dv_ref[rows, :] = jnp.zeros((BLK, 128), bf16)

            pl.when(j * BLK >= len_ref[0])(clear)
    dq_ref[...] = (dqa[...] * HD**-0.5).astype(bf16)


def attend_bwd(arrays, context, lse, grad, length, causal, first, blocks):
    seq = grad.shape[0]
    widths = (384,) if causal else (128, 256)
    vmem = pltpu.VMEM
    return pl.pallas_call(
        functools.partial(bwd_kernel, causal),
        grid=(blocks,),
        in_specs=[pl.BlockSpec(memory_space=pltpu.SMEM)]
        + [columns(seq, w, first) for w in widths + (128, 128, 128)],
        out_specs=[columns(seq, w) for w in widths],
        out_shape=[jax.ShapeDtypeStruct((seq, w * blocks), bf16) for w in widths],
        scratch_shapes=[
            vmem((seq, 256), bf16),
            vmem((2, seq, 128), bf16),
            vmem((2, seq, 256), bf16),
            vmem((seq, 256), bf16),
            vmem((2, seq, 128), bf16),
            vmem((2, seq, 256), bf16),
            vmem((seq, 128), f32),
        ],
        compiler_params=pltpu.CompilerParams(vmem_limit_bytes=48 * 2**20),
        cost_estimate=cost(5, blocks, seq, causal),
        name="attend_causal_back" if causal else "attend_memory_back",
    )(length, *arrays, context, lse, grad)


def partner(bit):
    d = lax.axis_index("dp")
    t = lax.axis_index("tensor")
    if bit == 0:
        return (d, 1 - t)
    size = 2 ** (bit - 1)
    return (d + size * (1 - 2 * ((d // size) % 2)), t)


X, CORE, Y, Z1, Z2 = range(5)
STAGES = 7
LINKS = (X, Y, Z1, Z2, Y, CORE, CORE)
DELAY = 2
SLOTS = 2 * DELAY


def greet():
    barrier = pltpu.get_barrier_semaphore()
    for bit in range(5):
        pl.semaphore_signal(barrier, inc=1, device_id=partner(bit), device_id_type=pl.DeviceIdType.MESH)
    pl.semaphore_wait(barrier, 5)


def sum_scratch(widths, chunk):
    shapes = []
    for w in widths:
        shapes += [
            pltpu.VMEM((2, SLOTS, chunk, 2 * w), bf16),
            pltpu.VMEM((8, SLOTS, chunk, w), bf16),
            pltpu.SemaphoreType.DMA((STAGES, SLOTS)),
            pltpu.SemaphoreType.DMA((STAGES, SLOTS)),
            pltpu.SemaphoreType.DMA((2, SLOTS)),
        ]
    return shapes


def sum_step(t, chunks, chunk, tensors):
    for stage in range(STAGES - 1, -1, -1):
        c = t - DELAY * stage
        pl.when((c >= 0) & (c < chunks))(functools.partial(sum_stage, stage, c, chunk, tensors))


def sum_stage(stage, c, chunk, tensors):
    slot = lax.rem(c, SLOTS)
    rows = pl.ds(pl.multiple_of(c * chunk, chunk), chunk)
    for oth, own, out, wide, narrow, send, recv, local in tensors:
        w = narrow.shape[-1]
        came, mine = wide.at[0, slot], wide.at[1, slot]
        side, kept, got_y, s3, got_z, s4, got_zz, s5 = [narrow.at[i, slot] for i in range(8)]

        def remote(k):
            src, dst = (
                (oth.at[rows], came),
                (side, got_y),
                (s3, got_z),
                (s4, got_zz),
                (s5, out.at[1, rows]),
                (s5, out.at[2, rows]),
                (out.at[1, rows], out.at[3, rows]),
            )[k]
            return pltpu.make_async_remote_copy(
                src_ref=src,
                dst_ref=dst,
                send_sem=send.at[k, slot],
                recv_sem=recv.at[k, slot],
                device_id=partner(LINKS[k]),
                device_id_type=pl.DeviceIdType.MESH,
            )

        def load():
            return pltpu.make_async_copy(own.at[rows], mine, local.at[0, slot])

        def keep():
            return pltpu.make_async_copy(s5, out.at[0, rows], local.at[1, slot])

        if stage == 0:
            remote(0).start()
            load().start()
        elif stage == 1:
            remote(0).wait()
            load().wait()
            v = came[...] + mine[...]
            side[...] = v[:, w:]
            kept[...] = v[:, :w]
            remote(1).start()
        elif stage == 2:
            remote(1).wait()
            s3[...] = kept[...] + got_y[...]
            remote(2).start()
        elif stage == 3:
            remote(2).wait()
            s4[...] = s3[...] + got_z[...]
            remote(3).start()
        elif stage == 4:
            remote(3).wait()
            s5[...] = s4[...] + got_zz[...]
            remote(4).start()
            remote(5).start()
            keep().start()
        elif stage == 5:
            remote(4).wait()
            remote(5).wait()
            keep().wait()
            remote(6).start()
        else:
            remote(6).wait()


def sum_kernel(count, chunks, chunk, *refs):
    ins, outs, scratch = refs[: 2 * count], refs[2 * count : 3 * count], refs[3 * count :]
    tensors = [(ins[2 * i], ins[2 * i + 1], outs[i], *scratch[5 * i : 5 * i + 5]) for i in range(count)]
    greet()

    @pl.loop(0, chunks + DELAY * (STAGES - 1))
    def _(t):
        sum_step(t, chunks, chunk, tensors)


def sum_all(pairs, ident, chunk=32):
    rows = pairs[0][0].shape[0]
    widths = [p[0].shape[1] // 2 for p in pairs]
    anywhere = pl.BlockSpec(memory_space=pl.ANY)
    return pl.pallas_call(
        functools.partial(sum_kernel, len(pairs), rows // chunk, chunk),
        in_specs=[anywhere] * (2 * len(pairs)),
        out_specs=[anywhere] * len(pairs),
        out_shape=[jax.ShapeDtypeStruct((4, rows, w), bf16) for w in widths],
        scratch_shapes=sum_scratch(widths, chunk),
        compiler_params=pltpu.CompilerParams(
            collective_id=ident, has_side_effects=True, vmem_limit_bytes=48 * 2**20
        ),
        cost_estimate=pl.CostEstimate(flops=0, bytes_accessed=sum(widths) * rows * 16, transcendentals=0),
        name="sum_gradients",
    )(*[x for p in pairs for x in p])


ALL = ("dp", "tensor")
DEVICES = 32
BOTH = (0, 1)


def swap(x, flip):
    return lax.ppermute(x, ALL, [(i, i ^ flip) for i in range(DEVICES)])


def swap_tensor(x):
    return swap(x, 1)


def swap_core(x):
    return swap(x, 2)


def swap_y(x):
    return swap(x, 4)


def my_block():
    d = lax.axis_index("dp")
    return 2 * (d % 2) + (d // 2) % 2


def add_low(*terms):
    return sum(t.astype(f32) for t in terms).astype(bf16)


def blocks_of(own, axis):
    size = own.shape[axis] // 4
    return [lax.dynamic_slice_in_dim(own, (my_block() ^ j) * size, size, axis) for j in range(4)]


def swap_pieces(x, move):
    return [move(p) for p in x] if isinstance(x, (list, tuple)) else move(x)


def tie(*xs):
    return lax.optimization_barrier(xs)


class Pipe:
    def __init__(self):
        self.live = []

    def put(self, gen):
        wait, arrays = next(gen)
        self.live.append([gen, wait, arrays])

    def step(self, due, landed):
        done = 0
        for item in due:
            arrays = landed[done : done + len(item[2])]
            done += len(item[2])
            try:
                item[1], item[2] = item[0].send(arrays)
            except StopIteration:
                self.live.remove(item)

    def cut(self, *xs):
        due = []
        for item in self.live:
            item[1] -= 1
            if item[1] <= 0:
                due.append(item)
        tied = tie(*xs, *[a for item in due for a in item[2]])
        self.step(due, tied[len(xs) :])
        return tied[: len(xs)] if len(xs) > 1 else tied[0]

    def drain(self):
        while self.live:
            self.step(list(self.live), [a for item in self.live for a in item[2]])


def fetch(out, key, block, waits):
    far = swap_tensor(block)
    (far,) = yield waits[0], [far]
    side = swap_y(far)
    near = swap_core(far)
    side, near = yield waits[1], [side, near]
    out[key] = [far, side, near, swap_core(side)]
    return


def assemble_kernel(axis, me_ref, x_ref, out_ref):
    x = x_ref[...].astype(f32)
    out_ref[...] = x.T if axis == 0 else x


def assemble(blocks, axis, members=1):
    _, rows, width = blocks.shape
    tiles = 2
    high = rows // tiles
    narrow = width // members
    if axis == 0:
        out_spec = pl.BlockSpec((narrow, high), lambda b, m, t, me: (b ^ me[0], t))
        shape = (4 * width, rows)
    else:
        out_spec = pl.BlockSpec((None, high, narrow), lambda b, m, t, me: (m, t, b ^ me[0]))
        shape = (members, rows, narrow * 4)
    return pl.pallas_call(
        functools.partial(assemble_kernel, axis),
        grid_spec=pltpu.PrefetchScalarGridSpec(
            num_scalar_prefetch=1,
            grid=(4, members, tiles),
            in_specs=[pl.BlockSpec((None, high, narrow), lambda b, m, t, me: (b, t, m))],
            out_specs=out_spec,
        ),
        out_shape=jax.ShapeDtypeStruct(shape, f32),
        compiler_params=pltpu.CompilerParams(vmem_limit_bytes=40 * 2**20),
        cost_estimate=pl.CostEstimate(flops=0, bytes_accessed=24 * rows * width, transcendentals=0),
        name="assemble",
    )(my_block().reshape(1), blocks)


def core_sum(part):
    send = [part(i, 2).astype(bf16) for i in BOTH]
    got = [swap_core(x) for x in send]
    keep = [add_low(part(i, 0), got[i]) for i in BOTH]
    return keep[1], keep[0]


def sum_small(out, x):
    for flip in (1, 2, 4, 8, 16):
        (other,) = yield 1, [swap(x, flip)]
        x = x + other
    out["small"] = x


def ffn_kernel(h_ref, *refs):
    ups, downs = refs[:4], refs[4:8]
    a_ref, d_ref, b_ref = refs[8:]
    h = h_ref[...]
    size = ups[0].shape[1]
    total = None
    for j in range(4):
        u = dot(h, ups[j][...])
        cdf = 0.5 + 0.5 * lax.erf(u * (0.5**0.5))
        slope = cdf + u * (jnp.exp(-0.5 * u * u) * 0.3989422804014327)
        act = (u * cdf).astype(bf16)
        cols = slice(j * size, (j + 1) * size)
        a_ref[:, cols] = act
        d_ref[:, cols] = slope.astype(bf16)
        term = dot(act, downs[j][...])
        total = term if total is None else total + term
    b_ref[...] = total


def whole(x):
    return pl.BlockSpec(x.shape, lambda r: (0, 0))


ROWS = 256


def ffn_forward(h, ups, downs):
    seq, width = h.shape
    units = 4 * ups[0].shape[1]
    rows = lambda w: pl.BlockSpec((ROWS, w), lambda r: (r, 0))
    return pl.pallas_call(
        ffn_kernel,
        grid=(seq // ROWS,),
        in_specs=[rows(width)] + [whole(x) for x in ups + downs],
        out_specs=[rows(units), rows(units), rows(width)],
        out_shape=[jax.ShapeDtypeStruct((seq, units), bf16)] * 2 + [jax.ShapeDtypeStruct((seq, width), f32)],
        compiler_params=pltpu.CompilerParams(vmem_limit_bytes=50 * 2**20),
        cost_estimate=pl.CostEstimate(flops=4 * seq * width * units, bytes_accessed=22 * 2**20, transcendentals=2 * seq * units),
        name="feed_forward",
    )(h, *ups, *downs)


def ffn_back_kernel(g_ref, d_ref, *refs):
    ups, downs = refs[:4], refs[4:8]
    du_ref, dh_ref = refs[-2:]
    g = g_ref[...]
    size = ups[0].shape[1]
    total = refs[8][...] if len(refs) > 10 else None
    for j in range(4):
        cols = slice(j * size, (j + 1) * size)
        du = (dot(g, downs[j][...], NT) * d_ref[:, cols].astype(f32)).astype(bf16)
        du_ref[:, cols] = du
        term = dot(du, ups[j][...], NT)
        total = term if total is None else total + term
    dh_ref[...] = total


def ffn_backward(g, slope, ups, downs, before=None):
    seq, width = g.shape
    units = slope.shape[1]
    rows = lambda w: pl.BlockSpec((ROWS, w), lambda r: (r, 0))
    extra = [] if before is None else [before]
    return pl.pallas_call(
        ffn_back_kernel,
        grid=(seq // ROWS,),
        in_specs=[rows(width), rows(units)] + [whole(x) for x in ups + downs] + [rows(width)] * len(extra),
        out_specs=[rows(units), rows(width)],
        out_shape=[jax.ShapeDtypeStruct((seq, units), bf16), jax.ShapeDtypeStruct((seq, width), f32)],
        compiler_params=pltpu.CompilerParams(vmem_limit_bytes=50 * 2**20),
        cost_estimate=pl.CostEstimate(flops=4 * seq * width * units, bytes_accessed=22 * 2**20, transcendentals=0),
        name="feed_forward_back",
    )(g, slope, *ups, *downs, *extra)


def side_by_side(parts):
    return jnp.concatenate(parts, axis=1)


def cols(x, first, last, of=4):
    size = x.shape[1] // of
    return x[:, first * size : last * size]


def one_pair_each(
    target,
    memory,
    mem_len,
    grad_out,
    self_qkv,
    self_out,
    cross_query,
    cross_kv,
    cross_out,
    ffn_up,
    ffn_down,
    ln_gain,
    ln_bias,
):
    length = lax.dynamic_slice_in_dim(mem_len, lax.axis_index("tensor"), 1)
    pipe = Pipe()
    got = {}

    qkv_b = [side_by_side(list(b)) for b in blocks_of(self_qkv, 2)]
    pipe.put(fetch(got, "qkv", qkv_b[0], (1, 1)))
    qkv_w = [side_by_side(qkv_b), None]
    qkv = [dot(target, qkv_w[0]).astype(bf16), None]
    at1 = [attend_fwd((qkv[0],), length, True), None]
    so_b = blocks_of(self_out, 0)
    kv_b = [side_by_side(list(b)) for b in blocks_of(cross_kv, 2)]
    cq_b = blocks_of(cross_query, 1)
    co_b = blocks_of(cross_out, 0)
    kv_w = [side_by_side(kv_b), None]
    mem, so_b[0], cq_b[0], co_b[0], _ = pipe.cut(memory, so_b[0], cq_b[0], co_b[0], at1[0][0])
    kv = [dot(mem, kv_w[0]).astype(bf16), None]
    pipe.put(fetch(got, "so", so_b[0], (2, 1)))
    pipe.put(fetch(got, "cq", cq_b[0], (2, 1)))
    tar, kv[0], kv_b[0] = pipe.cut(target, kv[0], kv_b[0])
    qkv_w[1] = side_by_side(got["qkv"])
    qkv[1] = dot(tar, qkv_w[1]).astype(bf16)
    pipe.put(fetch(got, "kv", kv_b[0], (1, 1)))
    pipe.put(fetch(got, "co", co_b[0], (2, 1)))
    qkv[1], = tie(qkv[1])
    at1[1] = attend_fwd((qkv[1],), length, True)
    c1 = [at1[i][0] for i in BOTH]
    up_b = blocks_of(ffn_up, 1)
    down_b = blocks_of(ffn_down, 0)
    c1[1], up_b[0] = pipe.cut(c1[1], up_b[0])
    pipe.put(fetch(got, "up", up_b[0], (1, 1)))
    c1[1] = pipe.cut(c1[1]) if False else c1[1]
    so_w = [jnp.concatenate(so_b, axis=0), jnp.concatenate(got["so"], axis=0)] if "so" in got else None
    if so_w is None:
        c1[1] = pipe.cut(c1[1])
        so_w = [jnp.concatenate(so_b, axis=0), jnp.concatenate(got["so"], axis=0)]
    b1 = dot(c1[0], so_w[0]) + dot(c1[1], so_w[1])
    h1, back1 = jax.vjp(norm_rows, alpha_res * target.astype(f32) + b1, ln_gain[0], ln_bias[0])
    h1_low = h1.astype(bf16)
    cq_w = [side_by_side(cq_b), side_by_side(got["cq"])]
    q2 = [dot(h1_low, cq_w[i]).astype(bf16) for i in BOTH]
    q2[0], down_b[0] = pipe.cut(q2[0], down_b[0])
    pipe.put(fetch(got, "down", down_b[0], (1, 1)))
    at2 = [attend_fwd((q2[0], kv[0]), length, False), None]
    if "kv" not in got:
        at2[0] = pipe.cut(*at2[0])
    kv_w[1] = side_by_side(got["kv"])
    kv[1] = dot(memory, kv_w[1]).astype(bf16)
    at2[1] = attend_fwd((q2[1], kv[1]), length, False)
    at2[1] = pipe.cut(*at2[1])
    c2 = [at2[i][0] for i in BOTH]
    co_w = [jnp.concatenate(co_b, axis=0), jnp.concatenate(got["co"], axis=0)]
    b2 = dot(c2[0], co_w[0]) + dot(c2[1], co_w[1])
    h2, back2 = jax.vjp(norm_rows, alpha_res * h1 + b2, ln_gain[1], ln_bias[1])
    h2_low = h2.astype(bf16)
    act0, slope0, b3 = ffn_forward(h2_low, up_b, down_b)
    while "up" not in got or "down" not in got:
        act0 = pipe.cut(act0)
    h2_again, _ = tie(h2_low, act0)
    act1, slope1, b3b = ffn_forward(h2_again, got["up"], got["down"])
    act, slope = (act0, act1), (slope0, slope1)
    result, back3 = jax.vjp(norm_rows, alpha_res * h2 + b3 + b3b, ln_gain[2], ln_bias[2])

    dz3, gain3, bias3 = back3(grad_out.astype(f32))
    g3 = dz3.astype(bf16)
    out = {}
    du1, dh2 = ffn_backward(g3, slope[1], got["up"], got["down"])
    du0, dh2 = ffn_backward(g3, slope[0], up_b, down_b, dh2)
    du = (du0, du1)
    down_pair = core_sum(lambda i, f: dot(g3, cols(act[i], f, f + 2), TN))
    up_pair = core_sum(lambda i, f: dot(h2_low, cols(du[i], f, f + 2), TN))
    dz2, gain2, bias2 = back2(alpha_res * dz3 + dh2)
    g2 = dz2.astype(bf16)
    co_pair = core_sum(lambda i, f: dot(g2, cols(c2[i], f, f + 2), TN))
    dc2 = [dot(g2, co_w[i], NT).astype(bf16) for i in BOTH]
    p2 = {
        (i, f): attend_bwd((q2[i], kv[i]), *at2[i], dc2[i], length, False, f, 2) for f in (2, 0) for i in (1, 0)
    }
    cq_pair = core_sum(lambda i, f: dot(h1_low, p2[i, f][0], TN))
    kv_pair = core_sum(lambda i, f: dot(memory, p2[i, f][1], TN))
    dq_terms = [(p2[i, f][0], cols(cq_w[i], f, f + 2)) for i in BOTH for f in (0, 2)]
    dh1 = alpha_res * dz2 + sum(dot(x, w, NT) for x, w in dq_terms)
    dz1, gain1, bias1 = back1(dh1)
    g1 = dz1.astype(bf16)
    pipe.put(sum_small(out, jnp.stack([gain1, gain2, gain3, bias1, bias2, bias3])))
    so_pair = core_sum(lambda i, f: dot(g1, cols(c1[i], f, f + 2), TN))
    dc1 = [dot(g1, so_w[i], NT).astype(bf16) for i in BOTH]
    p1 = {}
    for f in (2, 0):
        for i in (1, 0):
            dc1[i] = pipe.cut(dc1[i])
            p1[i, f] = attend_bwd((qkv[i],), *at1[i], dc1[i], length, True, f, 2)
            p1[i, f] = tie(*p1[i, f])
    tar = pipe.cut(target)
    qkv_pair = core_sum(lambda i, f: dot(tar, p1[i, f][0], TN))
    dmem = sum(dot(p2[i, f][1], cols(kv_w[i], f, f + 2), NT) for i in BOTH for f in (0, 2)).astype(bf16)
    dtar = alpha_res * dz1 + sum(dot(p1[i, f][0], cols(qkv_w[i], f, f + 2), NT) for i in BOTH for f in (0, 2))
    dtar = dtar.astype(bf16)
    pipe.drain()
    qkv_t, so_t, cq_t, kv_t, co_t, up_t, down_t = sum_all(
        [qkv_pair, so_pair, cq_pair, kv_pair, co_pair, up_pair, down_pair], 1
    )
    small = out["small"]
    return (
        result.astype(bf16),
        dtar,
        dmem,
        assemble(qkv_t, 1, 3),
        assemble(so_t, 0),
        assemble(cq_t, 1)[0],
        assemble(kv_t, 1, 2),
        assemble(co_t, 0),
        assemble(up_t, 1)[0],
        assemble(down_t, 0),
        small[:3],
        small[3:],
    )


def solution(mesh):
    placed = (
        P(("dp", "tensor"), None),
        P(("dp", "tensor"), None),
        P("dp"),
        P(("dp", "tensor"), None),
        P(None, None, "tensor"),
        P("tensor", None),
        P(None, "tensor"),
        P(None, None, "tensor"),
        P("tensor", None),
        P(None, "tensor"),
        P("tensor", None),
        P(),
        P(),
    )
    body = one_pair_each if mesh.shape["tensor"] == 2 and mesh.shape["dp"] == 16 else on_device
    return jax.shard_map(
        body,
        mesh=mesh,
        in_specs=placed,
        out_specs=(
            P(("dp", "tensor"), None),
            P(("dp", "tensor"), None),
            P(("dp", "tensor"), None),
            P(None, None, "tensor"),
            P("tensor", None),
            P(None, "tensor"),
            P(None, None, "tensor"),
            P("tensor", None),
            P(None, "tensor"),
            P("tensor", None),
            P(),
            P(),
        ),
        check_vma=False,
    )
```

```python
import functools

import jax
import jax.numpy as jnp
from jax import lax
from jax.experimental import pallas as pl
from jax.experimental.pallas import tpu as pltpu
from jax.sharding import PartitionSpec as P

HD = 64


alpha_res = 300.0**0.25
norm_eps = 1e-05
mask_fill = -1e30
contract_rows = (((0,), (0,)), ((), ()))
contract_cols = (((1,), (1,)), ((), ()))


def norm_rows(resid, gain_vec, bias_vec):
    average = jnp.mean(resid, axis=-1, keepdims=True)
    centered = resid - average
    variance = jnp.mean(centered * centered, axis=-1, keepdims=True)
    return centered * lax.rsqrt(variance + norm_eps) * gain_vec + bias_vec


def exact_gelu(values_in):
    return jax.nn.gelu(values_in, approximate=False)


def gather_rows(local_rows):
    return lax.all_gather(local_rows, "tensor", axis=0, tiled=True)


def gather_grads(local_rows):
    return lax.all_gather(local_rows, "tensor", axis=0, tiled=True)


def scatter_branch(left_mat, right_mat, row_count):

    def partial_term(offset, num_rows):
        return jnp.dot(left_mat, right_mat, preferred_element_type=jnp.float32)

    return lax.psum_scatter(
        partial_term(jnp.int32(0), row_count * lax.axis_size("tensor")),
        "tensor",
        scatter_dimension=0,
        tiled=True,
    )


def project_context(context, weight_local, row_count):
    return scatter_branch(context, weight_local, row_count)


def scatter_inputs(factor_pairs, row_count):

    def partial_term(offset, num_rows):
        terms = [
            lax.dot_general(grad_mat, weight_mat, contract_cols, preferred_element_type=jnp.float32)
            for grad_mat, weight_mat in factor_pairs
        ]
        return sum(terms)

    return lax.psum_scatter(
        partial_term(jnp.int32(0), row_count * lax.axis_size("tensor")).astype(jnp.bfloat16),
        "tensor",
        scatter_dimension=0,
        tiled=True,
    ).astype(jnp.float32)


def block_view(flat, pair_count, block_rows):
    tok_count, col_count = flat.shape
    seq_len = tok_count // pair_count
    return flat.reshape(pair_count, seq_len // block_rows, block_rows, col_count // HD, HD)


def pair_view(flat, pair_count):
    tok_count, col_count = flat.shape
    return flat.reshape(pair_count, tok_count // pair_count, col_count // HD, HD)


def block_scores(query_blk, key_pair, start_row, key_len, causal):
    block_rows = query_blk.shape[0]
    seq_len = key_pair.shape[0]
    products = jnp.einsum(
        "qhd,khd->hqk", query_blk, key_pair, preferred_element_type=jnp.float32
    ) * HD ** (-0.5)
    key_pos = lax.broadcasted_iota(jnp.int32, (block_rows, seq_len), 1)
    query_pos = start_row + lax.broadcasted_iota(jnp.int32, (block_rows, seq_len), 0)
    allowed = key_pos < key_len
    if causal:
        allowed = allowed & (key_pos <= query_pos)
    return jnp.where(allowed[None], products, mask_fill)


def attend_forward(queries, key_rows, value_rows, key_lens, causal):
    pair_count = key_lens.shape[0]
    seq_len = queries.shape[0] // pair_count
    block_rows = min(512, seq_len)
    starts = lax.iota(jnp.int32, seq_len // block_rows) * block_rows

    def one_pair(packed):
        query_pair, key_pair, value_pair, key_len = packed

        def one_block(inner):
            query_blk, start_row = inner
            scores = block_scores(query_blk, key_pair, start_row, key_len, causal)
            row_max = jnp.max(scores, axis=-1, keepdims=True)
            shifted = jnp.exp(scores - row_max)
            row_total = jnp.sum(shifted, axis=-1, keepdims=True)
            attn_prob = (shifted / row_total).astype(jnp.bfloat16)
            context = jnp.einsum(
                "hqk,khd->qhd", attn_prob, value_pair, preferred_element_type=jnp.float32
            )
            return (context.astype(jnp.bfloat16), (row_max + jnp.log(row_total))[..., 0])

        return lax.map(one_block, (query_pair, starts))

    context, log_total = lax.map(
        one_pair,
        (
            block_view(queries, pair_count, block_rows),
            pair_view(key_rows, pair_count),
            pair_view(value_rows, pair_count),
            key_lens,
        ),
    )
    return (context.reshape(queries.shape), log_total)


def attend_backward(queries, key_rows, value_rows, key_lens, causal, log_total, grad_context):
    pair_count = key_lens.shape[0]
    seq_len = queries.shape[0] // pair_count
    block_rows = min(512, seq_len)
    starts = lax.iota(jnp.int32, seq_len // block_rows) * block_rows
    score_scale = HD ** (-0.5)

    def one_pair(packed):
        query_pair, key_pair, value_pair, key_len, total_pair, grad_pair = packed

        def one_block(carry, inner):
            key_grad, value_grad = carry
            query_blk, start_row, total_blk, grad_blk = inner
            scores = block_scores(query_blk, key_pair, start_row, key_len, causal)
            attn_prob = jnp.exp(scores - total_blk[..., None])
            value_grad = value_grad + jnp.einsum(
                "hqk,qhd->khd",
                attn_prob.astype(jnp.bfloat16),
                grad_blk,
                preferred_element_type=jnp.float32,
            )
            prob_grad = jnp.einsum(
                "qhd,khd->hqk", grad_blk, value_pair, preferred_element_type=jnp.float32
            )
            score_grad = (
                attn_prob * (prob_grad - jnp.sum(attn_prob * prob_grad, axis=-1, keepdims=True))
            ).astype(jnp.bfloat16)
            query_grad = (
                jnp.einsum("hqk,khd->qhd", score_grad, key_pair, preferred_element_type=jnp.float32)
                * score_scale
            )
            key_grad = (
                key_grad
                + jnp.einsum(
                    "hqk,qhd->khd", score_grad, query_blk, preferred_element_type=jnp.float32
                )
                * score_scale
            )
            return ((key_grad, value_grad), query_grad.astype(jnp.bfloat16))

        zeros = jnp.zeros(key_pair.shape, jnp.float32)
        (key_grad, value_grad), query_grad = lax.scan(
            one_block, (zeros, zeros), (query_pair, starts, total_pair, grad_pair)
        )
        return (query_grad, key_grad.astype(jnp.bfloat16), value_grad.astype(jnp.bfloat16))

    query_grad, key_grad, value_grad = lax.map(
        one_pair,
        (
            block_view(queries, pair_count, block_rows),
            pair_view(key_rows, pair_count),
            pair_view(value_rows, pair_count),
            key_lens,
            log_total,
            block_view(grad_context, pair_count, block_rows),
        ),
    )
    return (
        query_grad.reshape(queries.shape),
        key_grad.reshape(queries.shape),
        value_grad.reshape(queries.shape),
    )


def on_device(
    target,
    memory,
    mem_len,
    grad_out,
    self_qkv,
    self_out,
    cross_query,
    cross_kv,
    cross_out,
    ffn_up,
    ffn_down,
    ln_gain,
    ln_bias,
):
    row_count = target.shape[0]
    pair_count = mem_len.shape[0]
    seq_len = row_count * lax.axis_size("tensor") // pair_count
    full_lens = jnp.full((pair_count,), seq_len, jnp.int32)
    target_all = gather_rows(target)
    qkv_rows = jnp.einsum(
        "td,ide->ite", target_all, self_qkv, preferred_element_type=jnp.float32
    ).astype(jnp.bfloat16)
    context_one, total_one = attend_forward(qkv_rows[0], qkv_rows[1], qkv_rows[2], full_lens, True)
    branch_one = project_context(context_one, self_out, row_count)
    normed_one, norm_back_one = jax.vjp(
        norm_rows, alpha_res * target.astype(jnp.float32) + branch_one, ln_gain[0], ln_bias[0]
    )
    normed_one_all = gather_rows(normed_one.astype(jnp.bfloat16))
    memory_all = gather_rows(memory)
    query_two = jnp.dot(normed_one_all, cross_query, preferred_element_type=jnp.float32).astype(
        jnp.bfloat16
    )
    kv_two = jnp.einsum(
        "td,ide->ite", memory_all, cross_kv, preferred_element_type=jnp.float32
    ).astype(jnp.bfloat16)
    context_two, total_two = attend_forward(query_two, kv_two[0], kv_two[1], mem_len, False)
    branch_two = project_context(context_two, cross_out, row_count)
    normed_two, norm_back_two = jax.vjp(
        norm_rows, alpha_res * normed_one + branch_two, ln_gain[1], ln_bias[1]
    )
    normed_two_low = normed_two.astype(jnp.bfloat16)
    normed_two_all = gather_rows(normed_two_low)
    hidden = jnp.dot(normed_two_all, ffn_up, preferred_element_type=jnp.float32)
    activated, gelu_back = jax.vjp(exact_gelu, hidden)
    activated_low = activated.astype(jnp.bfloat16)
    branch_three = scatter_branch(activated_low, ffn_down, row_count)
    result, norm_back_three = jax.vjp(
        norm_rows, alpha_res * normed_two + branch_three, ln_gain[2], ln_bias[2]
    )
    grad_sum_three, gain_three, bias_three = norm_back_three(grad_out.astype(jnp.float32))
    branch_grad_three = gather_grads(grad_sum_three.astype(jnp.bfloat16))
    down_grad = lax.dot_general(
        activated_low, branch_grad_three, contract_rows, preferred_element_type=jnp.float32
    )
    act_grad = lax.dot_general(
        branch_grad_three, ffn_down, contract_cols, preferred_element_type=jnp.float32
    )
    hidden_grad = gelu_back(act_grad)[0].astype(jnp.bfloat16)
    up_grad = lax.dot_general(
        normed_two_all, hidden_grad, contract_rows, preferred_element_type=jnp.float32
    )
    normed_two_grad = alpha_res * grad_sum_three + scatter_inputs(
        ((hidden_grad, ffn_up),), row_count
    )
    grad_sum_two, gain_two, bias_two = norm_back_two(normed_two_grad)
    branch_grad_two = gather_grads(grad_sum_two.astype(jnp.bfloat16))
    cross_out_grad = lax.dot_general(
        context_two, branch_grad_two, contract_rows, preferred_element_type=jnp.float32
    )
    context_grad_two = lax.dot_general(
        branch_grad_two, cross_out, contract_cols, preferred_element_type=jnp.float32
    ).astype(jnp.bfloat16)
    query_grad_two, key_grad_two, value_grad_two = attend_backward(
        query_two, kv_two[0], kv_two[1], mem_len, False, total_two, context_grad_two
    )
    cross_query_grad = lax.dot_general(
        normed_one_all, query_grad_two, contract_rows, preferred_element_type=jnp.float32
    )
    cross_kv_grad = jnp.einsum(
        "td,ite->ide",
        memory_all,
        jnp.stack([key_grad_two, value_grad_two]),
        preferred_element_type=jnp.float32,
    )
    memory_grad = scatter_inputs(
        ((key_grad_two, cross_kv[0]), (value_grad_two, cross_kv[1])), row_count
    )
    normed_one_grad = alpha_res * grad_sum_two + scatter_inputs(
        ((query_grad_two, cross_query),), row_count
    )
    grad_sum_one, gain_one, bias_one = norm_back_one(normed_one_grad)
    branch_grad_one = gather_grads(grad_sum_one.astype(jnp.bfloat16))
    self_out_grad = lax.dot_general(
        context_one, branch_grad_one, contract_rows, preferred_element_type=jnp.float32
    )
    context_grad_one = lax.dot_general(
        branch_grad_one, self_out, contract_cols, preferred_element_type=jnp.float32
    ).astype(jnp.bfloat16)
    query_grad_one, key_grad_one, value_grad_one = attend_backward(
        qkv_rows[0], qkv_rows[1], qkv_rows[2], full_lens, True, total_one, context_grad_one
    )
    self_qkv_grad = jnp.einsum(
        "td,ite->ide",
        target_all,
        jnp.stack([query_grad_one, key_grad_one, value_grad_one]),
        preferred_element_type=jnp.float32,
    )
    target_grad = alpha_res * grad_sum_one + scatter_inputs(
        ((query_grad_one, self_qkv[0]), (key_grad_one, self_qkv[1]), (value_grad_one, self_qkv[2])),
        row_count,
    )
    (
        self_qkv_total,
        self_out_total,
        cross_query_total,
        cross_kv_total,
        cross_out_total,
        up_total,
        down_total,
    ) = (
        lax.psum(self_qkv_grad.astype(jnp.bfloat16), "dp").astype(jnp.float32),
        lax.psum(self_out_grad.astype(jnp.bfloat16), "dp").astype(jnp.float32),
        lax.psum(cross_query_grad.astype(jnp.bfloat16), "dp").astype(jnp.float32),
        lax.psum(cross_kv_grad.astype(jnp.bfloat16), "dp").astype(jnp.float32),
        lax.psum(cross_out_grad.astype(jnp.bfloat16), "dp").astype(jnp.float32),
        lax.psum(up_grad.astype(jnp.bfloat16), "dp").astype(jnp.float32),
        lax.psum(down_grad.astype(jnp.bfloat16), "dp").astype(jnp.float32),
    )
    gain_total, bias_total = lax.psum(
        (jnp.stack([gain_one, gain_two, gain_three]), jnp.stack([bias_one, bias_two, bias_three])),
        ("dp", "tensor"),
    )
    return (
        result.astype(jnp.bfloat16),
        target_grad.astype(jnp.bfloat16),
        memory_grad.astype(jnp.bfloat16),
        self_qkv_total,
        self_out_total,
        cross_query_total,
        cross_kv_total,
        cross_out_total,
        up_total,
        down_total,
        gain_total,
        bias_total,
    )


BLK = 256
f32 = jnp.float32
bf16 = jnp.bfloat16
NN = (((1,), (0,)), ((), ()))
NT = (((1,), (1,)), ((), ()))
TN = (((0,), (0,)), ((), ()))


def dot(a, b, dims=NN):
    return lax.dot_general(a, b, dims, preferred_element_type=f32)


def lanes(rows):
    return lax.broadcasted_iota(jnp.int32, (rows, 128), 1)


def place3(x, rows):
    hi = x.astype(bf16)
    rest = x - hi.astype(f32)
    mid = rest.astype(bf16)
    lo = (rest - mid.astype(f32)).astype(bf16)
    at = lanes(rows) % 64
    return jnp.where(at == 0, hi, jnp.where(at == 1, mid, jnp.where(at == 2, lo, jnp.zeros_like(hi))))


def fwd_kernel(causal, len_ref, q_ref, k_ref, v_ref, c_ref, lse_ref, kaug, vaug):
    k2, v2 = k_ref[...], v_ref[...]
    seq = k2.shape[0]
    lane = lanes(seq)
    zero = jnp.zeros_like(k2)
    if not causal:
        pos = lax.broadcasted_iota(jnp.int32, (seq, 128), 0)
        bias = jnp.where((pos >= len_ref[0]) & (lane == 0), -1e30, 0.0).astype(bf16)
    for h in range(2):
        own = (lane // 64) == h
        kaug[h, :, :128] = jnp.where(own, k2, zero)
        if not causal:
            kaug[h, :, 128:] = bias
        vaug[h, :, :128] = jnp.where(own, v2, zero)
        vaug[h, :, 128:] = jnp.where(own, jnp.ones_like(v2), zero)
    lb = lanes(BLK)
    for i in range(seq // BLK):
        rows = slice(i * BLK, (i + 1) * BLK)
        q = q_ref[rows, :] * jnp.asarray(HD**-0.5, bf16)
        if not causal:
            q = jnp.concatenate([q, jnp.where(lb == 0, 1.0, 0.0).astype(bf16)], axis=1)
        nk = (i + 1) * BLK if causal else seq
        acc = None
        ms = []
        for h in range(2):
            s = dot(q, kaug[h, :nk, :128] if causal else kaug[h], NT)
            if causal:
                a = lax.broadcasted_iota(jnp.int32, (BLK, BLK), 0)
                b = lax.broadcasted_iota(jnp.int32, (BLK, BLK), 1)
                d = jnp.where(b <= a, s[:, nk - BLK :], mask_fill)
                s = d if nk == BLK else jnp.concatenate([s[:, : nk - BLK], d], axis=1)
            m = jnp.max(s, axis=1, keepdims=True)
            p = jnp.exp(s - m).astype(bf16)
            o = dot(p, vaug[h, :nk])
            acc = o if acc is None else acc + o
            ms.append(m)
        total = acc[:, 128:]
        c_ref[rows, :] = (acc[:, :128] / total).astype(bf16)
        lse_ref[rows, :] = place3(-(jnp.where(lb < 64, ms[0], ms[1]) + jnp.log(total)), BLK)


def cost(matmuls, blocks, seq, causal):
    area = seq * seq * blocks * 2 * (0.625 if causal else 1)
    return pl.CostEstimate(
        flops=int(matmuls * area * 2 * 256), bytes_accessed=16 * seq * 128 * blocks, transcendentals=int(area)
    )


def attend_fwd(q, k, v, length, causal):
    seq, width = q.shape
    spec = pl.BlockSpec((seq, 128), lambda i: (0, i))
    return pl.pallas_call(
        functools.partial(fwd_kernel, causal),
        grid=(width // 128,),
        in_specs=[pl.BlockSpec(memory_space=pltpu.SMEM)] + [spec] * 3,
        out_specs=[spec] * 2,
        out_shape=[jax.ShapeDtypeStruct((seq, width), bf16)] * 2,
        scratch_shapes=[pltpu.VMEM((2, seq, 256), bf16)] * 2,
        compiler_params=pltpu.CompilerParams(vmem_limit_bytes=48 * 2**20),
        cost_estimate=cost(2, width // 128, seq, causal),
        name="attend_causal" if causal else "attend_memory",
    )(length, q, k, v)


def back_scratch(seq):
    vmem = pltpu.VMEM
    return [
        vmem((seq, 256), bf16),
        vmem((2, seq, 128), bf16),
        vmem((2, seq, 256), bf16),
        vmem((seq, 256), bf16),
        vmem((2, seq, 128), bf16),
        vmem((2, seq, 256), bf16),
        vmem((seq, 128), f32),
    ]


def back_pair(causal, length, q2, k2, v2, c2, aug, g2, grads, scratch, tick):
    qs, qm, ka, gs, gm, va, dqa = scratch
    seq = k2.shape[0]
    lane = lanes(seq)
    l64 = lane % 64
    zero = jnp.zeros_like(k2)
    one = jnp.ones_like(k2)
    scale = jnp.asarray(HD**-0.5, bf16)
    prod = c2.astype(f32) * g2.astype(f32)
    d0 = jnp.sum(jnp.where(lane < 64, prod, 0.0), axis=1, keepdims=True)
    d1 = jnp.sum(jnp.where(lane < 64, 0.0, prod), axis=1, keepdims=True)
    qs[:, :128] = q2 * scale
    if not causal:
        aug = jnp.where(l64 == 3, one, aug)
        pos = lax.broadcasted_iota(jnp.int32, (seq, 128), 0)
        bias = jnp.where(pos >= length, -1e30, 0.0).astype(bf16)
    qs[:, 128:] = aug
    gs[:, :128] = g2
    gs[:, 128:] = place3(-jnp.where(lane < 64, d0, d1), seq)
    for h in range(2):
        own = (lane // 64) == h
        sel = own & (l64 < 3)
        qm[h] = jnp.where(own, q2 * scale, zero)
        gm[h] = jnp.where(own, g2, zero)
        ka[h, :, :128] = jnp.where(own, k2, zero)
        ko = jnp.where(sel, one, zero)
        if not causal:
            ko = jnp.where(own & (l64 == 3), bias, ko)
        ka[h, :, 128:] = ko
        va[h, :, :128] = jnp.where(own, v2, zero)
        va[h, :, 128:] = jnp.where(sel, one, zero)
    dqa[...] = jnp.zeros_like(dqa)
    grads[:, 384:] = c2
    for j in range(seq // BLK):
        rows = slice(j * BLK, (j + 1) * BLK)
        q0 = j * BLK if causal else 0
        dk = None
        dv = None
        for h in range(2):
            p = jnp.exp(dot(ka[h, rows, :], qs[q0:, :], NT))
            if causal:
                a = lax.broadcasted_iota(jnp.int32, (BLK, BLK), 0)
                b = lax.broadcasted_iota(jnp.int32, (BLK, BLK), 1)
                d = jnp.where(a <= b, p[:, :BLK], 0.0)
                p = d if q0 + BLK == seq else jnp.concatenate([d, p[:, BLK:]], axis=1)
            dp = dot(va[h, rows, :], gs[q0:, :], NT)
            ds = (p * dp).astype(bf16)
            p = p.astype(bf16)
            a = dot(p, gm[h, q0:, :])
            b = dot(ds, qm[h, q0:, :])
            dv = a if dv is None else dv + a
            dk = b if dk is None else dk + b
            dqa[q0:, :] += dot(ds, ka[h, rows, :128], TN)
        grads[rows, 128:256] = dk.astype(bf16)
        grads[rows, 256:384] = dv.astype(bf16)
        tick(j)
    grads[:, :128] = (dqa[...] * HD**-0.5).astype(bf16)


BOTH = (0, 1)
X, CORE, Y, Z1, Z2 = range(5)
DELAY = 2
SLOTS = 2 * DELAY
CHUNK = 32
SUBS = 8
PAIRS_HERE = 4
LEAD = SUBS
HBM_LINKS = (X, Y, Z1, Z2, Y, CORE, CORE)
PAIR_LINKS = (CORE, X, Y, Z1, Z2, Y, CORE, CORE)
dma_sem = pltpu.SemaphoreType.DMA


def partner(bit):
    d = lax.axis_index("dp")
    t = lax.axis_index("tensor")
    if bit == 0:
        return (d, 1 - t)
    size = 2 ** (bit - 1)
    return (d + size * (1 - 2 * ((d // size) % 2)), t)


def greet():
    barrier = pltpu.get_barrier_semaphore()
    for bit in range(5):
        pl.semaphore_signal(barrier, inc=1, device_id=partner(bit), device_id_type=pl.DeviceIdType.MESH)
    pl.semaphore_wait(barrier, 5)


def remote_copy(src, dst, send, recv, bit):
    return pltpu.make_async_remote_copy(
        src_ref=src,
        dst_ref=dst,
        send_sem=send,
        recv_sem=recv,
        device_id=partner(bit),
        device_id_type=pl.DeviceIdType.MESH,
    )


def whole_scratch(w):
    return [
        pltpu.VMEM((2, SLOTS, CHUNK, 2 * w), bf16),
        pltpu.VMEM((8, SLOTS, CHUNK, w), bf16),
        dma_sem((7, SLOTS)),
        dma_sem((7, SLOTS)),
        dma_sem((2, SLOTS)),
    ]


def whole_stage(stage, c, oth, own, out, wide, narrow, send, recv, local):
    slot = lax.rem(c, SLOTS)
    rows = pl.ds(pl.multiple_of(c * CHUNK, CHUNK), CHUNK)
    w = narrow.shape[-1]
    came, mine = wide.at[0, slot], wide.at[1, slot]
    side, kept, got_y, s3, got_z, s4, got_zz, s5 = [narrow.at[i, slot] for i in range(8)]

    def remote(k):
        src, dst = (
            (oth.at[rows], came),
            (side, got_y),
            (s3, got_z),
            (s4, got_zz),
            (s5, out.at[1, rows]),
            (s5, out.at[2, rows]),
            (out.at[1, rows], out.at[3, rows]),
        )[k]
        return remote_copy(src, dst, send.at[k, slot], recv.at[k, slot], HBM_LINKS[k])

    def load():
        return pltpu.make_async_copy(own.at[rows], mine, local.at[0, slot])

    def keep():
        return pltpu.make_async_copy(s5, out.at[0, rows], local.at[1, slot])

    if stage == 0:
        remote(0).start()
        load().start()
    elif stage == 1:
        remote(0).wait()
        load().wait()
        v = came[...] + mine[...]
        side[...] = v[:, w:]
        kept[...] = v[:, :w]
        remote(1).start()
    elif stage == 2:
        remote(1).wait()
        s3[...] = kept[...] + got_y[...]
        remote(2).start()
    elif stage == 3:
        remote(2).wait()
        s4[...] = s3[...] + got_z[...]
        remote(3).start()
    elif stage == 4:
        remote(3).wait()
        s5[...] = s4[...] + got_zz[...]
        remote(4).start()
        remote(5).start()
        keep().start()
    elif stage == 5:
        remote(4).wait()
        remote(5).wait()
        keep().wait()
        remote(6).start()
    else:
        remote(6).wait()


def pair_scratch(w):
    return [
        pltpu.VMEM((2, 2, 2, 2, SUBS, CHUNK, w), bf16),
        pltpu.VMEM((SLOTS, 2, 2, CHUNK, w), bf16),
        pltpu.VMEM((3, SLOTS, 2, CHUNK, w), bf16),
        pltpu.VMEM((6, SLOTS, CHUNK, w), bf16),
        dma_sem((8, SLOTS)),
        dma_sem((8, SLOTS)),
        dma_sem((SLOTS,)),
    ]


def pair_stage(stage, c, out, prod, near, wide, narrow, send, recv, local):
    d = lax.axis_index("dp")
    core = d % 2
    y = (d // 2) % 2
    slot = lax.rem(c, SLOTS)
    pair = c // SUBS
    place = pair - jnp.where(pair > PAIRS_HERE, 1, 0)
    sub = lax.rem(c, SUBS)
    par = lax.rem(pair, 2)
    away, came, own = [wide.at[i, slot] for i in range(3)]
    got_y, s3, got_z, s4, got_zz, s5 = [narrow.at[i, slot] for i in range(6)]

    def remote(k):
        src, dst = (
            (prod.at[par, :, 1 - core, :, sub], near.at[slot]),
            (away, came),
            (own.at[1 - y], got_y),
            (s3, got_z),
            (s4, got_zz),
            (s5, out.at[place, core, y, sub]),
            (s5, out.at[place, core, y, sub]),
            (out.at[place, core, 1 - y, sub], out.at[place, core, 1 - y, sub]),
        )[k]
        return remote_copy(src, dst, send.at[k, slot], recv.at[k, slot], PAIR_LINKS[k])

    def keep():
        return pltpu.make_async_copy(s5, out.at[place, core, y, sub], local.at[slot])

    if stage == 0:
        remote(0).start()
    elif stage == 1:
        remote(0).wait()
        away[...] = prod[par, 1, core, :, sub] + near[slot, 1]
        own[...] = prod[par, 0, core, :, sub] + near[slot, 0]
        remote(1).start()
    elif stage == 2:
        remote(1).wait()
        own[...] = own[...] + came[...]
        remote(2).start()
    elif stage == 3:
        remote(2).wait()
        s3[...] = wide[2, slot, y] + got_y[...]
        remote(3).start()
    elif stage == 4:
        remote(3).wait()
        s4[...] = s3[...] + got_z[...]
        remote(4).start()
    elif stage == 5:
        remote(4).wait()
        s5[...] = s4[...] + got_zz[...]
        remote(5).start()
        remote(6).start()
        keep().start()
    elif stage == 6:
        remote(5).wait()
        remote(6).wait()
        keep().wait()
        remote(7).start()
    else:
        remote(7).wait()


def small_scratch(shape):
    return [pltpu.VMEM((6,) + shape, f32), pltpu.VMEM((5,) + shape, f32), dma_sem((5,)), dma_sem((5,))]


def small_stage(k, out, acc, got, send, recv):
    def remote(i):
        return remote_copy(acc.at[i], got.at[i], send.at[i], recv.at[i], i)

    if k > 0:
        remote(k - 1).wait()
        acc[k] = acc[k - 1] + got[k - 1]
    if k < 5:
        remote(k).start()
    else:
        out[...] = acc[5]


HALF_STEPS = 2 * PAIRS_HERE
BETWEEN = 4 * HALF_STEPS
AFTER = BETWEEN + SUBS
CHUNKS = 2 * PAIRS_HERE * SUBS + SUBS
WHOLE = 1024 // CHUNK
TICKS = CHUNKS + LEAD + 7 * DELAY
TILE = 256


def between_step(dq2, cq, so, gain_ref, sum_ref, base_ref, dz_ref, dc1, g1_t, acc, zt, bt, sems, tick):
    def fetch_tile(a):
        rows = pl.ds(a * TILE, TILE)
        return [
            pltpu.make_async_copy(sum_ref.at[rows], zt.at[a % 2], sems.at[0, a % 2]),
            pltpu.make_async_copy(base_ref.at[rows], bt.at[a % 2], sems.at[1, a % 2]),
        ]

    def put_tile(a):
        return pltpu.make_async_copy(bt.at[a % 2], dz_ref.at[pl.ds(a * TILE, TILE)], sems.at[2, a % 2])

    tiles = dc1.shape[1] // TILE
    for copy in fetch_tile(0):
        copy.start()
    for a in range(tiles):
        rows = slice(a * TILE, (a + 1) * TILE)
        for copy in fetch_tile(a):
            copy.wait()
        if a >= 1:
            put_tile(a - 1).wait()
        if a + 1 < tiles:
            for copy in fetch_tile(a + 1):
                copy.start()
        z = zt[a % 2]
        dh = bt[a % 2]
        for i in BOTH:
            dh = dh + dot(dq2[i, rows, :], cq[i][...], NT)
        centered = z - jnp.mean(z, axis=1, keepdims=True)
        r = lax.rsqrt(jnp.mean(centered * centered, axis=1, keepdims=True) + norm_eps)
        n = centered * r
        acc[0, 0:1, :] = acc[0, 0:1, :] + jnp.sum(dh * n, axis=0, keepdims=True)
        acc[0, 3:4, :] = acc[0, 3:4, :] + jnp.sum(dh, axis=0, keepdims=True)
        e = dh * gain_ref[0:1, :]
        dz = r * (e - jnp.mean(e, axis=1, keepdims=True) - n * jnp.mean(e * n, axis=1, keepdims=True))
        bt[a % 2] = dz
        put_tile(a).start()
        g = dz.astype(bf16)
        g1_t[:, rows] = g.T
        for i in BOTH:
            dc1[i, rows, :] = dot(g, so[i][...], NT).astype(bf16)
        tick(BETWEEN + 2 * a)
        tick(BETWEEN + 2 * a + 1)
    put_tile(tiles - 1).wait()


def back_kernel(*refs):
    refs = list(refs)
    take = lambda n: [refs.pop(0) for _ in range(n)]
    (len_ref,) = take(1)
    cross_in = [take(6) for _ in BOTH]
    self_in = [take(5) for _ in BOTH]
    h1_t, mem_t, g2_t, tar_t = take(4)
    cq, so = take(2), take(2)
    gain_ref, small_ref, sum_ref, base_ref = take(4)
    down_in, up_in = take(2), take(2)
    dk2_ref, dv2_ref, dq1_ref, dk1_ref, dv1_ref, dz_ref, pair_out, down_out, up_out, small_out = take(10)
    grads, *scratch = take(8)
    pair_refs = [pair_out] + take(7)
    down_refs = down_in + [down_out] + take(5)
    up_refs = up_in + [up_out] + take(5)
    small_refs = [small_out] + take(4)
    acc = small_refs[1]
    dq2, dc1, g1_t, zt, bt, sems = take(6)
    step = pl.program_id(0)
    prod = pair_refs[1]

    def tick(t):
        for stage in range(7, -1, -1):
            c = t - LEAD - DELAY * stage
            real = (c >= 0) & (c < CHUNKS) & ((c < PAIRS_HERE * SUBS) | (c >= (PAIRS_HERE + 1) * SUBS))
            pl.when(real)(functools.partial(pair_stage, stage, c, *pair_refs))
        for first, whole_refs in ((0, down_refs), (WHOLE, up_refs)):
            for stage in range(6, -1, -1):
                c = t - first - DELAY * stage
                pl.when((c >= 0) & (c < WHOLE))(functools.partial(whole_stage, stage, c, *whole_refs))
        for k in range(5, -1, -1):
            pl.when(t == AFTER + 2 * k)(functools.partial(small_stage, k, *small_refs))

    half = lax.rem(step, 2)

    def products(pair, spans):
        par = lax.rem(pair, 2)
        for a in range(4):
            rows = slice(a * TILE, (a + 1) * TILE)
            at = prod.at[par, half, a // 2, a % 2]
            for left, lo, hi in spans:
                at[:, :, lo:hi] = dot(left[rows, :], grads[:, lo:hi]).astype(bf16).reshape(SUBS, CHUNK, hi - lo)

    @pl.when(step == 0)
    def _():
        greet()
        acc[0] = small_ref[...]

    @pl.when(step < HALF_STEPS)
    def _():
        pair = step // 2
        q2, k2, v2, c2, aug, g2 = [jnp.where(half == 0, a[...], b[...]) for a, b in zip(*cross_in)]
        back_pair(False, len_ref[0], q2, k2, v2, c2, aug, g2, grads, scratch, lambda j: tick(4 * step + j))
        dq2[half, :, pl.ds(pl.multiple_of(pair * 128, 128), 128)] = grads[:, :128]
        dk2_ref[...] = grads[:, 128:256]
        dv2_ref[...] = grads[:, 256:384]
        products(pair, ((h1_t, 0, 128), (mem_t, 128, 384), (g2_t, 384, 512)))

    @pl.when(step == HALF_STEPS)
    def _():
        between_step(dq2, cq, so, gain_ref, sum_ref, base_ref, dz_ref, dc1, g1_t, acc, zt, bt, sems, tick)

    @pl.when(step >= HALF_STEPS)
    def _():
        pair = step // 2 - PAIRS_HERE
        q2, k2, v2, c2, aug = [jnp.where(half == 0, a[...], b[...]) for a, b in zip(*self_in)]
        g2 = dc1[half, :, pl.ds(pl.multiple_of(pair * 128, 128), 128)]
        back_pair(True, 0, q2, k2, v2, c2, aug, g2, grads, scratch, lambda j: tick(4 * step + SUBS + j))
        dq1_ref[...] = grads[:, :128]
        dk1_ref[...] = grads[:, 128:256]
        dv1_ref[...] = grads[:, 256:384]
        products(pair + PAIRS_HERE + 1, ((tar_t, 0, 384), (g1_t, 384, 512)))

    @pl.when(step == 2 * HALF_STEPS - 1)
    def _():
        pl.loop(4 * 2 * HALF_STEPS + SUBS, TICKS)(tick)


def attention_back(length, cross_in, self_in, lefts, cq, so, gain, small, sums, base, down, up):
    seq, width = cross_in[0][0].shape
    w = down[0].shape[1] // 2
    low = lambda s: jnp.minimum(s, HALF_STEPS - 1)
    high = lambda s: jnp.maximum(s - HALF_STEPS, 0)
    cross_spec = pl.BlockSpec((seq, 128), lambda s: (0, low(s) // 2))
    self_spec = pl.BlockSpec((seq, 128), lambda s: (0, high(s) // 2))
    cross_out = pl.BlockSpec((None, seq, 128), lambda s: (low(s) % 2, 0, low(s) // 2))
    self_out = pl.BlockSpec((None, seq, 128), lambda s: (high(s) % 2, 0, high(s) // 2))
    anywhere = pl.BlockSpec(memory_space=pl.ANY)
    full = lambda x: pl.BlockSpec(x.shape, lambda s: (0, 0), pipeline_mode=pl.Buffered(1))
    shape = jax.ShapeDtypeStruct
    return pl.pallas_call(
        back_kernel,
        grid=(2 * HALF_STEPS,),
        in_specs=[pl.BlockSpec(memory_space=pltpu.SMEM)]
        + [cross_spec] * 12
        + [self_spec] * 10
        + [full(x) for x in (*lefts, *cq, *so, gain, small)]
        + [anywhere] * 6,
        out_specs=[cross_out] * 2 + [self_out] * 3 + [anywhere] * 4 + [full(small)],
        out_shape=[shape((2, seq, width), bf16)] * 5
        + [
            shape((seq, sums.shape[1]), f32),
            shape((2 * PAIRS_HERE, 2, 2, SUBS, CHUNK, 512), bf16),
            shape((4, seq, w), bf16),
            shape((4, seq, w), bf16),
            shape(small.shape, f32),
        ],
        scratch_shapes=[pltpu.VMEM((seq, 512), bf16)]
        + back_scratch(seq)
        + pair_scratch(512)
        + whole_scratch(w) * 2
        + small_scratch(small.shape)
        + [
            pltpu.VMEM((2, seq, width), bf16),
            pltpu.VMEM((2, seq, width), bf16),
            pltpu.VMEM((sums.shape[1], seq), bf16),
            pltpu.VMEM((2, TILE, sums.shape[1]), f32),
            pltpu.VMEM((2, TILE, sums.shape[1]), f32),
            dma_sem((3, 2)),
        ],
        compiler_params=pltpu.CompilerParams(
            collective_id=1, has_side_effects=True, vmem_limit_bytes=60 * 2**20
        ),
        cost_estimate=cost(12, 8, seq, False),
        name="attention_back",
    )(length, *cross_in[0], *cross_in[1], *self_in[0], *self_in[1], *lefts, *cq, *so, gain, small, sums, base, *down, *up)


ALL = ("dp", "tensor")
DEVICES = 32


def swap(x, flip):
    return lax.ppermute(x, ALL, [(i, i ^ flip) for i in range(DEVICES)])


def swap_tensor(x):
    return swap(x, 1)


def swap_core(x):
    return swap(x, 2)


def swap_y(x):
    return swap(x, 4)


def my_block():
    d = lax.axis_index("dp")
    return 2 * (d % 2) + (d // 2) % 2


def add_low(*terms):
    return sum(t.astype(f32) for t in terms).astype(bf16)


def blocks_of(own, axis):
    size = own.shape[axis] // 4
    return [lax.dynamic_slice_in_dim(own, (my_block() ^ j) * size, size, axis) for j in range(4)]


def swap_pieces(x, move):
    return [move(p) for p in x] if isinstance(x, (list, tuple)) else move(x)


def tie(*xs):
    return lax.optimization_barrier(xs)


class Pipe:
    def __init__(self):
        self.live = []

    def put(self, gen):
        wait, arrays = next(gen)
        self.live.append([gen, wait, arrays])

    def step(self, due, landed):
        done = 0
        for item in due:
            arrays = landed[done : done + len(item[2])]
            done += len(item[2])
            try:
                item[1], item[2] = item[0].send(arrays)
            except StopIteration:
                self.live.remove(item)

    def cut(self, *xs):
        due = []
        for item in self.live:
            item[1] -= 1
            if item[1] <= 0:
                due.append(item)
        tied = tie(*xs, *[a for item in due for a in item[2]])
        self.step(due, tied[len(xs) :])
        return tied[: len(xs)] if len(xs) > 1 else tied[0]

    def drain(self):
        while self.live:
            self.step(list(self.live), [a for item in self.live for a in item[2]])


def fetch(out, key, block, waits):
    far = swap_tensor(block)
    (far,) = yield waits[0], [far]
    side = swap_y(far)
    near = swap_core(far)
    side, near = yield waits[1], [side, near]
    out[key] = [far, side, near, swap_core(side)]
    return


def assemble_kernel(axis, me_ref, x_ref, out_ref):
    x = x_ref[...].astype(f32)
    out_ref[...] = x.T if axis == 0 else x


def assemble(blocks, axis, members=1):
    _, rows, width = blocks.shape
    tiles = 2
    high = rows // tiles
    narrow = width // members
    if axis == 0:
        out_spec = pl.BlockSpec((narrow, high), lambda b, m, t, me: (b ^ me[0], t))
        shape = (4 * width, rows)
    else:
        out_spec = pl.BlockSpec((None, high, narrow), lambda b, m, t, me: (m, t, b ^ me[0]))
        shape = (members, rows, narrow * 4)
    return pl.pallas_call(
        functools.partial(assemble_kernel, axis),
        grid_spec=pltpu.PrefetchScalarGridSpec(
            num_scalar_prefetch=1,
            grid=(4, members, tiles),
            in_specs=[pl.BlockSpec((None, high, narrow), lambda b, m, t, me: (b, t, m))],
            out_specs=out_spec,
        ),
        out_shape=jax.ShapeDtypeStruct(shape, f32),
        compiler_params=pltpu.CompilerParams(vmem_limit_bytes=40 * 2**20),
        cost_estimate=pl.CostEstimate(flops=0, bytes_accessed=24 * rows * width, transcendentals=0),
        name="assemble",
    )(my_block().reshape(1), blocks)


def core_sum(part):
    send = [part(i, 2).astype(bf16) for i in BOTH]
    got = [swap_core(x) for x in send]
    keep = [add_low(part(i, 0), got[i]) for i in BOTH]
    return keep[1], keep[0]


def ffn_kernel(h_ref, *refs):
    ups, downs = refs[:4], refs[4:8]
    a_ref, d_ref, b_ref = refs[8:]
    h = h_ref[...]
    size = ups[0].shape[1]
    total = None
    for j in range(4):
        u = dot(h, ups[j][...])
        cdf = 0.5 + 0.5 * lax.erf(u * (0.5**0.5))
        slope = cdf + u * (jnp.exp(-0.5 * u * u) * 0.3989422804014327)
        act = (u * cdf).astype(bf16)
        cols = slice(j * size, (j + 1) * size)
        a_ref[:, cols] = act
        d_ref[:, cols] = slope.astype(bf16)
        term = dot(act, downs[j][...])
        total = term if total is None else total + term
    b_ref[...] = total


def whole(x):
    return pl.BlockSpec(x.shape, lambda r: (0, 0))


ROWS = 256


def ffn_forward(h, ups, downs):
    seq, width = h.shape
    units = 4 * ups[0].shape[1]
    rows = lambda w: pl.BlockSpec((ROWS, w), lambda r: (r, 0))
    return pl.pallas_call(
        ffn_kernel,
        grid=(seq // ROWS,),
        in_specs=[rows(width)] + [whole(x) for x in ups + downs],
        out_specs=[rows(units), rows(units), rows(width)],
        out_shape=[jax.ShapeDtypeStruct((seq, units), bf16)] * 2 + [jax.ShapeDtypeStruct((seq, width), f32)],
        compiler_params=pltpu.CompilerParams(vmem_limit_bytes=50 * 2**20),
        cost_estimate=pl.CostEstimate(flops=4 * seq * width * units, bytes_accessed=22 * 2**20, transcendentals=2 * seq * units),
        name="feed_forward",
    )(h, *ups, *downs)


def ffn_back_kernel(g_ref, d_ref, *refs):
    ups, downs = refs[:4], refs[4:8]
    du_ref, dh_ref = refs[-2:]
    g = g_ref[...]
    size = ups[0].shape[1]
    total = refs[8][...] if len(refs) > 10 else None
    for j in range(4):
        cols = slice(j * size, (j + 1) * size)
        du = (dot(g, downs[j][...], NT) * d_ref[:, cols].astype(f32)).astype(bf16)
        du_ref[:, cols] = du
        term = dot(du, ups[j][...], NT)
        total = term if total is None else total + term
    dh_ref[...] = total


def ffn_backward(g, slope, ups, downs, before=None):
    seq, width = g.shape
    units = slope.shape[1]
    rows = lambda w: pl.BlockSpec((ROWS, w), lambda r: (r, 0))
    extra = [] if before is None else [before]
    return pl.pallas_call(
        ffn_back_kernel,
        grid=(seq // ROWS,),
        in_specs=[rows(width), rows(units)] + [whole(x) for x in ups + downs] + [rows(width)] * len(extra),
        out_specs=[rows(units), rows(width)],
        out_shape=[jax.ShapeDtypeStruct((seq, units), bf16), jax.ShapeDtypeStruct((seq, width), f32)],
        compiler_params=pltpu.CompilerParams(vmem_limit_bytes=50 * 2**20),
        cost_estimate=pl.CostEstimate(flops=4 * seq * width * units, bytes_accessed=22 * 2**20, transcendentals=0),
        name="feed_forward_back",
    )(g, slope, *ups, *downs, *extra)


def side_by_side(parts):
    return jnp.concatenate(parts, axis=1)


def cols(x, first, last, of=4):
    size = x.shape[1] // of
    return x[:, first * size : last * size]


def arrange_kernel(me_ref, *refs):
    for j in range(4):

        @pl.when(pl.program_id(0) == j)
        def _(j=j):
            refs[4][...] = refs[j][...]


def arrange(slabs):
    members, rows, width = slabs[0].shape
    return pl.pallas_call(
        arrange_kernel,
        grid_spec=pltpu.PrefetchScalarGridSpec(
            num_scalar_prefetch=1,
            grid=(4,),
            in_specs=[pl.BlockSpec((members, rows, width), lambda j, me: (0, 0, 0))] * 4,
            out_specs=pl.BlockSpec((members, rows, width), lambda j, me: (0, j ^ me[0], 0)),
        ),
        out_shape=jax.ShapeDtypeStruct((members, 4 * rows, width), bf16),
        compiler_params=pltpu.CompilerParams(vmem_limit_bytes=40 * 2**20),
        cost_estimate=pl.CostEstimate(flops=0, bytes_accessed=16 * members * rows * width, transcendentals=0),
        name="arrange",
    )(my_block().reshape(1), *slabs)


def slab_of(own):
    rows = own.shape[1] // 4
    return lax.dynamic_slice_in_dim(own, my_block() * rows, rows, 1)


def spread_kernel(spans, x_ref, *out_refs):
    for lo, hi, k, m in spans:
        x = x_ref[:, lo:hi].astype(f32)
        if m is None:
            out_refs[k][...] = x.T
        else:
            out_refs[k][m] = x


def spread(pairs, first, spans, outs):
    _, rows, width = pairs.shape
    tile = 512
    specs = []
    shapes = []
    for members in outs:
        if members is None:
            specs.append(pl.BlockSpec((128, tile), lambda p, t: (p, t)))
            shapes.append(jax.ShapeDtypeStruct((512, rows), f32))
        else:
            specs.append(pl.BlockSpec((members, tile, 128), lambda p, t: (0, t, p)))
            shapes.append(jax.ShapeDtypeStruct((members, rows, 512), f32))
    return pl.pallas_call(
        functools.partial(spread_kernel, spans),
        grid=(4, rows // tile),
        in_specs=[pl.BlockSpec((None, tile, width), lambda p, t: (p + first, t, 0))],
        out_specs=specs,
        out_shape=shapes,
        compiler_params=pltpu.CompilerParams(vmem_limit_bytes=40 * 2**20),
        cost_estimate=pl.CostEstimate(flops=0, bytes_accessed=24 * rows * width, transcendentals=0),
        name="spread",
    )(pairs)


def flip_kernel(x_ref, out_ref):
    out_ref[...] = x_ref[...].T


def flip(x):
    rows, width = x.shape
    return pl.pallas_call(
        flip_kernel,
        grid=(4,),
        in_specs=[pl.BlockSpec((rows // 4, width), lambda i: (i, 0))],
        out_specs=pl.BlockSpec((width, rows // 4), lambda i: (0, i)),
        out_shape=jax.ShapeDtypeStruct((width, rows), x.dtype),
        cost_estimate=pl.CostEstimate(flops=0, bytes_accessed=4 * rows * width, transcendentals=0),
        name="flip",
    )(x)


def one_pair_each(
    target,
    memory,
    mem_len,
    grad_out,
    self_qkv,
    self_out,
    cross_query,
    cross_kv,
    cross_out,
    ffn_up,
    ffn_down,
    ln_gain,
    ln_bias,
):
    length = lax.dynamic_slice_in_dim(mem_len, lax.axis_index("tensor"), 1)
    pipe = Pipe()
    got = {}
    so3, cq3, co3 = self_out[None], cross_query[None], cross_out[None]

    pipe.put(fetch(got, "qkv", slab_of(self_qkv), (1, 1)))
    q1 = [[dot(target, self_qkv[m]).astype(bf16) for m in range(3)], None]
    at1 = [attend_fwd(*q1[0], length, True), None]
    so_s, cq_s, kv_s, co_s = [slab_of(x) for x in (so3, cq3, cross_kv, co3)]
    mem, so_s, cq_s, kv_s, _ = pipe.cut(memory, so_s, cq_s, kv_s, at1[0][0])
    pipe.put(fetch(got, "so", so_s, (1, 1)))
    pipe.put(fetch(got, "cq", cq_s, (1, 1)))
    pipe.put(fetch(got, "kv", kv_s, (1, 1)))
    kv = [[dot(mem, cross_kv[m]).astype(bf16) for m in range(2)], None]
    up_b = blocks_of(ffn_up, 1)
    down_b = blocks_of(ffn_down, 0)
    target_t = flip(target)
    memory_t = flip(mem)
    *_, up_b[0], co_s, target_t, memory_t = tie(*kv[0], *up_b[1:], *down_b, up_b[0], co_s, target_t, memory_t)
    tar = pipe.cut(target)
    qkv_oth = arrange(got["qkv"])
    q1[1] = [dot(tar, qkv_oth[m]).astype(bf16) for m in range(3)]
    pipe.put(fetch(got, "co", co_s, (1, 1)))
    q1[1][0], up_b[0] = tie(q1[1][0], up_b[0])
    pipe.put(fetch(got, "up", up_b[0], (2, 1)))
    at1[1] = attend_fwd(*q1[1], length, True)
    at1[1], _ = tie(at1[1], at1[1][0])
    c1_oth = pipe.cut(at1[1][0])
    c1 = [at1[0][0], c1_oth]
    so_oth = arrange(got["so"])[0]
    b1 = dot(c1[0], self_out) + dot(c1[1], so_oth)
    h1 = norm_rows(alpha_res * target.astype(f32) + b1, ln_gain[0], ln_bias[0])
    h1_low = h1.astype(bf16)
    cq_oth = arrange(got["cq"])[0]
    kv_oth = arrange(got["kv"])
    q2 = [dot(h1_low, cross_query).astype(bf16), dot(h1_low, cq_oth).astype(bf16)]
    kv[1] = [dot(memory, kv_oth[m]).astype(bf16) for m in range(2)]
    q2[0], kv[1][0], down_b[0] = pipe.cut(q2[0], kv[1][0], down_b[0])
    pipe.put(fetch(got, "down", down_b[0], (1, 1)))
    at2 = [attend_fwd(q2[0], *kv[0], length, False), None]
    q2[1], _ = pipe.cut(q2[1], at2[0][0])
    at2[1] = attend_fwd(q2[1], *kv[1], length, False)
    co_oth = arrange(got["co"])[0]
    c2 = [at2[0][0], at2[1][0]]
    c2[1] = pipe.cut(c2[1])
    b2 = dot(c2[0], cross_out) + dot(c2[1], co_oth)
    h2, back2 = jax.vjp(norm_rows, alpha_res * h1 + b2, ln_gain[1], ln_bias[1])
    h2_low = h2.astype(bf16)
    act0, slope0, b3 = ffn_forward(h2_low, up_b, down_b)
    h1_t = flip(h1_low)
    while "up" not in got or "down" not in got:
        act0 = pipe.cut(act0)
    h2_again, _ = tie(h2_low, act0)
    act1, slope1, b3b = ffn_forward(h2_again, got["up"], got["down"])
    act, slope = (act0, act1), (slope0, slope1)
    result, back3 = jax.vjp(norm_rows, alpha_res * h2 + b3 + b3b, ln_gain[2], ln_bias[2])

    dz3, gain3, bias3 = back3(grad_out.astype(f32))
    g3 = dz3.astype(bf16)

    def down_part(i, f):
        return dot(g3, cols(act[i], f, f + 2), TN)

    down_send = [down_part(i, 2).astype(bf16) for i in BOTH]
    g3, *down_send = tie(g3, *down_send)
    down_got = [swap_core(x) for x in down_send]
    du1, dh2 = ffn_backward(g3, slope[1], got["up"], got["down"])
    g3, dh2, *down_got = tie(g3, dh2, *down_got)
    down_pair = (add_low(down_part(1, 0), down_got[1]), add_low(down_part(0, 0), down_got[0]))
    du0, dh2 = ffn_backward(g3, slope[0], up_b, down_b, dh2)
    du = (du0, du1)

    def up_part(i, f):
        return dot(h2_low, cols(du[i], f, f + 2), TN)

    up_send = [up_part(i, 2).astype(bf16) for i in BOTH]
    dh2, *up_send = tie(dh2, *up_send)
    up_got = [swap_core(x) for x in up_send]
    dz2, gain2, bias2 = back2(alpha_res * dz3 + dh2)
    g2 = dz2.astype(bf16)
    dc2 = [dot(g2, w, NT).astype(bf16) for w in (cross_out, co_oth)]
    g2_t = flip(g2)
    dc2[0], dc2[1], g2_t, *up_got = tie(*dc2, g2_t, *up_got)
    up_pair = (add_low(up_part(1, 0), up_got[1]), add_low(up_part(0, 0), up_got[0]))
    halves2 = [[q2[i], *kv[i], c2[i], at2[i][1], dc2[i]] for i in BOTH]
    halves1 = [[*q1[i], c1[i], at1[i][1]] for i in BOTH]
    none = jnp.zeros_like(gain2)
    small = jnp.stack([none, gain2, gain3, none, bias2, bias3, none, none])
    dk2, dv2, dq1, dk1, dv1, dz1, pairs, down_t, up_t, small = attention_back(
        length,
        halves2,
        halves1,
        [h1_t, memory_t, g2_t, target_t],
        (cross_query, cq_oth),
        (self_out, so_oth),
        ln_gain,
        small,
        alpha_res * target.astype(f32) + b1,
        alpha_res * dz2,
        down_pair,
        up_pair,
    )
    pairs = pairs.reshape(8, 1024, 512)
    cross_pairs, self_pairs = (pairs, 0), (pairs, 4)
    kv_both = (cross_kv, kv_oth)
    dmem = sum(dot(d[i], kv_both[i][m], NT) for i in BOTH for m, d in enumerate((dk2, dv2)))
    qkv_both = (self_qkv, qkv_oth)
    dtar = alpha_res * dz1 + sum(dot(d[i], qkv_both[i][m], NT) for i in BOTH for m, d in enumerate((dq1, dk1, dv1)))
    cq_total, kv_total, co_total = spread(
        *cross_pairs,
        ((0, 128, 0, 0), (128, 256, 1, 0), (256, 384, 1, 1), (384, 512, 2, None)),
        (1, 2, None),
    )
    qkv_total, so_total = spread(
        *self_pairs,
        ((0, 128, 0, 0), (128, 256, 0, 1), (256, 384, 0, 2), (384, 512, 1, None)),
        (3, None),
    )
    return (
        result.astype(bf16),
        dtar.astype(bf16),
        dmem.astype(bf16),
        qkv_total,
        so_total,
        cq_total[0],
        kv_total,
        co_total,
        assemble(up_t, 1)[0],
        assemble(down_t, 0),
        small[:3],
        small[3:6],
    )


def solution(mesh):
    placed = (
        P(("dp", "tensor"), None),
        P(("dp", "tensor"), None),
        P("dp"),
        P(("dp", "tensor"), None),
        P(None, None, "tensor"),
        P("tensor", None),
        P(None, "tensor"),
        P(None, None, "tensor"),
        P("tensor", None),
        P(None, "tensor"),
        P("tensor", None),
        P(),
        P(),
    )
    body = one_pair_each if mesh.shape["tensor"] == 2 and mesh.shape["dp"] == 16 else on_device
    return jax.shard_map(
        body,
        mesh=mesh,
        in_specs=placed,
        out_specs=(
            P(("dp", "tensor"), None),
            P(("dp", "tensor"), None),
            P(("dp", "tensor"), None),
            P(None, None, "tensor"),
            P("tensor", None),
            P(None, "tensor"),
            P(None, None, "tensor"),
            P("tensor", None),
            P(None, "tensor"),
            P("tensor", None),
            P(),
            P(),
        ),
        check_vma=False,
    )
```

```python
import functools

import jax
import jax.numpy as jnp
from jax import lax
from jax.experimental import pallas as pl
from jax.experimental.pallas import tpu as pltpu
from jax.sharding import PartitionSpec as P

HD = 64


alpha_res = 300.0**0.25
norm_eps = 1e-05
mask_fill = -1e30
contract_rows = (((0,), (0,)), ((), ()))
contract_cols = (((1,), (1,)), ((), ()))


def norm_rows(resid, gain_vec, bias_vec):
    average = jnp.mean(resid, axis=-1, keepdims=True)
    centered = resid - average
    variance = jnp.mean(centered * centered, axis=-1, keepdims=True)
    return centered * lax.rsqrt(variance + norm_eps) * gain_vec + bias_vec


def exact_gelu(values_in):
    return jax.nn.gelu(values_in, approximate=False)


def gather_rows(local_rows):
    return lax.all_gather(local_rows, "tensor", axis=0, tiled=True)


def gather_grads(local_rows):
    return lax.all_gather(local_rows, "tensor", axis=0, tiled=True)


def scatter_branch(left_mat, right_mat, row_count):

    def partial_term(offset, num_rows):
        return jnp.dot(left_mat, right_mat, preferred_element_type=jnp.float32)

    return lax.psum_scatter(
        partial_term(jnp.int32(0), row_count * lax.axis_size("tensor")),
        "tensor",
        scatter_dimension=0,
        tiled=True,
    )


def project_context(context, weight_local, row_count):
    return scatter_branch(context, weight_local, row_count)


def scatter_inputs(factor_pairs, row_count):

    def partial_term(offset, num_rows):
        terms = [
            lax.dot_general(grad_mat, weight_mat, contract_cols, preferred_element_type=jnp.float32)
            for grad_mat, weight_mat in factor_pairs
        ]
        return sum(terms)

    return lax.psum_scatter(
        partial_term(jnp.int32(0), row_count * lax.axis_size("tensor")).astype(jnp.bfloat16),
        "tensor",
        scatter_dimension=0,
        tiled=True,
    ).astype(jnp.float32)


def block_view(flat, pair_count, block_rows):
    tok_count, col_count = flat.shape
    seq_len = tok_count // pair_count
    return flat.reshape(pair_count, seq_len // block_rows, block_rows, col_count // HD, HD)


def pair_view(flat, pair_count):
    tok_count, col_count = flat.shape
    return flat.reshape(pair_count, tok_count // pair_count, col_count // HD, HD)


def block_scores(query_blk, key_pair, start_row, key_len, causal):
    block_rows = query_blk.shape[0]
    seq_len = key_pair.shape[0]
    products = jnp.einsum(
        "qhd,khd->hqk", query_blk, key_pair, preferred_element_type=jnp.float32
    ) * HD ** (-0.5)
    key_pos = lax.broadcasted_iota(jnp.int32, (block_rows, seq_len), 1)
    query_pos = start_row + lax.broadcasted_iota(jnp.int32, (block_rows, seq_len), 0)
    allowed = key_pos < key_len
    if causal:
        allowed = allowed & (key_pos <= query_pos)
    return jnp.where(allowed[None], products, mask_fill)


def attend_forward(queries, key_rows, value_rows, key_lens, causal):
    pair_count = key_lens.shape[0]
    seq_len = queries.shape[0] // pair_count
    block_rows = min(512, seq_len)
    starts = lax.iota(jnp.int32, seq_len // block_rows) * block_rows

    def one_pair(packed):
        query_pair, key_pair, value_pair, key_len = packed

        def one_block(inner):
            query_blk, start_row = inner
            scores = block_scores(query_blk, key_pair, start_row, key_len, causal)
            row_max = jnp.max(scores, axis=-1, keepdims=True)
            shifted = jnp.exp(scores - row_max)
            row_total = jnp.sum(shifted, axis=-1, keepdims=True)
            attn_prob = (shifted / row_total).astype(jnp.bfloat16)
            context = jnp.einsum(
                "hqk,khd->qhd", attn_prob, value_pair, preferred_element_type=jnp.float32
            )
            return (context.astype(jnp.bfloat16), (row_max + jnp.log(row_total))[..., 0])

        return lax.map(one_block, (query_pair, starts))

    context, log_total = lax.map(
        one_pair,
        (
            block_view(queries, pair_count, block_rows),
            pair_view(key_rows, pair_count),
            pair_view(value_rows, pair_count),
            key_lens,
        ),
    )
    return (context.reshape(queries.shape), log_total)


def attend_backward(queries, key_rows, value_rows, key_lens, causal, log_total, grad_context):
    pair_count = key_lens.shape[0]
    seq_len = queries.shape[0] // pair_count
    block_rows = min(512, seq_len)
    starts = lax.iota(jnp.int32, seq_len // block_rows) * block_rows
    score_scale = HD ** (-0.5)

    def one_pair(packed):
        query_pair, key_pair, value_pair, key_len, total_pair, grad_pair = packed

        def one_block(carry, inner):
            key_grad, value_grad = carry
            query_blk, start_row, total_blk, grad_blk = inner
            scores = block_scores(query_blk, key_pair, start_row, key_len, causal)
            attn_prob = jnp.exp(scores - total_blk[..., None])
            value_grad = value_grad + jnp.einsum(
                "hqk,qhd->khd",
                attn_prob.astype(jnp.bfloat16),
                grad_blk,
                preferred_element_type=jnp.float32,
            )
            prob_grad = jnp.einsum(
                "qhd,khd->hqk", grad_blk, value_pair, preferred_element_type=jnp.float32
            )
            score_grad = (
                attn_prob * (prob_grad - jnp.sum(attn_prob * prob_grad, axis=-1, keepdims=True))
            ).astype(jnp.bfloat16)
            query_grad = (
                jnp.einsum("hqk,khd->qhd", score_grad, key_pair, preferred_element_type=jnp.float32)
                * score_scale
            )
            key_grad = (
                key_grad
                + jnp.einsum(
                    "hqk,qhd->khd", score_grad, query_blk, preferred_element_type=jnp.float32
                )
                * score_scale
            )
            return ((key_grad, value_grad), query_grad.astype(jnp.bfloat16))

        zeros = jnp.zeros(key_pair.shape, jnp.float32)
        (key_grad, value_grad), query_grad = lax.scan(
            one_block, (zeros, zeros), (query_pair, starts, total_pair, grad_pair)
        )
        return (query_grad, key_grad.astype(jnp.bfloat16), value_grad.astype(jnp.bfloat16))

    query_grad, key_grad, value_grad = lax.map(
        one_pair,
        (
            block_view(queries, pair_count, block_rows),
            pair_view(key_rows, pair_count),
            pair_view(value_rows, pair_count),
            key_lens,
            log_total,
            block_view(grad_context, pair_count, block_rows),
        ),
    )
    return (
        query_grad.reshape(queries.shape),
        key_grad.reshape(queries.shape),
        value_grad.reshape(queries.shape),
    )


def on_device(
    target,
    memory,
    mem_len,
    grad_out,
    self_qkv,
    self_out,
    cross_query,
    cross_kv,
    cross_out,
    ffn_up,
    ffn_down,
    ln_gain,
    ln_bias,
):
    row_count = target.shape[0]
    pair_count = mem_len.shape[0]
    seq_len = row_count * lax.axis_size("tensor") // pair_count
    full_lens = jnp.full((pair_count,), seq_len, jnp.int32)
    target_all = gather_rows(target)
    qkv_rows = jnp.einsum(
        "td,ide->ite", target_all, self_qkv, preferred_element_type=jnp.float32
    ).astype(jnp.bfloat16)
    context_one, total_one = attend_forward(qkv_rows[0], qkv_rows[1], qkv_rows[2], full_lens, True)
    branch_one = project_context(context_one, self_out, row_count)
    normed_one, norm_back_one = jax.vjp(
        norm_rows, alpha_res * target.astype(jnp.float32) + branch_one, ln_gain[0], ln_bias[0]
    )
    normed_one_all = gather_rows(normed_one.astype(jnp.bfloat16))
    memory_all = gather_rows(memory)
    query_two = jnp.dot(normed_one_all, cross_query, preferred_element_type=jnp.float32).astype(
        jnp.bfloat16
    )
    kv_two = jnp.einsum(
        "td,ide->ite", memory_all, cross_kv, preferred_element_type=jnp.float32
    ).astype(jnp.bfloat16)
    context_two, total_two = attend_forward(query_two, kv_two[0], kv_two[1], mem_len, False)
    branch_two = project_context(context_two, cross_out, row_count)
    normed_two, norm_back_two = jax.vjp(
        norm_rows, alpha_res * normed_one + branch_two, ln_gain[1], ln_bias[1]
    )
    normed_two_low = normed_two.astype(jnp.bfloat16)
    normed_two_all = gather_rows(normed_two_low)
    hidden = jnp.dot(normed_two_all, ffn_up, preferred_element_type=jnp.float32)
    activated, gelu_back = jax.vjp(exact_gelu, hidden)
    activated_low = activated.astype(jnp.bfloat16)
    branch_three = scatter_branch(activated_low, ffn_down, row_count)
    result, norm_back_three = jax.vjp(
        norm_rows, alpha_res * normed_two + branch_three, ln_gain[2], ln_bias[2]
    )
    grad_sum_three, gain_three, bias_three = norm_back_three(grad_out.astype(jnp.float32))
    branch_grad_three = gather_grads(grad_sum_three.astype(jnp.bfloat16))
    down_grad = lax.dot_general(
        activated_low, branch_grad_three, contract_rows, preferred_element_type=jnp.float32
    )
    act_grad = lax.dot_general(
        branch_grad_three, ffn_down, contract_cols, preferred_element_type=jnp.float32
    )
    hidden_grad = gelu_back(act_grad)[0].astype(jnp.bfloat16)
    up_grad = lax.dot_general(
        normed_two_all, hidden_grad, contract_rows, preferred_element_type=jnp.float32
    )
    normed_two_grad = alpha_res * grad_sum_three + scatter_inputs(
        ((hidden_grad, ffn_up),), row_count
    )
    grad_sum_two, gain_two, bias_two = norm_back_two(normed_two_grad)
    branch_grad_two = gather_grads(grad_sum_two.astype(jnp.bfloat16))
    cross_out_grad = lax.dot_general(
        context_two, branch_grad_two, contract_rows, preferred_element_type=jnp.float32
    )
    context_grad_two = lax.dot_general(
        branch_grad_two, cross_out, contract_cols, preferred_element_type=jnp.float32
    ).astype(jnp.bfloat16)
    query_grad_two, key_grad_two, value_grad_two = attend_backward(
        query_two, kv_two[0], kv_two[1], mem_len, False, total_two, context_grad_two
    )
    cross_query_grad = lax.dot_general(
        normed_one_all, query_grad_two, contract_rows, preferred_element_type=jnp.float32
    )
    cross_kv_grad = jnp.einsum(
        "td,ite->ide",
        memory_all,
        jnp.stack([key_grad_two, value_grad_two]),
        preferred_element_type=jnp.float32,
    )
    memory_grad = scatter_inputs(
        ((key_grad_two, cross_kv[0]), (value_grad_two, cross_kv[1])), row_count
    )
    normed_one_grad = alpha_res * grad_sum_two + scatter_inputs(
        ((query_grad_two, cross_query),), row_count
    )
    grad_sum_one, gain_one, bias_one = norm_back_one(normed_one_grad)
    branch_grad_one = gather_grads(grad_sum_one.astype(jnp.bfloat16))
    self_out_grad = lax.dot_general(
        context_one, branch_grad_one, contract_rows, preferred_element_type=jnp.float32
    )
    context_grad_one = lax.dot_general(
        branch_grad_one, self_out, contract_cols, preferred_element_type=jnp.float32
    ).astype(jnp.bfloat16)
    query_grad_one, key_grad_one, value_grad_one = attend_backward(
        qkv_rows[0], qkv_rows[1], qkv_rows[2], full_lens, True, total_one, context_grad_one
    )
    self_qkv_grad = jnp.einsum(
        "td,ite->ide",
        target_all,
        jnp.stack([query_grad_one, key_grad_one, value_grad_one]),
        preferred_element_type=jnp.float32,
    )
    target_grad = alpha_res * grad_sum_one + scatter_inputs(
        ((query_grad_one, self_qkv[0]), (key_grad_one, self_qkv[1]), (value_grad_one, self_qkv[2])),
        row_count,
    )
    (
        self_qkv_total,
        self_out_total,
        cross_query_total,
        cross_kv_total,
        cross_out_total,
        up_total,
        down_total,
    ) = (
        lax.psum(self_qkv_grad.astype(jnp.bfloat16), "dp").astype(jnp.float32),
        lax.psum(self_out_grad.astype(jnp.bfloat16), "dp").astype(jnp.float32),
        lax.psum(cross_query_grad.astype(jnp.bfloat16), "dp").astype(jnp.float32),
        lax.psum(cross_kv_grad.astype(jnp.bfloat16), "dp").astype(jnp.float32),
        lax.psum(cross_out_grad.astype(jnp.bfloat16), "dp").astype(jnp.float32),
        lax.psum(up_grad.astype(jnp.bfloat16), "dp").astype(jnp.float32),
        lax.psum(down_grad.astype(jnp.bfloat16), "dp").astype(jnp.float32),
    )
    gain_total, bias_total = lax.psum(
        (jnp.stack([gain_one, gain_two, gain_three]), jnp.stack([bias_one, bias_two, bias_three])),
        ("dp", "tensor"),
    )
    return (
        result.astype(jnp.bfloat16),
        target_grad.astype(jnp.bfloat16),
        memory_grad.astype(jnp.bfloat16),
        self_qkv_total,
        self_out_total,
        cross_query_total,
        cross_kv_total,
        cross_out_total,
        up_total,
        down_total,
        gain_total,
        bias_total,
    )


BLK = 256
f32 = jnp.float32
bf16 = jnp.bfloat16
NN = (((1,), (0,)), ((), ()))
NT = (((1,), (1,)), ((), ()))
TN = (((0,), (0,)), ((), ()))


def dot(a, b, dims=NN):
    return lax.dot_general(a, b, dims, preferred_element_type=f32)


def lanes(rows):
    return lax.broadcasted_iota(jnp.int32, (rows, 128), 1)


def place3(x, rows):
    hi = x.astype(bf16)
    rest = x - hi.astype(f32)
    mid = rest.astype(bf16)
    lo = (rest - mid.astype(f32)).astype(bf16)
    at = lanes(rows) % 64
    return jnp.where(at == 0, hi, jnp.where(at == 1, mid, jnp.where(at == 2, lo, jnp.zeros_like(hi))))


def fwd_kernel(causal, len_ref, q_ref, k_ref, v_ref, c_ref, lse_ref, kaug, vaug):
    k2, v2 = k_ref[...], v_ref[...]
    seq = k2.shape[0]
    lane = lanes(seq)
    zero = jnp.zeros_like(k2)
    if not causal:
        pos = lax.broadcasted_iota(jnp.int32, (seq, 128), 0)
        bias = jnp.where((pos >= len_ref[0]) & (lane == 0), -1e30, 0.0).astype(bf16)
    for h in range(2):
        own = (lane // 64) == h
        kaug[h, :, :128] = jnp.where(own, k2, zero)
        if not causal:
            kaug[h, :, 128:] = bias
        vaug[h, :, :128] = jnp.where(own, v2, zero)
        vaug[h, :, 128:] = jnp.where(own, jnp.ones_like(v2), zero)
    lb = lanes(BLK)
    for i in range(seq // BLK):
        rows = slice(i * BLK, (i + 1) * BLK)
        q = q_ref[rows, :] * jnp.asarray(HD**-0.5, bf16)
        if not causal:
            q = jnp.concatenate([q, jnp.where(lb == 0, 1.0, 0.0).astype(bf16)], axis=1)
        nk = (i + 1) * BLK if causal else seq
        acc = None
        ms = []
        for h in range(2):
            s = dot(q, kaug[h, :nk, :128] if causal else kaug[h], NT)
            if causal:
                a = lax.broadcasted_iota(jnp.int32, (BLK, BLK), 0)
                b = lax.broadcasted_iota(jnp.int32, (BLK, BLK), 1)
                d = jnp.where(b <= a, s[:, nk - BLK :], mask_fill)
                s = d if nk == BLK else jnp.concatenate([s[:, : nk - BLK], d], axis=1)
            m = jnp.max(s, axis=1, keepdims=True)
            p = jnp.exp(s - m).astype(bf16)
            o = dot(p, vaug[h, :nk])
            acc = o if acc is None else acc + o
            ms.append(m)
        total = acc[:, 128:]
        c_ref[rows, :] = (acc[:, :128] / total).astype(bf16)
        lse_ref[rows, :] = place3(-(jnp.where(lb < 64, ms[0], ms[1]) + jnp.log(total)), BLK)


def cost(matmuls, blocks, seq, causal):
    area = seq * seq * blocks * 2 * (0.625 if causal else 1)
    return pl.CostEstimate(
        flops=int(matmuls * area * 2 * 256), bytes_accessed=16 * seq * 128 * blocks, transcendentals=int(area)
    )


def attend_fwd(q, k, v, length, causal):
    seq, width = q.shape
    spec = pl.BlockSpec((seq, 128), lambda i: (0, i))
    return pl.pallas_call(
        functools.partial(fwd_kernel, causal),
        grid=(width // 128,),
        in_specs=[pl.BlockSpec(memory_space=pltpu.SMEM)] + [spec] * 3,
        out_specs=[spec] * 2,
        out_shape=[jax.ShapeDtypeStruct((seq, width), bf16)] * 2,
        scratch_shapes=[pltpu.VMEM((2, seq, 256), bf16)] * 2,
        compiler_params=pltpu.CompilerParams(vmem_limit_bytes=48 * 2**20),
        cost_estimate=cost(2, width // 128, seq, causal),
        name="attend_causal" if causal else "attend_memory",
    )(length, q, k, v)


def back_scratch(seq):
    vmem = pltpu.VMEM
    return [
        vmem((seq, 256), bf16),
        vmem((2, seq, 128), bf16),
        vmem((2, seq, 256), bf16),
        vmem((seq, 256), bf16),
        vmem((2, seq, 128), bf16),
        vmem((2, seq, 256), bf16),
        vmem((128, seq), f32),
        vmem((2, 128, seq), bf16),
    ]


def back_pair(causal, length, q2, k2, v2, c2, aug, g2, grads, scratch, tick):
    qs, qm, ka, gs, gm, va, dqa, kt = scratch
    seq = k2.shape[0]
    lane = lanes(seq)
    l64 = lane % 64
    zero = jnp.zeros_like(k2)
    one = jnp.ones_like(k2)
    scale = jnp.asarray(HD**-0.5, bf16)
    prod = c2.astype(f32) * g2.astype(f32)
    d0 = jnp.sum(jnp.where(lane < 64, prod, 0.0), axis=1, keepdims=True)
    d1 = jnp.sum(jnp.where(lane < 64, 0.0, prod), axis=1, keepdims=True)
    qs[:, :128] = q2 * scale
    if not causal:
        aug = jnp.where(l64 == 3, one, aug)
        pos = lax.broadcasted_iota(jnp.int32, (seq, 128), 0)
        bias = jnp.where(pos >= length, -1e30, 0.0).astype(bf16)
    qs[:, 128:] = aug
    gs[:, :128] = g2
    gs[:, 128:] = place3(-jnp.where(lane < 64, d0, d1), seq)
    for h in range(2):
        own = (lane // 64) == h
        sel = own & (l64 < 3)
        qm[h] = jnp.where(own, q2 * scale, zero)
        gm[h] = jnp.where(own, g2, zero)
        ka[h, :, :128] = jnp.where(own, k2, zero)
        ko = jnp.where(sel, one, zero)
        if not causal:
            ko = jnp.where(own & (l64 == 3), bias, ko)
        ka[h, :, 128:] = ko
        va[h, :, :128] = jnp.where(own, v2, zero)
        va[h, :, 128:] = jnp.where(sel, one, zero)
        kt[h] = ka[h, :, :128].T
    dqa[...] = jnp.zeros_like(dqa)
    grads[:, 384:] = c2
    for j in range(seq // BLK):
        rows = slice(j * BLK, (j + 1) * BLK)
        q0 = j * BLK if causal else 0
        dk = None
        dv = None
        dq = None
        for h in range(2):
            p = jnp.exp(dot(ka[h, rows, :], qs[q0:, :], NT))
            if causal:
                a = lax.broadcasted_iota(jnp.int32, (BLK, BLK), 0)
                b = lax.broadcasted_iota(jnp.int32, (BLK, BLK), 1)
                d = jnp.where(a <= b, p[:, :BLK], 0.0)
                p = d if q0 + BLK == seq else jnp.concatenate([d, p[:, BLK:]], axis=1)
            dp = dot(va[h, rows, :], gs[q0:, :], NT)
            ds = (p * dp).astype(bf16)
            p = p.astype(bf16)
            a = dot(p, gm[h, q0:, :])
            b = dot(ds, qm[h, q0:, :])
            c = dot(kt[h, :, rows], ds)
            dv = a if dv is None else dv + a
            dk = b if dk is None else dk + b
            dq = c if dq is None else dq + c
        dqa[:, q0:] += dq
        grads[rows, 128:256] = dk.astype(bf16)
        grads[rows, 256:384] = dv.astype(bf16)
        tick(j)
    grads[:, :128] = (dqa[...] * HD**-0.5).T.astype(bf16)


BOTH = (0, 1)
X, CORE, Y, Z1, Z2 = range(5)
DELAY = 2
SLOTS = 2 * DELAY
CHUNK = 64
SUBS = 4
QUADS = 4
WIDTH = 512
LEAD = 5
LINKS = (CORE, X, Y, Z1, Z2, Y, CORE, CORE)
CHUNKS = 4 * QUADS * SUBS
TICKS = CHUNKS + LEAD + 7 * DELAY
STEPS = 2 * QUADS
FEED_TICKS, CROSS_TICKS, SELF_TICKS, NORM_TICKS = 2, 3, 2, 4
CROSS_AT = STEPS * FEED_TICKS + NORM_TICKS
SELF_AT = CROSS_AT + STEPS * CROSS_TICKS + NORM_TICKS
DRAIN_AT = SELF_AT + STEPS * SELF_TICKS
TILE = 256
dma_sem = pltpu.SemaphoreType.DMA


def partner(bit):
    d = lax.axis_index("dp")
    t = lax.axis_index("tensor")
    if bit == 0:
        return (d, 1 - t)
    size = 2 ** (bit - 1)
    return (d + size * (1 - 2 * ((d // size) % 2)), t)


def greet():
    barrier = pltpu.get_barrier_semaphore()
    for bit in range(5):
        pl.semaphore_signal(barrier, inc=1, device_id=partner(bit), device_id_type=pl.DeviceIdType.MESH)
    pl.semaphore_wait(barrier, 5)


def remote_copy(src, dst, send, recv, bit):
    return pltpu.make_async_remote_copy(
        src_ref=src,
        dst_ref=dst,
        send_sem=send,
        recv_sem=recv,
        device_id=partner(bit),
        device_id_type=pl.DeviceIdType.MESH,
    )


def stream_scratch():
    return [
        pltpu.VMEM((2, SLOTS, 2, 2, CHUNK, WIDTH), bf16),
        pltpu.VMEM((3, SLOTS, 2, CHUNK, WIDTH), bf16),
        pltpu.VMEM((6, SLOTS, CHUNK, WIDTH), bf16),
        dma_sem((8, SLOTS)),
        dma_sem((8, SLOTS)),
        dma_sem((2, SLOTS)),
    ]


def stream_stage(stage, c, queue, out, pairs, wide, narrow, send, recv, local):
    d = lax.axis_index("dp")
    core = d % 2
    y = (d // 2) % 2
    slot = lax.rem(c, SLOTS)
    block = c // SUBS
    sub = lax.rem(c, SUBS)
    away, came, own = [wide.at[i, slot] for i in range(3)]
    got_y, s3, got_z, s4, got_zz, s5 = [narrow.at[i, slot] for i in range(6)]

    def remote(k):
        src, dst = (
            (queue.at[block, :, 1 - core, :, sub], pairs.at[0, slot]),
            (away, came),
            (own.at[1 - y], got_y),
            (s3, got_z),
            (s4, got_zz),
            (s5, out.at[block, core, y, sub]),
            (s5, out.at[block, core, y, sub]),
            (out.at[block, core, 1 - y, sub], out.at[block, core, 1 - y, sub]),
        )[k]
        return remote_copy(src, dst, send.at[k, slot], recv.at[k, slot], LINKS[k])

    def load():
        return pltpu.make_async_copy(queue.at[block, :, core, :, sub], pairs.at[1, slot], local.at[0, slot])

    def keep():
        return pltpu.make_async_copy(s5, out.at[block, core, y, sub], local.at[1, slot])

    if stage == 0:
        remote(0).start()
        load().start()
    elif stage == 1:
        remote(0).wait()
        load().wait()
        away[...] = pairs[1, slot, 1] + pairs[0, slot, 1]
        remote(1).start()
        own[...] = pairs[1, slot, 0] + pairs[0, slot, 0]
    elif stage == 2:
        remote(1).wait()
        own[...] = own[...] + came[...]
        remote(2).start()
    elif stage == 3:
        remote(2).wait()
        s3[...] = wide[2, slot, y] + got_y[...]
        remote(3).start()
    elif stage == 4:
        remote(3).wait()
        s4[...] = s3[...] + got_z[...]
        remote(4).start()
    elif stage == 5:
        remote(4).wait()
        s5[...] = s4[...] + got_zz[...]
        remote(5).start()
        remote(6).start()
        keep().start()
    elif stage == 6:
        remote(5).wait()
        remote(6).wait()
        keep().wait()
        remote(7).start()
    else:
        remote(7).wait()


def small_scratch(shape):
    return [pltpu.VMEM((6,) + shape, f32), pltpu.VMEM((5,) + shape, f32), dma_sem((5,)), dma_sem((5,))]


def small_stage(k, out, acc, got, send, recv):
    def remote(i):
        return remote_copy(acc.at[i], got.at[i], send.at[i], recv.at[i], i)

    if k > 0:
        remote(k - 1).wait()
        acc[k] = acc[k - 1] + got[k - 1]
    if k < 5:
        remote(k).start()
    else:
        out[...] = acc[5]


def norm_step(index, more, weights, gain_ref, sum_ref, total, dc, left, acc, zt, sems, tick):
    def fetch_tile(a):
        slot = lax.rem(a, 2)
        rows = pl.ds(pl.multiple_of(a * TILE, TILE), TILE)
        return pltpu.make_async_copy(sum_ref.at[rows], zt.at[slot], sems.at[slot])

    tiles = total.shape[0] // TILE
    fetch_tile(0).start()

    @pl.loop(0, tiles)
    def _(a):
        rows = pl.ds(pl.multiple_of(a * TILE, TILE), TILE)
        fetch_tile(a).wait()

        @pl.when(a + 1 < tiles)
        def _():
            fetch_tile(a + 1).start()

        z = zt[lax.rem(a, 2)]
        dh = total[rows, :]
        for x, w in more:
            dh = dh + dot(x[rows, :], w[...], NT)
        centered = z - jnp.mean(z, axis=1, keepdims=True)
        r = lax.rsqrt(jnp.mean(centered * centered, axis=1, keepdims=True) + norm_eps)
        n = centered * r
        acc[0, index : index + 1, :] = acc[0, index : index + 1, :] + jnp.sum(dh * n, axis=0, keepdims=True)
        acc[0, 3 + index : 4 + index, :] = acc[0, 3 + index : 4 + index, :] + jnp.sum(dh, axis=0, keepdims=True)
        e = dh * gain_ref[index : index + 1, :]
        dz = r * (e - jnp.mean(e, axis=1, keepdims=True) - n * jnp.mean(e * n, axis=1, keepdims=True))
        total[rows, :] = alpha_res * dz
        g = dz.astype(bf16)
        left[:, rows] = g.T
        for i in BOTH:
            dc[i, rows, :] = dot(g, weights[i][...], NT).astype(bf16)
        tick(a)


def back_kernel(*refs):
    refs = list(refs)
    take = lambda n: [refs.pop(0) for _ in range(n)]
    (len_ref,) = take(1)
    cross_in = [take(5) for _ in BOTH]
    self_in = [take(5) for _ in BOTH]
    co, cq, so = take(2), take(2), take(2)
    gain_ref, small_ref = take(2)
    feed_in = [take(4) for _ in BOTH]
    g3_ref, g3t_ref, h2t_ref, h1t_ref, memt_ref, tart_ref, base_ref, sum2_ref, sum1_ref = take(9)
    dk2_ref, dv2_ref, dq1_ref, dk1_ref, dv1_ref, dz_ref, out, queue, small_out = take(9)
    grads, *scratch = take(9)
    stream = [queue, out] + take(6)
    small_refs = [small_out] + take(4)
    acc = small_refs[1]
    lefts, tall, flat, total, dq2, dc, zt, staged = take(8)
    left_sems, feed_sems, zt_sems, staged_sems, base_sem = take(5)
    step = pl.program_id(0)
    half = lax.rem(step, 2)
    pair = lax.rem(step // 2, QUADS)

    def tick(t):
        for stage in range(7, -1, -1):
            c = t - LEAD - DELAY * stage
            pl.when((c >= 0) & (c < CHUNKS))(functools.partial(stream_stage, stage, c, *stream))

    def load_left(i, ref):
        return pltpu.make_async_copy(ref, lefts.at[i], left_sems.at[i])

    def load_feed(i, j):
        cols_j = pl.ds(pl.multiple_of(j * WIDTH, WIDTH), WIDTH)
        act, slope, up, down = feed_in[i]
        return [
            pltpu.make_async_copy(act.at[:, cols_j], tall.at[0, i], feed_sems.at[0, i]),
            pltpu.make_async_copy(slope.at[:, cols_j], tall.at[1, i], feed_sems.at[1, i]),
            pltpu.make_async_copy(up.at[:, cols_j], tall.at[2, i], feed_sems.at[2, i]),
            pltpu.make_async_copy(down.at[cols_j], flat.at[i], feed_sems.at[3, i]),
        ]

    def post(slot, block):
        return pltpu.make_async_copy(staged.at[slot], queue.at[block, half], staged_sems.at[slot])

    def products(slot, block, spans, ticks):
        for a in range(2):
            rows = slice(2 * a * TILE, 2 * (a + 1) * TILE)
            for left, right, lo, hi in spans:
                result = dot(lefts[left, rows, :], right[:, lo:hi]).astype(bf16)
                staged[slot, a, :, :, :, lo:hi] = result.reshape(2, SUBS, CHUNK, hi - lo)
            if a in ticks:
                tick(ticks[a])
        post(slot, block).start()

    @pl.when(step == 0)
    def _():
        for copy in load_feed(0, 0) + [load_left(i, r) for i, r in enumerate((g3t_ref, h2t_ref, g3_ref))]:
            copy.start()
        base = pltpu.make_async_copy(base_ref, total, base_sem)
        base.start()
        acc[0] = small_ref[...]
        greet()
        for copy in [load_left(i, r) for i, r in enumerate((g3t_ref, h2t_ref, g3_ref))]:
            copy.wait()
        base.wait()

    @pl.when(step < STEPS)
    def _():
        t = step * FEED_TICKS
        for i in BOTH:

            @pl.when(half == i)
            def _(i=i):
                for copy in load_feed(i, pair):
                    copy.wait()

                @pl.when(step < STEPS - 1)
                def _():
                    for copy in load_feed(1 - i, pair + i):
                        copy.start()

        for a in range(2):
            rows = slice(2 * a * TILE, 2 * (a + 1) * TILE)
            du = dot(lefts[2, rows, :], flat[half], NT) * tall[1, half, rows, :].astype(f32)
            grads[rows, :] = du.astype(bf16)
        @pl.when(step > 0)
        def _():
            post(0, 0).wait()

        products(0, 2 * pair, ((0, tall.at[0, half], 0, WIDTH),), {1: t})
        for a in range(2):
            rows = slice(2 * a * TILE, 2 * (a + 1) * TILE)
            total[rows, :] += dot(grads[rows, :], tall[2, half], NT)

        @pl.when(step > 0)
        def _():
            post(1, 0).wait()

        products(1, 2 * pair + 1, ((1, grads, 0, WIDTH),), {1: t + 1})

    @pl.when(step == STEPS)
    def _():
        fetch = [load_left(0, h1t_ref), load_left(1, memt_ref)]
        for copy in fetch:
            copy.start()
        norm_step(
            1, [], co, gain_ref, sum2_ref, total, dc, lefts.at[2], acc, zt, zt_sems, lambda k: tick(STEPS * FEED_TICKS + k)
        )
        for copy in fetch:
            copy.wait()
        post(1, 0).wait()

    at = pl.ds(pl.multiple_of(pair * 128, 128), 128)

    @pl.when((step >= STEPS) & (step < 2 * STEPS))
    def _():
        t = CROSS_AT + (step - STEPS) * CROSS_TICKS
        q2, k2, v2, c2, aug = [jnp.where(half == 0, a[...], b[...]) for a, b in zip(*cross_in)]

        def ticks(j):
            if j % 2 == 1:
                tick(t + j // 2)

        back_pair(False, len_ref[0], q2, k2, v2, c2, aug, dc[half, :, at], grads, scratch, ticks)
        dq2[half, :, at] = grads[:, :128]
        dk2_ref[...] = grads[:, 128:256]
        dv2_ref[...] = grads[:, 256:384]
        post(0, 0).wait()
        spans = ((0, grads, 0, 128), (1, grads, 128, 384), (2, grads, 384, 512))
        products(0, 2 * QUADS + pair, spans, {1: t + 2})

    @pl.when(step == 2 * STEPS)
    def _():
        fetch = load_left(0, tart_ref)
        fetch.start()
        more = [(dq2.at[i], cq[i]) for i in BOTH]
        norm_step(
            0, more, so, gain_ref, sum1_ref, total, dc, lefts.at[2], acc, zt, zt_sems, lambda k: tick(SELF_AT - NORM_TICKS + k)
        )
        fetch.wait()
        pltpu.make_async_copy(total, dz_ref, base_sem).start()

    @pl.when(step >= 2 * STEPS)
    def _():
        t = SELF_AT + (step - 2 * STEPS) * SELF_TICKS
        q2, k2, v2, c2, aug = [jnp.where(half == 0, a[...], b[...]) for a, b in zip(*self_in)]
        def ticks(j):
            if j == 0:
                tick(t)

        back_pair(True, 0, q2, k2, v2, c2, aug, dc[half, :, at], grads, scratch, ticks)
        dq1_ref[...] = grads[:, :128]
        dk1_ref[...] = grads[:, 128:256]
        dv1_ref[...] = grads[:, 256:384]
        post(0, 0).wait()
        products(0, 3 * QUADS + pair, ((0, grads, 0, 384), (2, grads, 384, 512)), {0: t + 1})
        for k in range(5, -1, -1):
            pl.when(step == 2 * STEPS + 1 + k)(functools.partial(small_stage, k, *small_refs))

    @pl.when(step == 3 * STEPS - 1)
    def _():
        post(0, 0).wait()
        pltpu.make_async_copy(total, dz_ref, base_sem).wait()
        pl.loop(DRAIN_AT, TICKS)(tick)


def layer_back(length, cross_in, self_in, weights, gain, small, feed_in, rest):
    seq, width = cross_in[0][0].shape
    model = gain.shape[1]
    early = lambda s: jnp.clip(s - STEPS, 0, STEPS - 1)
    late = lambda s: jnp.clip(s - 2 * STEPS, 0, STEPS - 1)
    cross_spec = pl.BlockSpec((seq, 128), lambda s: (0, early(s) // 2))
    self_spec = pl.BlockSpec((seq, 128), lambda s: (0, late(s) // 2))
    cross_out = pl.BlockSpec((None, seq, 128), lambda s: (early(s) % 2, 0, early(s) // 2))
    self_out = pl.BlockSpec((None, seq, 128), lambda s: (late(s) % 2, 0, late(s) // 2))
    anywhere = pl.BlockSpec(memory_space=pl.ANY)
    full = lambda x: pl.BlockSpec(x.shape, lambda s: (0, 0), pipeline_mode=pl.Buffered(1))
    shape = jax.ShapeDtypeStruct
    vmem = pltpu.VMEM
    blocks = 4 * QUADS
    return pl.pallas_call(
        back_kernel,
        grid=(3 * STEPS,),
        in_specs=[pl.BlockSpec(memory_space=pltpu.SMEM)]
        + [cross_spec] * 10
        + [self_spec] * 10
        + [full(x) for x in (*weights, gain, small)]
        + [anywhere] * 17,
        out_specs=[cross_out] * 2 + [self_out] * 3 + [anywhere] * 3 + [full(small)],
        out_shape=[shape((2, seq, width), bf16)] * 5
        + [
            shape((seq, model), f32),
            shape((blocks, 2, 2, SUBS, CHUNK, WIDTH), bf16),
            shape((blocks, 2, 2, 2, SUBS, CHUNK, WIDTH), bf16),
            shape(small.shape, f32),
        ],
        scratch_shapes=[vmem((seq, WIDTH), bf16)]
        + back_scratch(seq)
        + stream_scratch()
        + small_scratch(small.shape)
        + [
            vmem((3, model, seq), bf16),
            vmem((3, 2, seq, WIDTH), bf16),
            vmem((2, WIDTH, model), bf16),
            vmem((seq, model), f32),
            vmem((2, seq, width), bf16),
            vmem((2, seq, width), bf16),
            vmem((2, TILE, model), f32),
            vmem((2, 2, 2, SUBS, CHUNK, WIDTH), bf16),
            dma_sem((3,)),
            dma_sem((4, 2)),
            dma_sem((2,)),
            dma_sem((2,)),
            dma_sem,
        ],
        compiler_params=pltpu.CompilerParams(
            collective_id=1, has_side_effects=True, vmem_limit_bytes=60 * 2**20
        ),
        cost_estimate=cost(16, 8, seq, False),
        name="layer_back",
    )(length, *cross_in[0], *cross_in[1], *self_in[0], *self_in[1], *weights, gain, small, *feed_in[0], *feed_in[1], *rest)


ALL = ("dp", "tensor")
DEVICES = 32


def swap(x, flip):
    return lax.ppermute(x, ALL, [(i, i ^ flip) for i in range(DEVICES)])


def swap_tensor(x):
    return swap(x, 1)


def swap_core(x):
    return swap(x, 2)


def swap_y(x):
    return swap(x, 4)


def my_block():
    d = lax.axis_index("dp")
    return 2 * (d % 2) + (d // 2) % 2


def add_low(*terms):
    return sum(t.astype(f32) for t in terms).astype(bf16)


def blocks_of(own, axis):
    size = own.shape[axis] // 4
    return [lax.dynamic_slice_in_dim(own, (my_block() ^ j) * size, size, axis) for j in range(4)]


def swap_pieces(x, move):
    return [move(p) for p in x] if isinstance(x, (list, tuple)) else move(x)


def tie(*xs):
    return lax.optimization_barrier(xs)


class Pipe:
    def __init__(self):
        self.live = []

    def put(self, gen):
        wait, arrays = next(gen)
        self.live.append([gen, wait, arrays])

    def step(self, due, landed):
        done = 0
        for item in due:
            arrays = landed[done : done + len(item[2])]
            done += len(item[2])
            try:
                item[1], item[2] = item[0].send(arrays)
            except StopIteration:
                self.live.remove(item)

    def cut(self, *xs):
        due = []
        for item in self.live:
            item[1] -= 1
            if item[1] <= 0:
                due.append(item)
        tied = tie(*xs, *[a for item in due for a in item[2]])
        self.step(due, tied[len(xs) :])
        return tied[: len(xs)] if len(xs) > 1 else tied[0]

    def drain(self):
        while self.live:
            self.step(list(self.live), [a for item in self.live for a in item[2]])


def fetch(out, key, block, waits):
    far = swap_tensor(block)
    (far,) = yield waits[0], [far]
    side = swap_y(far)
    near = swap_core(far)
    side, near = yield waits[1], [side, near]
    out[key] = [far, side, near, swap_core(side)]
    return


def ffn_kernel(h_ref, up_ref, down_ref, a_ref, d_ref, b_ref):
    h = h_ref[...]
    size = 512
    total = None
    for j in range(4):
        cols = slice(j * size, (j + 1) * size)
        u = dot(h, up_ref[:, cols])
        cdf = 0.5 + 0.5 * lax.erf(u * (0.5**0.5))
        slope = cdf + u * (jnp.exp(-0.5 * u * u) * 0.3989422804014327)
        act = (u * cdf).astype(bf16)
        a_ref[:, cols] = act
        d_ref[:, cols] = slope.astype(bf16)
        term = dot(act, down_ref[cols, :])
        total = term if total is None else total + term
    b_ref[...] = total


def whole(x):
    return pl.BlockSpec(x.shape, lambda r: (0, 0))


ROWS = 512


def ffn_forward(h, up, down):
    seq, width = h.shape
    units = up.shape[1]
    rows = lambda w: pl.BlockSpec((ROWS, w), lambda r: (r, 0))
    return pl.pallas_call(
        ffn_kernel,
        grid=(seq // ROWS,),
        in_specs=[rows(width)] + [whole(up), whole(down)],
        out_specs=[rows(units), rows(units), rows(width)],
        out_shape=[jax.ShapeDtypeStruct((seq, units), bf16)] * 2 + [jax.ShapeDtypeStruct((seq, width), f32)],
        compiler_params=pltpu.CompilerParams(vmem_limit_bytes=50 * 2**20),
        cost_estimate=pl.CostEstimate(flops=4 * seq * width * units, bytes_accessed=22 * 2**20, transcendentals=2 * seq * units),
        name="feed_forward",
    )(h, up, down)


def arrange_kernel(me_ref, *refs):
    for j in range(4):

        @pl.when(pl.program_id(0) == j)
        def _(j=j):
            refs[4][...] = refs[j][...]


def arrange(slabs):
    members, rows, width = slabs[0].shape
    return pl.pallas_call(
        arrange_kernel,
        grid_spec=pltpu.PrefetchScalarGridSpec(
            num_scalar_prefetch=1,
            grid=(4,),
            in_specs=[pl.BlockSpec((members, rows, width), lambda j, me: (0, 0, 0))] * 4,
            out_specs=pl.BlockSpec((members, rows, width), lambda j, me: (0, j ^ me[0], 0)),
        ),
        out_shape=jax.ShapeDtypeStruct((members, 4 * rows, width), bf16),
        compiler_params=pltpu.CompilerParams(vmem_limit_bytes=40 * 2**20),
        cost_estimate=pl.CostEstimate(flops=0, bytes_accessed=16 * members * rows * width, transcendentals=0),
        name="arrange",
    )(my_block().reshape(1), *slabs)


def slab_of(own):
    rows = own.shape[1] // 4
    return lax.dynamic_slice_in_dim(own, my_block() * rows, rows, 1)


def spread_kernel(spans, x_ref, *out_refs):
    for lo, hi, k, m in spans:
        x = x_ref[:, lo:hi].astype(f32)
        if m is None:
            out_refs[k][...] = x.T
        else:
            out_refs[k][m] = x


def spread(pairs, first, spans, outs):
    _, rows, width = pairs.shape
    tile = 512
    specs = []
    shapes = []
    for members in outs:
        if members is None:
            specs.append(pl.BlockSpec((128, tile), lambda p, t: (p, t)))
            shapes.append(jax.ShapeDtypeStruct((512, rows), f32))
        else:
            specs.append(pl.BlockSpec((members, tile, 128), lambda p, t: (0, t, p)))
            shapes.append(jax.ShapeDtypeStruct((members, rows, 512), f32))
    return pl.pallas_call(
        functools.partial(spread_kernel, spans),
        grid=(4, rows // tile),
        in_specs=[pl.BlockSpec((None, tile, width), lambda p, t: (p + first, t, 0))],
        out_specs=specs,
        out_shape=shapes,
        compiler_params=pltpu.CompilerParams(vmem_limit_bytes=40 * 2**20),
        cost_estimate=pl.CostEstimate(flops=0, bytes_accessed=24 * rows * width, transcendentals=0),
        name="spread",
    )(pairs)


def flip_kernel(x_ref, out_ref):
    out_ref[...] = x_ref[...].T


def flip(x):
    rows, width = x.shape
    return pl.pallas_call(
        flip_kernel,
        grid=(4,),
        in_specs=[pl.BlockSpec((rows // 4, width), lambda i: (i, 0))],
        out_specs=pl.BlockSpec((width, rows // 4), lambda i: (0, i)),
        out_shape=jax.ShapeDtypeStruct((width, rows), x.dtype),
        cost_estimate=pl.CostEstimate(flops=0, bytes_accessed=4 * rows * width, transcendentals=0),
        name="flip",
    )(x)


def spread_feed_kernel(x_ref, down_ref, up_ref):
    even = lax.rem(pl.program_id(0), 2) == 0

    @pl.when(even)
    def _():
        down_ref[...] = x_ref[...].astype(f32).T

    @pl.when(jnp.logical_not(even))
    def _():
        up_ref[...] = x_ref[...].astype(f32)


def spread_feed(blocks):
    _, rows, width = blocks.shape
    return pl.pallas_call(
        spread_feed_kernel,
        grid=(8,),
        in_specs=[pl.BlockSpec((None, rows, width), lambda b: (b, 0, 0))],
        out_specs=[
            pl.BlockSpec((width, rows), lambda b: (b // 2, 0)),
            pl.BlockSpec((rows, width), lambda b: (0, b // 2)),
        ],
        out_shape=[jax.ShapeDtypeStruct((4 * width, rows), f32), jax.ShapeDtypeStruct((rows, 4 * width), f32)],
        compiler_params=pltpu.CompilerParams(vmem_limit_bytes=40 * 2**20),
        cost_estimate=pl.CostEstimate(flops=0, bytes_accessed=48 * rows * width, transcendentals=0),
        name="spread_feed",
    )(blocks)


def one_pair_each(
    target,
    memory,
    mem_len,
    grad_out,
    self_qkv,
    self_out,
    cross_query,
    cross_kv,
    cross_out,
    ffn_up,
    ffn_down,
    ln_gain,
    ln_bias,
):
    length = lax.dynamic_slice_in_dim(mem_len, lax.axis_index("tensor"), 1)
    pipe = Pipe()
    got = {}
    so3, cq3, co3 = self_out[None], cross_query[None], cross_out[None]

    pipe.put(fetch(got, "qkv", slab_of(self_qkv), (1, 1)))
    q1 = [[dot(target, self_qkv[m]).astype(bf16) for m in range(3)], None]
    at1 = [attend_fwd(*q1[0], length, True), None]
    so_s, cq_s, kv_s, co_s = [slab_of(x) for x in (so3, cq3, cross_kv, co3)]
    mem, so_s, cq_s, kv_s, _ = pipe.cut(memory, so_s, cq_s, kv_s, at1[0][0])
    pipe.put(fetch(got, "so", so_s, (1, 1)))
    pipe.put(fetch(got, "cq", cq_s, (1, 1)))
    pipe.put(fetch(got, "kv", kv_s, (1, 1)))
    kv = [[dot(mem, cross_kv[m]).astype(bf16) for m in range(2)], None]
    up_s, down_s = slab_of(ffn_up[None]), slab_of(ffn_down[None])
    target_t = flip(target)
    memory_t = flip(mem)
    kv[0][0], up_s, co_s, target_t, memory_t = tie(kv[0][0], up_s, co_s, target_t, memory_t)
    tar = pipe.cut(target)
    qkv_oth = arrange(got["qkv"])
    q1[1] = [dot(tar, qkv_oth[m]).astype(bf16) for m in range(3)]
    pipe.put(fetch(got, "co", co_s, (1, 1)))
    q1[1][0], up_s = tie(q1[1][0], up_s)
    pipe.put(fetch(got, "up", up_s, (2, 1)))
    at1[1] = attend_fwd(*q1[1], length, True)
    at1[1], _ = tie(at1[1], at1[1][0])
    c1_oth = pipe.cut(at1[1][0])
    c1 = [at1[0][0], c1_oth]
    so_oth = arrange(got["so"])[0]
    b1 = dot(c1[0], self_out) + dot(c1[1], so_oth)
    sum1 = alpha_res * target.astype(f32) + b1
    h1 = norm_rows(sum1, ln_gain[0], ln_bias[0])
    h1_low = h1.astype(bf16)
    cq_oth = arrange(got["cq"])[0]
    kv_oth = arrange(got["kv"])
    q2 = [dot(h1_low, cross_query).astype(bf16), dot(h1_low, cq_oth).astype(bf16)]
    kv[1] = [dot(memory, kv_oth[m]).astype(bf16) for m in range(2)]
    q2[0], kv[1][0], down_s = pipe.cut(q2[0], kv[1][0], down_s)
    pipe.put(fetch(got, "down", down_s, (1, 1)))
    at2 = [attend_fwd(q2[0], *kv[0], length, False), None]
    q2[1], _ = pipe.cut(q2[1], at2[0][0])
    at2[1] = attend_fwd(q2[1], *kv[1], length, False)
    co_oth = arrange(got["co"])[0]
    c2 = [at2[0][0], at2[1][0]]
    c2[1] = pipe.cut(c2[1])
    b2 = dot(c2[0], cross_out) + dot(c2[1], co_oth)
    sum2 = alpha_res * h1 + b2
    h2 = norm_rows(sum2, ln_gain[1], ln_bias[1])
    h2_low = h2.astype(bf16)
    act0, slope0, b3 = ffn_forward(h2_low, ffn_up, ffn_down)
    h1_t, h2_t = flip(h1_low), flip(h2_low)
    while "up" not in got or "down" not in got:
        act0 = pipe.cut(act0)
    h2_again, h1_t, h2_t, _ = tie(h2_low, h1_t, h2_t, act0)
    up_oth, down_oth = arrange(got["up"])[0], arrange(got["down"])[0]
    act1, slope1, b3b = ffn_forward(h2_again, up_oth, down_oth)
    result, back3 = jax.vjp(norm_rows, alpha_res * h2 + b3 + b3b, ln_gain[2], ln_bias[2])
    dz3, gain3, bias3 = back3(grad_out.astype(f32))
    g3 = dz3.astype(bf16)
    none = jnp.zeros_like(gain3)
    small = jnp.stack([none, none, gain3, none, none, bias3, none, none])
    dk2, dv2, dq1, dk1, dv1, dz1, blocks, _, small = layer_back(
        length,
        [[q2[i], *kv[i], c2[i], at2[i][1]] for i in BOTH],
        [[*q1[i], c1[i], at1[i][1]] for i in BOTH],
        (cross_out, co_oth, cross_query, cq_oth, self_out, so_oth),
        ln_gain,
        small,
        [(act0, slope0, ffn_up, ffn_down), (act1, slope1, up_oth, down_oth)],
        (g3, flip(g3), h2_t, h1_t, memory_t, target_t, alpha_res * dz3, sum2, sum1),
    )
    blocks = blocks.reshape(16, 1024, 512)
    kv_both = (cross_kv, kv_oth)
    dmem = sum(dot(d[i], kv_both[i][m], NT) for i in BOTH for m, d in enumerate((dk2, dv2)))
    qkv_both = (self_qkv, qkv_oth)
    dtar = dz1 + sum(dot(d[i], qkv_both[i][m], NT) for i in BOTH for m, d in enumerate((dq1, dk1, dv1)))
    cq_total, kv_total, co_total = spread(
        blocks,
        8,
        ((0, 128, 0, 0), (128, 256, 1, 0), (256, 384, 1, 1), (384, 512, 2, None)),
        (1, 2, None),
    )
    qkv_total, so_total = spread(
        blocks,
        12,
        ((0, 128, 0, 0), (128, 256, 0, 1), (256, 384, 0, 2), (384, 512, 1, None)),
        (3, None),
    )
    down_total, up_total = spread_feed(blocks)
    return (
        result.astype(bf16),
        dtar.astype(bf16),
        dmem.astype(bf16),
        qkv_total,
        so_total,
        cq_total[0],
        kv_total,
        co_total,
        up_total,
        down_total,
        small[:3],
        small[3:6],
    )


def solution(mesh):
    placed = (
        P(("dp", "tensor"), None),
        P(("dp", "tensor"), None),
        P("dp"),
        P(("dp", "tensor"), None),
        P(None, None, "tensor"),
        P("tensor", None),
        P(None, "tensor"),
        P(None, None, "tensor"),
        P("tensor", None),
        P(None, "tensor"),
        P("tensor", None),
        P(),
        P(),
    )
    body = one_pair_each if mesh.shape["tensor"] == 2 and mesh.shape["dp"] == 16 else on_device
    return jax.shard_map(
        body,
        mesh=mesh,
        in_specs=placed,
        out_specs=(
            P(("dp", "tensor"), None),
            P(("dp", "tensor"), None),
            P(("dp", "tensor"), None),
            P(None, None, "tensor"),
            P("tensor", None),
            P(None, "tensor"),
            P(None, None, "tensor"),
            P("tensor", None),
            P(None, "tensor"),
            P("tensor", None),
            P(),
            P(),
        ),
        check_vma=False,
    )
```

```python
import functools

import jax
import jax.numpy as jnp
from jax import lax
from jax.experimental import pallas as pl
from jax.experimental.pallas import tpu as pltpu
from jax.sharding import PartitionSpec as P

HD = 64


alpha_res = 300.0**0.25
norm_eps = 1e-05
mask_fill = -1e30
contract_rows = (((0,), (0,)), ((), ()))
contract_cols = (((1,), (1,)), ((), ()))


def norm_rows(resid, gain_vec, bias_vec):
    average = jnp.mean(resid, axis=-1, keepdims=True)
    centered = resid - average
    variance = jnp.mean(centered * centered, axis=-1, keepdims=True)
    return centered * lax.rsqrt(variance + norm_eps) * gain_vec + bias_vec


def exact_gelu(values_in):
    return jax.nn.gelu(values_in, approximate=False)


def gather_rows(local_rows):
    return lax.all_gather(local_rows, "tensor", axis=0, tiled=True)


def gather_grads(local_rows):
    return lax.all_gather(local_rows, "tensor", axis=0, tiled=True)


def scatter_branch(left_mat, right_mat, row_count):

    def partial_term(offset, num_rows):
        return jnp.dot(left_mat, right_mat, preferred_element_type=jnp.float32)

    return lax.psum_scatter(
        partial_term(jnp.int32(0), row_count * lax.axis_size("tensor")),
        "tensor",
        scatter_dimension=0,
        tiled=True,
    )


def project_context(context, weight_local, row_count):
    return scatter_branch(context, weight_local, row_count)


def scatter_inputs(factor_pairs, row_count):

    def partial_term(offset, num_rows):
        terms = [
            lax.dot_general(grad_mat, weight_mat, contract_cols, preferred_element_type=jnp.float32)
            for grad_mat, weight_mat in factor_pairs
        ]
        return sum(terms)

    return lax.psum_scatter(
        partial_term(jnp.int32(0), row_count * lax.axis_size("tensor")).astype(jnp.bfloat16),
        "tensor",
        scatter_dimension=0,
        tiled=True,
    ).astype(jnp.float32)


def block_view(flat, pair_count, block_rows):
    tok_count, col_count = flat.shape
    seq_len = tok_count // pair_count
    return flat.reshape(pair_count, seq_len // block_rows, block_rows, col_count // HD, HD)


def pair_view(flat, pair_count):
    tok_count, col_count = flat.shape
    return flat.reshape(pair_count, tok_count // pair_count, col_count // HD, HD)


def block_scores(query_blk, key_pair, start_row, key_len, causal):
    block_rows = query_blk.shape[0]
    seq_len = key_pair.shape[0]
    products = jnp.einsum(
        "qhd,khd->hqk", query_blk, key_pair, preferred_element_type=jnp.float32
    ) * HD ** (-0.5)
    key_pos = lax.broadcasted_iota(jnp.int32, (block_rows, seq_len), 1)
    query_pos = start_row + lax.broadcasted_iota(jnp.int32, (block_rows, seq_len), 0)
    allowed = key_pos < key_len
    if causal:
        allowed = allowed & (key_pos <= query_pos)
    return jnp.where(allowed[None], products, mask_fill)


def attend_forward(queries, key_rows, value_rows, key_lens, causal):
    pair_count = key_lens.shape[0]
    seq_len = queries.shape[0] // pair_count
    block_rows = min(512, seq_len)
    starts = lax.iota(jnp.int32, seq_len // block_rows) * block_rows

    def one_pair(packed):
        query_pair, key_pair, value_pair, key_len = packed

        def one_block(inner):
            query_blk, start_row = inner
            scores = block_scores(query_blk, key_pair, start_row, key_len, causal)
            row_max = jnp.max(scores, axis=-1, keepdims=True)
            shifted = jnp.exp(scores - row_max)
            row_total = jnp.sum(shifted, axis=-1, keepdims=True)
            attn_prob = (shifted / row_total).astype(jnp.bfloat16)
            context = jnp.einsum(
                "hqk,khd->qhd", attn_prob, value_pair, preferred_element_type=jnp.float32
            )
            return (context.astype(jnp.bfloat16), (row_max + jnp.log(row_total))[..., 0])

        return lax.map(one_block, (query_pair, starts))

    context, log_total = lax.map(
        one_pair,
        (
            block_view(queries, pair_count, block_rows),
            pair_view(key_rows, pair_count),
            pair_view(value_rows, pair_count),
            key_lens,
        ),
    )
    return (context.reshape(queries.shape), log_total)


def attend_backward(queries, key_rows, value_rows, key_lens, causal, log_total, grad_context):
    pair_count = key_lens.shape[0]
    seq_len = queries.shape[0] // pair_count
    block_rows = min(512, seq_len)
    starts = lax.iota(jnp.int32, seq_len // block_rows) * block_rows
    score_scale = HD ** (-0.5)

    def one_pair(packed):
        query_pair, key_pair, value_pair, key_len, total_pair, grad_pair = packed

        def one_block(carry, inner):
            key_grad, value_grad = carry
            query_blk, start_row, total_blk, grad_blk = inner
            scores = block_scores(query_blk, key_pair, start_row, key_len, causal)
            attn_prob = jnp.exp(scores - total_blk[..., None])
            value_grad = value_grad + jnp.einsum(
                "hqk,qhd->khd",
                attn_prob.astype(jnp.bfloat16),
                grad_blk,
                preferred_element_type=jnp.float32,
            )
            prob_grad = jnp.einsum(
                "qhd,khd->hqk", grad_blk, value_pair, preferred_element_type=jnp.float32
            )
            score_grad = (
                attn_prob * (prob_grad - jnp.sum(attn_prob * prob_grad, axis=-1, keepdims=True))
            ).astype(jnp.bfloat16)
            query_grad = (
                jnp.einsum("hqk,khd->qhd", score_grad, key_pair, preferred_element_type=jnp.float32)
                * score_scale
            )
            key_grad = (
                key_grad
                + jnp.einsum(
                    "hqk,qhd->khd", score_grad, query_blk, preferred_element_type=jnp.float32
                )
                * score_scale
            )
            return ((key_grad, value_grad), query_grad.astype(jnp.bfloat16))

        zeros = jnp.zeros(key_pair.shape, jnp.float32)
        (key_grad, value_grad), query_grad = lax.scan(
            one_block, (zeros, zeros), (query_pair, starts, total_pair, grad_pair)
        )
        return (query_grad, key_grad.astype(jnp.bfloat16), value_grad.astype(jnp.bfloat16))

    query_grad, key_grad, value_grad = lax.map(
        one_pair,
        (
            block_view(queries, pair_count, block_rows),
            pair_view(key_rows, pair_count),
            pair_view(value_rows, pair_count),
            key_lens,
            log_total,
            block_view(grad_context, pair_count, block_rows),
        ),
    )
    return (
        query_grad.reshape(queries.shape),
        key_grad.reshape(queries.shape),
        value_grad.reshape(queries.shape),
    )


def on_device(
    target,
    memory,
    mem_len,
    grad_out,
    self_qkv,
    self_out,
    cross_query,
    cross_kv,
    cross_out,
    ffn_up,
    ffn_down,
    ln_gain,
    ln_bias,
):
    row_count = target.shape[0]
    pair_count = mem_len.shape[0]
    seq_len = row_count * lax.axis_size("tensor") // pair_count
    full_lens = jnp.full((pair_count,), seq_len, jnp.int32)
    target_all = gather_rows(target)
    qkv_rows = jnp.einsum(
        "td,ide->ite", target_all, self_qkv, preferred_element_type=jnp.float32
    ).astype(jnp.bfloat16)
    context_one, total_one = attend_forward(qkv_rows[0], qkv_rows[1], qkv_rows[2], full_lens, True)
    branch_one = project_context(context_one, self_out, row_count)
    normed_one, norm_back_one = jax.vjp(
        norm_rows, alpha_res * target.astype(jnp.float32) + branch_one, ln_gain[0], ln_bias[0]
    )
    normed_one_all = gather_rows(normed_one.astype(jnp.bfloat16))
    memory_all = gather_rows(memory)
    query_two = jnp.dot(normed_one_all, cross_query, preferred_element_type=jnp.float32).astype(
        jnp.bfloat16
    )
    kv_two = jnp.einsum(
        "td,ide->ite", memory_all, cross_kv, preferred_element_type=jnp.float32
    ).astype(jnp.bfloat16)
    context_two, total_two = attend_forward(query_two, kv_two[0], kv_two[1], mem_len, False)
    branch_two = project_context(context_two, cross_out, row_count)
    normed_two, norm_back_two = jax.vjp(
        norm_rows, alpha_res * normed_one + branch_two, ln_gain[1], ln_bias[1]
    )
    normed_two_low = normed_two.astype(jnp.bfloat16)
    normed_two_all = gather_rows(normed_two_low)
    hidden = jnp.dot(normed_two_all, ffn_up, preferred_element_type=jnp.float32)
    activated, gelu_back = jax.vjp(exact_gelu, hidden)
    activated_low = activated.astype(jnp.bfloat16)
    branch_three = scatter_branch(activated_low, ffn_down, row_count)
    result, norm_back_three = jax.vjp(
        norm_rows, alpha_res * normed_two + branch_three, ln_gain[2], ln_bias[2]
    )
    grad_sum_three, gain_three, bias_three = norm_back_three(grad_out.astype(jnp.float32))
    branch_grad_three = gather_grads(grad_sum_three.astype(jnp.bfloat16))
    down_grad = lax.dot_general(
        activated_low, branch_grad_three, contract_rows, preferred_element_type=jnp.float32
    )
    act_grad = lax.dot_general(
        branch_grad_three, ffn_down, contract_cols, preferred_element_type=jnp.float32
    )
    hidden_grad = gelu_back(act_grad)[0].astype(jnp.bfloat16)
    up_grad = lax.dot_general(
        normed_two_all, hidden_grad, contract_rows, preferred_element_type=jnp.float32
    )
    normed_two_grad = alpha_res * grad_sum_three + scatter_inputs(
        ((hidden_grad, ffn_up),), row_count
    )
    grad_sum_two, gain_two, bias_two = norm_back_two(normed_two_grad)
    branch_grad_two = gather_grads(grad_sum_two.astype(jnp.bfloat16))
    cross_out_grad = lax.dot_general(
        context_two, branch_grad_two, contract_rows, preferred_element_type=jnp.float32
    )
    context_grad_two = lax.dot_general(
        branch_grad_two, cross_out, contract_cols, preferred_element_type=jnp.float32
    ).astype(jnp.bfloat16)
    query_grad_two, key_grad_two, value_grad_two = attend_backward(
        query_two, kv_two[0], kv_two[1], mem_len, False, total_two, context_grad_two
    )
    cross_query_grad = lax.dot_general(
        normed_one_all, query_grad_two, contract_rows, preferred_element_type=jnp.float32
    )
    cross_kv_grad = jnp.einsum(
        "td,ite->ide",
        memory_all,
        jnp.stack([key_grad_two, value_grad_two]),
        preferred_element_type=jnp.float32,
    )
    memory_grad = scatter_inputs(
        ((key_grad_two, cross_kv[0]), (value_grad_two, cross_kv[1])), row_count
    )
    normed_one_grad = alpha_res * grad_sum_two + scatter_inputs(
        ((query_grad_two, cross_query),), row_count
    )
    grad_sum_one, gain_one, bias_one = norm_back_one(normed_one_grad)
    branch_grad_one = gather_grads(grad_sum_one.astype(jnp.bfloat16))
    self_out_grad = lax.dot_general(
        context_one, branch_grad_one, contract_rows, preferred_element_type=jnp.float32
    )
    context_grad_one = lax.dot_general(
        branch_grad_one, self_out, contract_cols, preferred_element_type=jnp.float32
    ).astype(jnp.bfloat16)
    query_grad_one, key_grad_one, value_grad_one = attend_backward(
        qkv_rows[0], qkv_rows[1], qkv_rows[2], full_lens, True, total_one, context_grad_one
    )
    self_qkv_grad = jnp.einsum(
        "td,ite->ide",
        target_all,
        jnp.stack([query_grad_one, key_grad_one, value_grad_one]),
        preferred_element_type=jnp.float32,
    )
    target_grad = alpha_res * grad_sum_one + scatter_inputs(
        ((query_grad_one, self_qkv[0]), (key_grad_one, self_qkv[1]), (value_grad_one, self_qkv[2])),
        row_count,
    )
    (
        self_qkv_total,
        self_out_total,
        cross_query_total,
        cross_kv_total,
        cross_out_total,
        up_total,
        down_total,
    ) = (
        lax.psum(self_qkv_grad.astype(jnp.bfloat16), "dp").astype(jnp.float32),
        lax.psum(self_out_grad.astype(jnp.bfloat16), "dp").astype(jnp.float32),
        lax.psum(cross_query_grad.astype(jnp.bfloat16), "dp").astype(jnp.float32),
        lax.psum(cross_kv_grad.astype(jnp.bfloat16), "dp").astype(jnp.float32),
        lax.psum(cross_out_grad.astype(jnp.bfloat16), "dp").astype(jnp.float32),
        lax.psum(up_grad.astype(jnp.bfloat16), "dp").astype(jnp.float32),
        lax.psum(down_grad.astype(jnp.bfloat16), "dp").astype(jnp.float32),
    )
    gain_total, bias_total = lax.psum(
        (jnp.stack([gain_one, gain_two, gain_three]), jnp.stack([bias_one, bias_two, bias_three])),
        ("dp", "tensor"),
    )
    return (
        result.astype(jnp.bfloat16),
        target_grad.astype(jnp.bfloat16),
        memory_grad.astype(jnp.bfloat16),
        self_qkv_total,
        self_out_total,
        cross_query_total,
        cross_kv_total,
        cross_out_total,
        up_total,
        down_total,
        gain_total,
        bias_total,
    )


BLK = 256
f32 = jnp.float32
bf16 = jnp.bfloat16
NN = (((1,), (0,)), ((), ()))
NT = (((1,), (1,)), ((), ()))
TN = (((0,), (0,)), ((), ()))


def dot(a, b, dims=NN):
    return lax.dot_general(a, b, dims, preferred_element_type=f32)


def lanes(rows):
    return lax.broadcasted_iota(jnp.int32, (rows, 128), 1)


def place3(x, rows):
    hi = x.astype(bf16)
    rest = x - hi.astype(f32)
    mid = rest.astype(bf16)
    lo = (rest - mid.astype(f32)).astype(bf16)
    at = lanes(rows) % 64
    return jnp.where(at == 0, hi, jnp.where(at == 1, mid, jnp.where(at == 2, lo, jnp.zeros_like(hi))))


def fwd_kernel(causal, len_ref, q_ref, k_ref, v_ref, c_ref, lse_ref, kaug, vaug):
    k2, v2 = k_ref[...], v_ref[...]
    seq = k2.shape[0]
    lane = lanes(seq)
    zero = jnp.zeros_like(k2)
    if not causal:
        pos = lax.broadcasted_iota(jnp.int32, (seq, 128), 0)
        bias = jnp.where((pos >= len_ref[0]) & (lane == 0), -1e30, 0.0).astype(bf16)
    for h in range(2):
        own = (lane // 64) == h
        kaug[h, :, :128] = jnp.where(own, k2, zero)
        if not causal:
            kaug[h, :, 128:] = bias
        vaug[h, :, :128] = jnp.where(own, v2, zero)
        vaug[h, :, 128:] = jnp.where(own, jnp.ones_like(v2), zero)
    lb = lanes(BLK)
    for i in range(seq // BLK):
        rows = slice(i * BLK, (i + 1) * BLK)
        q = q_ref[rows, :] * jnp.asarray(HD**-0.5, bf16)
        if not causal:
            q = jnp.concatenate([q, jnp.where(lb == 0, 1.0, 0.0).astype(bf16)], axis=1)
        nk = (i + 1) * BLK if causal else seq
        acc = None
        ms = []
        for h in range(2):
            s = dot(q, kaug[h, :nk, :128] if causal else kaug[h], NT)
            if causal:
                a = lax.broadcasted_iota(jnp.int32, (BLK, BLK), 0)
                b = lax.broadcasted_iota(jnp.int32, (BLK, BLK), 1)
                d = jnp.where(b <= a, s[:, nk - BLK :], mask_fill)
                s = d if nk == BLK else jnp.concatenate([s[:, : nk - BLK], d], axis=1)
            m = jnp.max(s, axis=1, keepdims=True)
            p = jnp.exp(s - m).astype(bf16)
            o = dot(p, vaug[h, :nk])
            acc = o if acc is None else acc + o
            ms.append(m)
        total = acc[:, 128:]
        c_ref[rows, :] = (acc[:, :128] / total).astype(bf16)
        lse_ref[rows, :] = place3(-(jnp.where(lb < 64, ms[0], ms[1]) + jnp.log(total)), BLK)


def cost(matmuls, blocks, seq, causal):
    area = seq * seq * blocks * 2 * (0.625 if causal else 1)
    return pl.CostEstimate(
        flops=int(matmuls * area * 2 * 256), bytes_accessed=16 * seq * 128 * blocks, transcendentals=int(area)
    )


def attend_fwd(q, k, v, length, causal):
    seq, width = q.shape
    spec = pl.BlockSpec((seq, 128), lambda i: (0, i))
    return pl.pallas_call(
        functools.partial(fwd_kernel, causal),
        grid=(width // 128,),
        in_specs=[pl.BlockSpec(memory_space=pltpu.SMEM)] + [spec] * 3,
        out_specs=[spec] * 2,
        out_shape=[jax.ShapeDtypeStruct((seq, width), bf16)] * 2,
        scratch_shapes=[pltpu.VMEM((2, seq, 256), bf16)] * 2,
        compiler_params=pltpu.CompilerParams(vmem_limit_bytes=48 * 2**20),
        cost_estimate=cost(2, width // 128, seq, causal),
        name="attend_causal" if causal else "attend_memory",
    )(length, q, k, v)


def back_scratch(seq):
    vmem = pltpu.VMEM
    return [
        vmem((seq, 256), bf16),
        vmem((2, seq, 128), bf16),
        vmem((2, seq, 256), bf16),
        vmem((seq, 256), bf16),
        vmem((2, seq, 128), bf16),
        vmem((2, seq, 256), bf16),
        vmem((128, seq), f32),
        vmem((2, 128, seq), bf16),
    ]


def back_pair(causal, length, q2, k2, v2, c2, aug, g2, grads, scratch, tick):
    qs, qm, ka, gs, gm, va, dqa, kt = scratch
    seq = k2.shape[0]
    lane = lanes(seq)
    l64 = lane % 64
    zero = jnp.zeros_like(k2)
    one = jnp.ones_like(k2)
    scale = jnp.asarray(HD**-0.5, bf16)
    prod = c2.astype(f32) * g2.astype(f32)
    d0 = jnp.sum(jnp.where(lane < 64, prod, 0.0), axis=1, keepdims=True)
    d1 = jnp.sum(jnp.where(lane < 64, 0.0, prod), axis=1, keepdims=True)
    qs[:, :128] = q2 * scale
    if not causal:
        aug = jnp.where(l64 == 3, one, aug)
        pos = lax.broadcasted_iota(jnp.int32, (seq, 128), 0)
        bias = jnp.where(pos >= length, -1e30, 0.0).astype(bf16)
    qs[:, 128:] = aug
    gs[:, :128] = g2
    gs[:, 128:] = place3(-jnp.where(lane < 64, d0, d1), seq)
    for h in range(2):
        own = (lane // 64) == h
        sel = own & (l64 < 3)
        qm[h] = jnp.where(own, q2 * scale, zero)
        gm[h] = jnp.where(own, g2, zero)
        ka[h, :, :128] = jnp.where(own, k2, zero)
        ko = jnp.where(sel, one, zero)
        if not causal:
            ko = jnp.where(own & (l64 == 3), bias, ko)
        ka[h, :, 128:] = ko
        va[h, :, :128] = jnp.where(own, v2, zero)
        va[h, :, 128:] = jnp.where(sel, one, zero)
        kt[h] = ka[h, :, :128].T
    dqa[...] = jnp.zeros_like(dqa)
    grads[:, 384:] = c2
    for j in range(seq // BLK):
        rows = slice(j * BLK, (j + 1) * BLK)
        q0 = j * BLK if causal else 0
        dk = None
        dv = None
        dq = None
        for h in range(2):
            p = jnp.exp(dot(ka[h, rows, :], qs[q0:, :], NT))
            if causal:
                a = lax.broadcasted_iota(jnp.int32, (BLK, BLK), 0)
                b = lax.broadcasted_iota(jnp.int32, (BLK, BLK), 1)
                d = jnp.where(a <= b, p[:, :BLK], 0.0)
                p = d if q0 + BLK == seq else jnp.concatenate([d, p[:, BLK:]], axis=1)
            dp = dot(va[h, rows, :], gs[q0:, :], NT)
            ds = (p * dp).astype(bf16)
            p = p.astype(bf16)
            a = dot(p, gm[h, q0:, :])
            b = dot(ds, qm[h, q0:, :])
            c = dot(kt[h, :, rows], ds)
            dv = a if dv is None else dv + a
            dk = b if dk is None else dk + b
            dq = c if dq is None else dq + c
        dqa[:, q0:] += dq
        grads[rows, 128:256] = dk.astype(bf16)
        grads[rows, 256:384] = dv.astype(bf16)
        tick(j)
    grads[:, :128] = (dqa[...] * HD**-0.5).T.astype(bf16)


BOTH = (0, 1)
X, CORE, Y, Z1, Z2 = range(5)
DELAY = 3
SLOTS = 2 * DELAY
CHUNK = 64
SUBS = 4
QUADS = 4
WIDTH = 512
LEAD = 5
LINKS = (CORE, X, Y, Z1, Z2, Y, CORE, CORE)
CHUNKS = 4 * QUADS * SUBS
TICKS = CHUNKS + LEAD + 7 * DELAY
STEPS = 2 * QUADS
FEED_TICKS, CROSS_TICKS, SELF_TICKS, NORM_TICKS = 2, 3, 2, 4
CROSS_AT = STEPS * FEED_TICKS + NORM_TICKS
SELF_AT = CROSS_AT + STEPS * CROSS_TICKS + NORM_TICKS
DRAIN_AT = SELF_AT + STEPS * SELF_TICKS
TILE = 256
dma_sem = pltpu.SemaphoreType.DMA


def partner(bit):
    d = lax.axis_index("dp")
    t = lax.axis_index("tensor")
    if bit == 0:
        return (d, 1 - t)
    size = 2 ** (bit - 1)
    return (d + size * (1 - 2 * ((d // size) % 2)), t)


def greet():
    barrier = pltpu.get_barrier_semaphore()
    for bit in range(5):
        pl.semaphore_signal(barrier, inc=1, device_id=partner(bit), device_id_type=pl.DeviceIdType.MESH)
    pl.semaphore_wait(barrier, 5)


def remote_copy(src, dst, send, recv, bit):
    return pltpu.make_async_remote_copy(
        src_ref=src,
        dst_ref=dst,
        send_sem=send,
        recv_sem=recv,
        device_id=partner(bit),
        device_id_type=pl.DeviceIdType.MESH,
    )


def stream_scratch():
    return [
        pltpu.VMEM((2, SLOTS, 2, 2, CHUNK, WIDTH), bf16),
        pltpu.VMEM((3, SLOTS, 2, CHUNK, WIDTH), bf16),
        pltpu.VMEM((6, SLOTS, CHUNK, WIDTH), bf16),
        dma_sem((8, SLOTS)),
        dma_sem((8, SLOTS)),
        dma_sem((2, SLOTS)),
    ]


def stream_stage(stage, c, queue, out, pairs, wide, narrow, send, recv, local):
    d = lax.axis_index("dp")
    core = d % 2
    y = (d // 2) % 2
    slot = lax.rem(c, SLOTS)
    block = c // SUBS
    sub = lax.rem(c, SUBS)
    away, came, own = [wide.at[i, slot] for i in range(3)]
    got_y, s3, got_z, s4, got_zz, s5 = [narrow.at[i, slot] for i in range(6)]

    def remote(k):
        src, dst = (
            (queue.at[block, :, 1 - core, :, sub], pairs.at[0, slot]),
            (away, came),
            (own.at[1 - y], got_y),
            (s3, got_z),
            (s4, got_zz),
            (s5, out.at[block, core, y, sub]),
            (s5, out.at[block, core, y, sub]),
            (out.at[block, core, 1 - y, sub], out.at[block, core, 1 - y, sub]),
        )[k]
        return remote_copy(src, dst, send.at[k, slot], recv.at[k, slot], LINKS[k])

    def load():
        return pltpu.make_async_copy(queue.at[block, :, core, :, sub], pairs.at[1, slot], local.at[0, slot])

    def keep():
        return pltpu.make_async_copy(s5, out.at[block, core, y, sub], local.at[1, slot])

    if stage == 0:
        remote(0).start()
        load().start()
    elif stage == 1:
        remote(0).wait()
        load().wait()
        away[...] = pairs[1, slot, 1] + pairs[0, slot, 1]
        remote(1).start()
        own[...] = pairs[1, slot, 0] + pairs[0, slot, 0]
    elif stage == 2:
        remote(1).wait()
        own[...] = own[...] + came[...]
        remote(2).start()
    elif stage == 3:
        remote(2).wait()
        s3[...] = wide[2, slot, y] + got_y[...]
        remote(3).start()
    elif stage == 4:
        remote(3).wait()
        s4[...] = s3[...] + got_z[...]
        remote(4).start()
    elif stage == 5:
        remote(4).wait()
        s5[...] = s4[...] + got_zz[...]
        remote(5).start()
        remote(6).start()
        keep().start()
    elif stage == 6:
        remote(5).wait()
        remote(6).wait()
        keep().wait()
        remote(7).start()
    else:
        remote(7).wait()


def small_scratch(shape):
    return [pltpu.VMEM((6,) + shape, f32), pltpu.VMEM((5,) + shape, f32), dma_sem((5,)), dma_sem((5,))]


def small_stage(k, out, acc, got, send, recv):
    def remote(i):
        return remote_copy(acc.at[i], got.at[i], send.at[i], recv.at[i], i)

    if k > 0:
        remote(k - 1).wait()
        acc[k] = acc[k - 1] + got[k - 1]
    if k < 5:
        remote(k).start()
    else:
        out[...] = acc[5]


def norm_step(index, more, weights, gain_ref, sum_ref, total, dc, left, acc, zt, sems, tick):
    def fetch_tile(a):
        slot = lax.rem(a, 2)
        rows = pl.ds(pl.multiple_of(a * TILE, TILE), TILE)
        return pltpu.make_async_copy(sum_ref.at[rows], zt.at[slot], sems.at[slot])

    tiles = total.shape[0] // TILE
    fetch_tile(0).start()

    @pl.loop(0, tiles)
    def _(a):
        rows = pl.ds(pl.multiple_of(a * TILE, TILE), TILE)
        fetch_tile(a).wait()

        @pl.when(a + 1 < tiles)
        def _():
            fetch_tile(a + 1).start()

        z = zt[lax.rem(a, 2)]
        dh = total[rows, :]
        for x, w in more:
            dh = dh + dot(x[rows, :], w[...], NT)
        centered = z - jnp.mean(z, axis=1, keepdims=True)
        r = lax.rsqrt(jnp.mean(centered * centered, axis=1, keepdims=True) + norm_eps)
        n = centered * r
        acc[0, index : index + 1, :] = acc[0, index : index + 1, :] + jnp.sum(dh * n, axis=0, keepdims=True)
        acc[0, 3 + index : 4 + index, :] = acc[0, 3 + index : 4 + index, :] + jnp.sum(dh, axis=0, keepdims=True)
        e = dh * gain_ref[index : index + 1, :]
        dz = r * (e - jnp.mean(e, axis=1, keepdims=True) - n * jnp.mean(e * n, axis=1, keepdims=True))
        total[rows, :] = alpha_res * dz
        g = dz.astype(bf16)
        left[:, rows] = g.T
        for i in BOTH:
            dc[i, rows, :] = dot(g, weights[i][...], NT).astype(bf16)
        tick(a)


def back_kernel(*refs):
    refs = list(refs)
    take = lambda n: [refs.pop(0) for _ in range(n)]
    (len_ref,) = take(1)
    cross_in = [take(5) for _ in BOTH]
    self_in = [take(5) for _ in BOTH]
    co = take(2)
    gain_ref, small_ref = take(2)
    feed_in = [take(4) for _ in BOTH]
    g3_ref, g3t_ref, h2t_ref, h1t_ref, memt_ref, tart_ref, base_ref, sum2_ref, sum1_ref = take(9)
    cq_in, so_in, kv_in, qkv_in = take(2), take(2), take(2), take(2)
    dmem_ref, dtar_ref, out, queue, small_out = take(5)
    grads, *scratch = take(9)
    stream = [queue, out] + take(6)
    small_refs = [small_out] + take(4)
    acc = small_refs[1]
    lefts, tall, flat, total, ends, dc, zt, staged = take(8)
    left_sems, feed_sems, zt_sems, staged_sems, base_sem = take(5)
    step = pl.program_id(0)
    half = lax.rem(step, 2)
    pair = lax.rem(step // 2, QUADS)

    def tick(t):
        for stage in range(7, -1, -1):
            c = t - LEAD - DELAY * stage
            pl.when((c >= 0) & (c < CHUNKS))(functools.partial(stream_stage, stage, c, *stream))

    def load_left(i, ref):
        return pltpu.make_async_copy(ref, lefts.at[i], left_sems.at[i])

    def load_feed(i, j):
        cols_j = pl.ds(pl.multiple_of(j * WIDTH, WIDTH), WIDTH)
        act, slope, up, down = feed_in[i]
        return [
            pltpu.make_async_copy(act.at[:, cols_j], tall.at[0, i], feed_sems.at[0, i]),
            pltpu.make_async_copy(slope.at[:, cols_j], tall.at[1, i], feed_sems.at[1, i]),
            pltpu.make_async_copy(up.at[:, cols_j], tall.at[2, i], feed_sems.at[2, i]),
            pltpu.make_async_copy(down.at[cols_j], flat.at[i], feed_sems.at[3, i]),
        ]

    def load_late():
        return [
            copy
            for i in BOTH
            for copy in (
                pltpu.make_async_copy(kv_in[i].at[0], tall.at[0, i], feed_sems.at[0, i]),
                pltpu.make_async_copy(kv_in[i].at[1], tall.at[1, i], feed_sems.at[1, i]),
                pltpu.make_async_copy(cq_in[i], tall.at[2, i], feed_sems.at[2, i]),
                pltpu.make_async_copy(so_in[i], flat.at[i], feed_sems.at[3, i]),
            )
        ]

    def load_last():
        return [pltpu.make_async_copy(qkv_in[i].at[m], tall.at[m, i], feed_sems.at[m, i]) for i in BOTH for m in range(3)]

    def input_grad(rows, members, start):
        for m in range(members):
            for i in BOTH:
                term = dot(ends[m, i, rows, :], tall[m, i], NT)
                start = term if start is None else start + term
        lefts[1, rows, :] = start.astype(bf16)

    def send_grad(ref):
        return pltpu.make_async_copy(lefts.at[1], ref, base_sem)

    def post(slot, block):
        return pltpu.make_async_copy(staged.at[slot], queue.at[block, half], staged_sems.at[slot])

    def products(slot, block, spans, ticks):
        for a in range(2):
            rows = slice(2 * a * TILE, 2 * (a + 1) * TILE)
            for left, right, lo, hi in spans:
                result = dot(lefts[left, rows, :], right[:, lo:hi]).astype(bf16)
                staged[slot, a, :, :, :, lo:hi] = result.reshape(2, SUBS, CHUNK, hi - lo)
            if a in ticks:
                tick(ticks[a])
        post(slot, block).start()

    @pl.when(step == 0)
    def _():
        for copy in load_feed(0, 0) + [load_left(i, r) for i, r in enumerate((g3t_ref, h2t_ref, g3_ref))]:
            copy.start()
        base = pltpu.make_async_copy(base_ref, total, base_sem)
        base.start()
        acc[0] = small_ref[...]
        greet()
        for copy in [load_left(i, r) for i, r in enumerate((g3t_ref, h2t_ref, g3_ref))]:
            copy.wait()
        base.wait()

    @pl.when(step < STEPS)
    def _():
        t = step * FEED_TICKS
        for i in BOTH:

            @pl.when(half == i)
            def _(i=i):
                for copy in load_feed(i, pair):
                    copy.wait()

                @pl.when(step < STEPS - 1)
                def _():
                    for copy in load_feed(1 - i, pair + i):
                        copy.start()

        for a in range(2):
            rows = slice(2 * a * TILE, 2 * (a + 1) * TILE)
            du = dot(lefts[2, rows, :], flat[half], NT) * tall[1, half, rows, :].astype(f32)
            grads[rows, :] = du.astype(bf16)
        @pl.when(step > 0)
        def _():
            post(0, 0).wait()

        products(0, 2 * pair, ((0, tall.at[0, half], 0, WIDTH),), {1: t})
        for a in range(2):
            rows = slice(2 * a * TILE, 2 * (a + 1) * TILE)
            total[rows, :] += dot(grads[rows, :], tall[2, half], NT)

        @pl.when(step > 0)
        def _():
            post(1, 0).wait()

        products(1, 2 * pair + 1, ((1, grads, 0, WIDTH),), {1: t + 1})

    @pl.when(step == STEPS)
    def _():
        fetch = [load_left(0, h1t_ref), load_left(1, memt_ref)]
        for copy in fetch + load_late():
            copy.start()
        norm_step(
            1, [], co, gain_ref, sum2_ref, total, dc, lefts.at[2], acc, zt, zt_sems, lambda k: tick(STEPS * FEED_TICKS + k)
        )
        for copy in fetch:
            copy.wait()
        post(1, 0).wait()

    at = pl.ds(pl.multiple_of(pair * 128, 128), 128)

    @pl.when((step >= STEPS) & (step < 2 * STEPS))
    def _():
        t = CROSS_AT + (step - STEPS) * CROSS_TICKS
        q2, k2, v2, c2, aug = [jnp.where(half == 0, a[...], b[...]) for a, b in zip(*cross_in)]

        def ticks(j):
            if j % 2 == 1:
                tick(t + j // 2)

        back_pair(False, len_ref[0], q2, k2, v2, c2, aug, dc[half, :, at], grads, scratch, ticks)
        ends[2, half, :, at] = grads[:, :128]
        ends[0, half, :, at] = grads[:, 128:256]
        ends[1, half, :, at] = grads[:, 256:384]
        post(0, 0).wait()
        spans = ((0, grads, 0, 128), (1, grads, 128, 384), (2, grads, 384, 512))
        products(0, 2 * QUADS + pair, spans, {1: t + 2})

    @pl.when(step == 2 * STEPS)
    def _():
        fetch = load_left(0, tart_ref)
        fetch.start()
        for copy in load_late():
            copy.wait()
        more = [(ends.at[2, i], tall.at[2, i]) for i in BOTH]
        so = [flat.at[i] for i in BOTH]
        norm_step(
            0, more, so, gain_ref, sum1_ref, total, dc, lefts.at[2], acc, zt, zt_sems, lambda k: tick(SELF_AT - NORM_TICKS + k)
        )
        fetch.wait()

        @pl.loop(0, 4)
        def _(a):
            input_grad(pl.ds(pl.multiple_of(a * TILE, TILE), TILE), 2, None)

        send_grad(dmem_ref).start()
        for copy in load_last():
            copy.start()

    @pl.when(step >= 2 * STEPS)
    def _():
        t = SELF_AT + (step - 2 * STEPS) * SELF_TICKS
        q2, k2, v2, c2, aug = [jnp.where(half == 0, a[...], b[...]) for a, b in zip(*self_in)]
        def ticks(j):
            if j == 0:
                tick(t)

        back_pair(True, 0, q2, k2, v2, c2, aug, dc[half, :, at], grads, scratch, ticks)
        ends[0, half, :, at] = grads[:, :128]
        ends[1, half, :, at] = grads[:, 128:256]
        ends[2, half, :, at] = grads[:, 256:384]
        post(0, 0).wait()
        products(0, 3 * QUADS + pair, ((0, grads, 0, 384), (2, grads, 384, 512)), {0: t + 1})
        for k in range(5, -1, -1):
            pl.when(step == 2 * STEPS + 1 + k)(functools.partial(small_stage, k, *small_refs))

    @pl.when(step == 3 * STEPS - 1)
    def _():
        post(0, 0).wait()
        send_grad(dmem_ref).wait()
        for copy in load_last():
            copy.wait()

        @pl.loop(0, 4)
        def _(a):
            tick(DRAIN_AT + a)
            rows = pl.ds(pl.multiple_of(a * TILE, TILE), TILE)
            input_grad(rows, 3, total[rows, :])

        send_grad(dtar_ref).start()
        pl.loop(DRAIN_AT + 4, TICKS)(tick)
        send_grad(dtar_ref).wait()


def layer_back(length, cross_in, self_in, weights, gain, small, feed_in, rest):
    seq, width = cross_in[0][0].shape
    model = gain.shape[1]
    early = lambda s: jnp.clip(s - STEPS, 0, STEPS - 1)
    late = lambda s: jnp.clip(s - 2 * STEPS, 0, STEPS - 1)
    cross_spec = pl.BlockSpec((seq, 128), lambda s: (0, early(s) // 2))
    self_spec = pl.BlockSpec((seq, 128), lambda s: (0, late(s) // 2))
    anywhere = pl.BlockSpec(memory_space=pl.ANY)
    full = lambda x: pl.BlockSpec(x.shape, lambda s: (0, 0), pipeline_mode=pl.Buffered(1))
    shape = jax.ShapeDtypeStruct
    vmem = pltpu.VMEM
    blocks = 4 * QUADS
    return pl.pallas_call(
        back_kernel,
        grid=(3 * STEPS,),
        in_specs=[pl.BlockSpec(memory_space=pltpu.SMEM)]
        + [cross_spec] * 10
        + [self_spec] * 10
        + [full(x) for x in (*weights, gain, small)]
        + [anywhere] * 25,
        out_specs=[anywhere] * 4 + [full(small)],
        out_shape=[shape((seq, model), bf16)] * 2
        + [
            shape((blocks, 2, 2, SUBS, CHUNK, WIDTH), bf16),
            shape((blocks, 2, 2, 2, SUBS, CHUNK, WIDTH), bf16),
            shape(small.shape, f32),
        ],
        scratch_shapes=[vmem((seq, WIDTH), bf16)]
        + back_scratch(seq)
        + stream_scratch()
        + small_scratch(small.shape)
        + [
            vmem((3, model, seq), bf16),
            vmem((3, 2, seq, WIDTH), bf16),
            vmem((2, WIDTH, model), bf16),
            vmem((seq, model), f32),
            vmem((3, 2, seq, width), bf16),
            vmem((2, seq, width), bf16),
            vmem((2, TILE, model), f32),
            vmem((2, 2, 2, SUBS, CHUNK, WIDTH), bf16),
            dma_sem((3,)),
            dma_sem((4, 2)),
            dma_sem((2,)),
            dma_sem((2,)),
            dma_sem,
        ],
        compiler_params=pltpu.CompilerParams(
            collective_id=1, has_side_effects=True, vmem_limit_bytes=60 * 2**20
        ),
        cost_estimate=cost(16, 8, seq, False),
        name="layer_back",
    )(length, *cross_in[0], *cross_in[1], *self_in[0], *self_in[1], *weights, gain, small, *feed_in[0], *feed_in[1], *rest)


ALL = ("dp", "tensor")
DEVICES = 32


def swap(x, flip):
    return lax.ppermute(x, ALL, [(i, i ^ flip) for i in range(DEVICES)])


def swap_tensor(x):
    return swap(x, 1)


def swap_core(x):
    return swap(x, 2)


def swap_y(x):
    return swap(x, 4)


def my_block():
    d = lax.axis_index("dp")
    return 2 * (d % 2) + (d // 2) % 2


def add_low(*terms):
    return sum(t.astype(f32) for t in terms).astype(bf16)


def blocks_of(own, axis):
    size = own.shape[axis] // 4
    return [lax.dynamic_slice_in_dim(own, (my_block() ^ j) * size, size, axis) for j in range(4)]


def swap_pieces(x, move):
    return [move(p) for p in x] if isinstance(x, (list, tuple)) else move(x)


def tie(*xs):
    return lax.optimization_barrier(xs)


class Pipe:
    def __init__(self):
        self.live = []

    def put(self, gen):
        wait, arrays = next(gen)
        self.live.append([gen, wait, arrays])

    def step(self, due, landed):
        done = 0
        for item in due:
            arrays = landed[done : done + len(item[2])]
            done += len(item[2])
            try:
                item[1], item[2] = item[0].send(arrays)
            except StopIteration:
                self.live.remove(item)

    def cut(self, *xs):
        due = []
        for item in self.live:
            item[1] -= 1
            if item[1] <= 0:
                due.append(item)
        tied = tie(*xs, *[a for item in due for a in item[2]])
        self.step(due, tied[len(xs) :])
        return tied[: len(xs)] if len(xs) > 1 else tied[0]

    def drain(self):
        while self.live:
            self.step(list(self.live), [a for item in self.live for a in item[2]])


def fetch(out, key, block, waits):
    far = swap_tensor(block)
    (far,) = yield waits[0], [far]
    side = swap_y(far)
    near = swap_core(far)
    side, near = yield waits[1], [side, near]
    out[key] = [far, side, near, swap_core(side)]
    return


def ffn_kernel(h_ref, up_ref, down_ref, a_ref, d_ref, b_ref):
    h = h_ref[...]
    size = 512
    total = None
    for j in range(4):
        cols = slice(j * size, (j + 1) * size)
        u = dot(h, up_ref[:, cols])
        cdf = 0.5 + 0.5 * lax.erf(u * (0.5**0.5))
        slope = cdf + u * (jnp.exp(-0.5 * u * u) * 0.3989422804014327)
        act = (u * cdf).astype(bf16)
        a_ref[:, cols] = act
        d_ref[:, cols] = slope.astype(bf16)
        term = dot(act, down_ref[cols, :])
        total = term if total is None else total + term
    b_ref[...] = total


def whole(x):
    return pl.BlockSpec(x.shape, lambda r: (0, 0))


ROWS = 512


def ffn_forward(h, up, down):
    seq, width = h.shape
    units = up.shape[1]
    rows = lambda w: pl.BlockSpec((ROWS, w), lambda r: (r, 0))
    return pl.pallas_call(
        ffn_kernel,
        grid=(seq // ROWS,),
        in_specs=[rows(width)] + [whole(up), whole(down)],
        out_specs=[rows(units), rows(units), rows(width)],
        out_shape=[jax.ShapeDtypeStruct((seq, units), bf16)] * 2 + [jax.ShapeDtypeStruct((seq, width), f32)],
        compiler_params=pltpu.CompilerParams(vmem_limit_bytes=50 * 2**20),
        cost_estimate=pl.CostEstimate(flops=4 * seq * width * units, bytes_accessed=22 * 2**20, transcendentals=2 * seq * units),
        name="feed_forward",
    )(h, up, down)


def arrange_kernel(me_ref, *refs):
    for j in range(4):

        @pl.when(pl.program_id(0) == j)
        def _(j=j):
            refs[4][...] = refs[j][...]


def arrange(slabs):
    members, rows, width = slabs[0].shape
    return pl.pallas_call(
        arrange_kernel,
        grid_spec=pltpu.PrefetchScalarGridSpec(
            num_scalar_prefetch=1,
            grid=(4,),
            in_specs=[pl.BlockSpec((members, rows, width), lambda j, me: (0, 0, 0))] * 4,
            out_specs=pl.BlockSpec((members, rows, width), lambda j, me: (0, j ^ me[0], 0)),
        ),
        out_shape=jax.ShapeDtypeStruct((members, 4 * rows, width), bf16),
        compiler_params=pltpu.CompilerParams(vmem_limit_bytes=40 * 2**20),
        cost_estimate=pl.CostEstimate(flops=0, bytes_accessed=16 * members * rows * width, transcendentals=0),
        name="arrange",
    )(my_block().reshape(1), *slabs)


def slab_of(own):
    rows = own.shape[1] // 4
    return lax.dynamic_slice_in_dim(own, my_block() * rows, rows, 1)


def spread_kernel(spans, x_ref, *out_refs):
    for lo, hi, k, m in spans:
        x = x_ref[:, lo:hi].astype(f32)
        if m is None:
            out_refs[k][...] = x.T
        else:
            out_refs[k][m] = x


def spread(pairs, first, spans, outs):
    _, rows, width = pairs.shape
    tile = 512
    specs = []
    shapes = []
    for members in outs:
        if members is None:
            specs.append(pl.BlockSpec((128, tile), lambda p, t: (p, t)))
            shapes.append(jax.ShapeDtypeStruct((512, rows), f32))
        else:
            specs.append(pl.BlockSpec((members, tile, 128), lambda p, t: (0, t, p)))
            shapes.append(jax.ShapeDtypeStruct((members, rows, 512), f32))
    return pl.pallas_call(
        functools.partial(spread_kernel, spans),
        grid=(4, rows // tile),
        in_specs=[pl.BlockSpec((None, tile, width), lambda p, t: (p + first, t, 0))],
        out_specs=specs,
        out_shape=shapes,
        compiler_params=pltpu.CompilerParams(vmem_limit_bytes=40 * 2**20),
        cost_estimate=pl.CostEstimate(flops=0, bytes_accessed=24 * rows * width, transcendentals=0),
        name="spread",
    )(pairs)


def flip_kernel(x_ref, out_ref):
    out_ref[...] = x_ref[...].T


def flip(x):
    rows, width = x.shape
    return pl.pallas_call(
        flip_kernel,
        grid=(4,),
        in_specs=[pl.BlockSpec((rows // 4, width), lambda i: (i, 0))],
        out_specs=pl.BlockSpec((width, rows // 4), lambda i: (0, i)),
        out_shape=jax.ShapeDtypeStruct((width, rows), x.dtype),
        cost_estimate=pl.CostEstimate(flops=0, bytes_accessed=4 * rows * width, transcendentals=0),
        name="flip",
    )(x)


def spread_feed_kernel(x_ref, down_ref, up_ref):
    even = lax.rem(pl.program_id(0), 2) == 0

    @pl.when(even)
    def _():
        down_ref[...] = x_ref[...].astype(f32).T

    @pl.when(jnp.logical_not(even))
    def _():
        up_ref[...] = x_ref[...].astype(f32)


def spread_feed(blocks):
    _, rows, width = blocks.shape
    return pl.pallas_call(
        spread_feed_kernel,
        grid=(8,),
        in_specs=[pl.BlockSpec((None, rows, width), lambda b: (b, 0, 0))],
        out_specs=[
            pl.BlockSpec((width, rows), lambda b: (b // 2, 0)),
            pl.BlockSpec((rows, width), lambda b: (0, b // 2)),
        ],
        out_shape=[jax.ShapeDtypeStruct((4 * width, rows), f32), jax.ShapeDtypeStruct((rows, 4 * width), f32)],
        compiler_params=pltpu.CompilerParams(vmem_limit_bytes=40 * 2**20),
        cost_estimate=pl.CostEstimate(flops=0, bytes_accessed=48 * rows * width, transcendentals=0),
        name="spread_feed",
    )(blocks)


def one_pair_each(
    target,
    memory,
    mem_len,
    grad_out,
    self_qkv,
    self_out,
    cross_query,
    cross_kv,
    cross_out,
    ffn_up,
    ffn_down,
    ln_gain,
    ln_bias,
):
    length = lax.dynamic_slice_in_dim(mem_len, lax.axis_index("tensor"), 1)
    pipe = Pipe()
    got = {}
    so3, cq3, co3 = self_out[None], cross_query[None], cross_out[None]

    pipe.put(fetch(got, "qkv", slab_of(self_qkv), (1, 1)))
    q1 = [[dot(target, self_qkv[m]).astype(bf16) for m in range(3)], None]
    at1 = [attend_fwd(*q1[0], length, True), None]
    so_s, cq_s, kv_s, co_s = [slab_of(x) for x in (so3, cq3, cross_kv, co3)]
    mem, so_s, cq_s, kv_s, _ = pipe.cut(memory, so_s, cq_s, kv_s, at1[0][0])
    pipe.put(fetch(got, "so", so_s, (1, 1)))
    pipe.put(fetch(got, "cq", cq_s, (1, 1)))
    pipe.put(fetch(got, "kv", kv_s, (1, 1)))
    kv = [[dot(mem, cross_kv[m]).astype(bf16) for m in range(2)], None]
    up_s, down_s = slab_of(ffn_up[None]), slab_of(ffn_down[None])
    target_t = flip(target)
    memory_t = flip(mem)
    kv[0][0], up_s, co_s, target_t, memory_t = tie(kv[0][0], up_s, co_s, target_t, memory_t)
    tar, kv[0][0], kv[0][1], target_t, memory_t = pipe.cut(target, *kv[0], target_t, memory_t)
    qkv_oth = arrange(got["qkv"])
    q1[1] = [dot(tar, qkv_oth[m]).astype(bf16) for m in range(3)]
    pipe.put(fetch(got, "co", co_s, (1, 1)))
    q1[1][0], up_s = tie(q1[1][0], up_s)
    pipe.put(fetch(got, "up", up_s, (2, 1)))
    at1[1] = attend_fwd(*q1[1], length, True)
    at1[1], _ = tie(at1[1], at1[1][0])
    c1_oth = pipe.cut(at1[1][0])
    c1 = [at1[0][0], c1_oth]
    so_oth = arrange(got["so"])[0]
    b1 = dot(c1[0], self_out) + dot(c1[1], so_oth)
    sum1 = alpha_res * target.astype(f32) + b1
    h1 = norm_rows(sum1, ln_gain[0], ln_bias[0])
    h1_low = h1.astype(bf16)
    cq_oth = arrange(got["cq"])[0]
    kv_oth = arrange(got["kv"])
    q2 = [dot(h1_low, cross_query).astype(bf16), dot(h1_low, cq_oth).astype(bf16)]
    kv[1] = [dot(memory, kv_oth[m]).astype(bf16) for m in range(2)]
    q2[0], kv[1][0], down_s = pipe.cut(q2[0], kv[1][0], down_s)
    pipe.put(fetch(got, "down", down_s, (1, 1)))
    at2 = [attend_fwd(q2[0], *kv[0], length, False), None]
    h1_again, _ = tie(h1_low, at2[0][0])
    h1_t = flip(h1_again)
    q2[1], h1_t, _ = pipe.cut(q2[1], h1_t, at2[0][0])
    at2[1] = attend_fwd(q2[1], *kv[1], length, False)
    co_oth = arrange(got["co"])[0]
    c2 = [at2[0][0], at2[1][0]]
    c2[1] = pipe.cut(c2[1])
    b2 = dot(c2[0], cross_out) + dot(c2[1], co_oth)
    sum2 = alpha_res * h1 + b2
    h2 = norm_rows(sum2, ln_gain[1], ln_bias[1])
    h2_low = h2.astype(bf16)
    act0, slope0, b3 = ffn_forward(h2_low, ffn_up, ffn_down)
    h2_t = flip(h2_low)
    while "up" not in got or "down" not in got:
        act0 = pipe.cut(act0)
    h2_again, h1_t, h2_t, _ = tie(h2_low, h1_t, h2_t, act0)
    up_oth, down_oth = arrange(got["up"])[0], arrange(got["down"])[0]
    act1, slope1, b3b = ffn_forward(h2_again, up_oth, down_oth)
    result, back3 = jax.vjp(norm_rows, alpha_res * h2 + b3 + b3b, ln_gain[2], ln_bias[2])
    dz3, gain3, bias3 = back3(grad_out.astype(f32))
    g3 = dz3.astype(bf16)
    none = jnp.zeros_like(gain3)
    small = jnp.stack([none, none, gain3, none, none, bias3, none, none])
    dmem, dtar, blocks, _, small = layer_back(
        length,
        [[q2[i], *kv[i], c2[i], at2[i][1]] for i in BOTH],
        [[*q1[i], c1[i], at1[i][1]] for i in BOTH],
        (cross_out, co_oth),
        ln_gain,
        small,
        [(act0, slope0, ffn_up, ffn_down), (act1, slope1, up_oth, down_oth)],
        (g3, flip(g3), h2_t, h1_t, memory_t, target_t, alpha_res * dz3, sum2, sum1)
        + (cross_query, cq_oth, self_out, so_oth, cross_kv, kv_oth, self_qkv, qkv_oth),
    )
    blocks = blocks.reshape(16, 1024, 512)
    cq_total, kv_total, co_total = spread(
        blocks,
        8,
        ((0, 128, 0, 0), (128, 256, 1, 0), (256, 384, 1, 1), (384, 512, 2, None)),
        (1, 2, None),
    )
    qkv_total, so_total = spread(
        blocks,
        12,
        ((0, 128, 0, 0), (128, 256, 0, 1), (256, 384, 0, 2), (384, 512, 1, None)),
        (3, None),
    )
    down_total, up_total = spread_feed(blocks)
    return (
        result.astype(bf16),
        dtar,
        dmem,
        qkv_total,
        so_total,
        cq_total[0],
        kv_total,
        co_total,
        up_total,
        down_total,
        small[:3],
        small[3:6],
    )


def solution(mesh):
    placed = (
        P(("dp", "tensor"), None),
        P(("dp", "tensor"), None),
        P("dp"),
        P(("dp", "tensor"), None),
        P(None, None, "tensor"),
        P("tensor", None),
        P(None, "tensor"),
        P(None, None, "tensor"),
        P("tensor", None),
        P(None, "tensor"),
        P("tensor", None),
        P(),
        P(),
    )
    body = one_pair_each if mesh.shape["tensor"] == 2 and mesh.shape["dp"] == 16 else on_device
    return jax.shard_map(
        body,
        mesh=mesh,
        in_specs=placed,
        out_specs=(
            P(("dp", "tensor"), None),
            P(("dp", "tensor"), None),
            P(("dp", "tensor"), None),
            P(None, None, "tensor"),
            P("tensor", None),
            P(None, "tensor"),
            P(None, None, "tensor"),
            P("tensor", None),
            P(None, "tensor"),
            P("tensor", None),
            P(),
            P(),
        ),
        check_vma=False,
    )
```

```python
import functools

import jax
import jax.numpy as jnp
from jax import lax
from jax.experimental import pallas as pl
from jax.experimental.pallas import tpu as pltpu
from jax.sharding import PartitionSpec as P

HD = 64


alpha_res = 300.0**0.25
norm_eps = 1e-05
mask_fill = -1e30
contract_rows = (((0,), (0,)), ((), ()))
contract_cols = (((1,), (1,)), ((), ()))


def norm_rows(resid, gain_vec, bias_vec):
    average = jnp.mean(resid, axis=-1, keepdims=True)
    centered = resid - average
    variance = jnp.mean(centered * centered, axis=-1, keepdims=True)
    return centered * lax.rsqrt(variance + norm_eps) * gain_vec + bias_vec


def exact_gelu(values_in):
    return jax.nn.gelu(values_in, approximate=False)


def gather_rows(local_rows):
    return lax.all_gather(local_rows, "tensor", axis=0, tiled=True)


def gather_grads(local_rows):
    return lax.all_gather(local_rows, "tensor", axis=0, tiled=True)


def scatter_branch(left_mat, right_mat, row_count):

    def partial_term(offset, num_rows):
        return jnp.dot(left_mat, right_mat, preferred_element_type=jnp.float32)

    return lax.psum_scatter(
        partial_term(jnp.int32(0), row_count * lax.axis_size("tensor")),
        "tensor",
        scatter_dimension=0,
        tiled=True,
    )


def project_context(context, weight_local, row_count):
    return scatter_branch(context, weight_local, row_count)


def scatter_inputs(factor_pairs, row_count):

    def partial_term(offset, num_rows):
        terms = [
            lax.dot_general(grad_mat, weight_mat, contract_cols, preferred_element_type=jnp.float32)
            for grad_mat, weight_mat in factor_pairs
        ]
        return sum(terms)

    return lax.psum_scatter(
        partial_term(jnp.int32(0), row_count * lax.axis_size("tensor")).astype(jnp.bfloat16),
        "tensor",
        scatter_dimension=0,
        tiled=True,
    ).astype(jnp.float32)


def block_view(flat, pair_count, block_rows):
    tok_count, col_count = flat.shape
    seq_len = tok_count // pair_count
    return flat.reshape(pair_count, seq_len // block_rows, block_rows, col_count // HD, HD)


def pair_view(flat, pair_count):
    tok_count, col_count = flat.shape
    return flat.reshape(pair_count, tok_count // pair_count, col_count // HD, HD)


def block_scores(query_blk, key_pair, start_row, key_len, causal):
    block_rows = query_blk.shape[0]
    seq_len = key_pair.shape[0]
    products = jnp.einsum(
        "qhd,khd->hqk", query_blk, key_pair, preferred_element_type=jnp.float32
    ) * HD ** (-0.5)
    key_pos = lax.broadcasted_iota(jnp.int32, (block_rows, seq_len), 1)
    query_pos = start_row + lax.broadcasted_iota(jnp.int32, (block_rows, seq_len), 0)
    allowed = key_pos < key_len
    if causal:
        allowed = allowed & (key_pos <= query_pos)
    return jnp.where(allowed[None], products, mask_fill)


def attend_forward(queries, key_rows, value_rows, key_lens, causal):
    pair_count = key_lens.shape[0]
    seq_len = queries.shape[0] // pair_count
    block_rows = min(512, seq_len)
    starts = lax.iota(jnp.int32, seq_len // block_rows) * block_rows

    def one_pair(packed):
        query_pair, key_pair, value_pair, key_len = packed

        def one_block(inner):
            query_blk, start_row = inner
            scores = block_scores(query_blk, key_pair, start_row, key_len, causal)
            row_max = jnp.max(scores, axis=-1, keepdims=True)
            shifted = jnp.exp(scores - row_max)
            row_total = jnp.sum(shifted, axis=-1, keepdims=True)
            attn_prob = (shifted / row_total).astype(jnp.bfloat16)
            context = jnp.einsum(
                "hqk,khd->qhd", attn_prob, value_pair, preferred_element_type=jnp.float32
            )
            return (context.astype(jnp.bfloat16), (row_max + jnp.log(row_total))[..., 0])

        return lax.map(one_block, (query_pair, starts))

    context, log_total = lax.map(
        one_pair,
        (
            block_view(queries, pair_count, block_rows),
            pair_view(key_rows, pair_count),
            pair_view(value_rows, pair_count),
            key_lens,
        ),
    )
    return (context.reshape(queries.shape), log_total)


def attend_backward(queries, key_rows, value_rows, key_lens, causal, log_total, grad_context):
    pair_count = key_lens.shape[0]
    seq_len = queries.shape[0] // pair_count
    block_rows = min(512, seq_len)
    starts = lax.iota(jnp.int32, seq_len // block_rows) * block_rows
    score_scale = HD ** (-0.5)

    def one_pair(packed):
        query_pair, key_pair, value_pair, key_len, total_pair, grad_pair = packed

        def one_block(carry, inner):
            key_grad, value_grad = carry
            query_blk, start_row, total_blk, grad_blk = inner
            scores = block_scores(query_blk, key_pair, start_row, key_len, causal)
            attn_prob = jnp.exp(scores - total_blk[..., None])
            value_grad = value_grad + jnp.einsum(
                "hqk,qhd->khd",
                attn_prob.astype(jnp.bfloat16),
                grad_blk,
                preferred_element_type=jnp.float32,
            )
            prob_grad = jnp.einsum(
                "qhd,khd->hqk", grad_blk, value_pair, preferred_element_type=jnp.float32
            )
            score_grad = (
                attn_prob * (prob_grad - jnp.sum(attn_prob * prob_grad, axis=-1, keepdims=True))
            ).astype(jnp.bfloat16)
            query_grad = (
                jnp.einsum("hqk,khd->qhd", score_grad, key_pair, preferred_element_type=jnp.float32)
                * score_scale
            )
            key_grad = (
                key_grad
                + jnp.einsum(
                    "hqk,qhd->khd", score_grad, query_blk, preferred_element_type=jnp.float32
                )
                * score_scale
            )
            return ((key_grad, value_grad), query_grad.astype(jnp.bfloat16))

        zeros = jnp.zeros(key_pair.shape, jnp.float32)
        (key_grad, value_grad), query_grad = lax.scan(
            one_block, (zeros, zeros), (query_pair, starts, total_pair, grad_pair)
        )
        return (query_grad, key_grad.astype(jnp.bfloat16), value_grad.astype(jnp.bfloat16))

    query_grad, key_grad, value_grad = lax.map(
        one_pair,
        (
            block_view(queries, pair_count, block_rows),
            pair_view(key_rows, pair_count),
            pair_view(value_rows, pair_count),
            key_lens,
            log_total,
            block_view(grad_context, pair_count, block_rows),
        ),
    )
    return (
        query_grad.reshape(queries.shape),
        key_grad.reshape(queries.shape),
        value_grad.reshape(queries.shape),
    )


def on_device(
    target,
    memory,
    mem_len,
    grad_out,
    self_qkv,
    self_out,
    cross_query,
    cross_kv,
    cross_out,
    ffn_up,
    ffn_down,
    ln_gain,
    ln_bias,
):
    row_count = target.shape[0]
    pair_count = mem_len.shape[0]
    seq_len = row_count * lax.axis_size("tensor") // pair_count
    full_lens = jnp.full((pair_count,), seq_len, jnp.int32)
    target_all = gather_rows(target)
    qkv_rows = jnp.einsum(
        "td,ide->ite", target_all, self_qkv, preferred_element_type=jnp.float32
    ).astype(jnp.bfloat16)
    context_one, total_one = attend_forward(qkv_rows[0], qkv_rows[1], qkv_rows[2], full_lens, True)
    branch_one = project_context(context_one, self_out, row_count)
    normed_one, norm_back_one = jax.vjp(
        norm_rows, alpha_res * target.astype(jnp.float32) + branch_one, ln_gain[0], ln_bias[0]
    )
    normed_one_all = gather_rows(normed_one.astype(jnp.bfloat16))
    memory_all = gather_rows(memory)
    query_two = jnp.dot(normed_one_all, cross_query, preferred_element_type=jnp.float32).astype(
        jnp.bfloat16
    )
    kv_two = jnp.einsum(
        "td,ide->ite", memory_all, cross_kv, preferred_element_type=jnp.float32
    ).astype(jnp.bfloat16)
    context_two, total_two = attend_forward(query_two, kv_two[0], kv_two[1], mem_len, False)
    branch_two = project_context(context_two, cross_out, row_count)
    normed_two, norm_back_two = jax.vjp(
        norm_rows, alpha_res * normed_one + branch_two, ln_gain[1], ln_bias[1]
    )
    normed_two_low = normed_two.astype(jnp.bfloat16)
    normed_two_all = gather_rows(normed_two_low)
    hidden = jnp.dot(normed_two_all, ffn_up, preferred_element_type=jnp.float32)
    activated, gelu_back = jax.vjp(exact_gelu, hidden)
    activated_low = activated.astype(jnp.bfloat16)
    branch_three = scatter_branch(activated_low, ffn_down, row_count)
    result, norm_back_three = jax.vjp(
        norm_rows, alpha_res * normed_two + branch_three, ln_gain[2], ln_bias[2]
    )
    grad_sum_three, gain_three, bias_three = norm_back_three(grad_out.astype(jnp.float32))
    branch_grad_three = gather_grads(grad_sum_three.astype(jnp.bfloat16))
    down_grad = lax.dot_general(
        activated_low, branch_grad_three, contract_rows, preferred_element_type=jnp.float32
    )
    act_grad = lax.dot_general(
        branch_grad_three, ffn_down, contract_cols, preferred_element_type=jnp.float32
    )
    hidden_grad = gelu_back(act_grad)[0].astype(jnp.bfloat16)
    up_grad = lax.dot_general(
        normed_two_all, hidden_grad, contract_rows, preferred_element_type=jnp.float32
    )
    normed_two_grad = alpha_res * grad_sum_three + scatter_inputs(
        ((hidden_grad, ffn_up),), row_count
    )
    grad_sum_two, gain_two, bias_two = norm_back_two(normed_two_grad)
    branch_grad_two = gather_grads(grad_sum_two.astype(jnp.bfloat16))
    cross_out_grad = lax.dot_general(
        context_two, branch_grad_two, contract_rows, preferred_element_type=jnp.float32
    )
    context_grad_two = lax.dot_general(
        branch_grad_two, cross_out, contract_cols, preferred_element_type=jnp.float32
    ).astype(jnp.bfloat16)
    query_grad_two, key_grad_two, value_grad_two = attend_backward(
        query_two, kv_two[0], kv_two[1], mem_len, False, total_two, context_grad_two
    )
    cross_query_grad = lax.dot_general(
        normed_one_all, query_grad_two, contract_rows, preferred_element_type=jnp.float32
    )
    cross_kv_grad = jnp.einsum(
        "td,ite->ide",
        memory_all,
        jnp.stack([key_grad_two, value_grad_two]),
        preferred_element_type=jnp.float32,
    )
    memory_grad = scatter_inputs(
        ((key_grad_two, cross_kv[0]), (value_grad_two, cross_kv[1])), row_count
    )
    normed_one_grad = alpha_res * grad_sum_two + scatter_inputs(
        ((query_grad_two, cross_query),), row_count
    )
    grad_sum_one, gain_one, bias_one = norm_back_one(normed_one_grad)
    branch_grad_one = gather_grads(grad_sum_one.astype(jnp.bfloat16))
    self_out_grad = lax.dot_general(
        context_one, branch_grad_one, contract_rows, preferred_element_type=jnp.float32
    )
    context_grad_one = lax.dot_general(
        branch_grad_one, self_out, contract_cols, preferred_element_type=jnp.float32
    ).astype(jnp.bfloat16)
    query_grad_one, key_grad_one, value_grad_one = attend_backward(
        qkv_rows[0], qkv_rows[1], qkv_rows[2], full_lens, True, total_one, context_grad_one
    )
    self_qkv_grad = jnp.einsum(
        "td,ite->ide",
        target_all,
        jnp.stack([query_grad_one, key_grad_one, value_grad_one]),
        preferred_element_type=jnp.float32,
    )
    target_grad = alpha_res * grad_sum_one + scatter_inputs(
        ((query_grad_one, self_qkv[0]), (key_grad_one, self_qkv[1]), (value_grad_one, self_qkv[2])),
        row_count,
    )
    (
        self_qkv_total,
        self_out_total,
        cross_query_total,
        cross_kv_total,
        cross_out_total,
        up_total,
        down_total,
    ) = (
        lax.psum(self_qkv_grad.astype(jnp.bfloat16), "dp").astype(jnp.float32),
        lax.psum(self_out_grad.astype(jnp.bfloat16), "dp").astype(jnp.float32),
        lax.psum(cross_query_grad.astype(jnp.bfloat16), "dp").astype(jnp.float32),
        lax.psum(cross_kv_grad.astype(jnp.bfloat16), "dp").astype(jnp.float32),
        lax.psum(cross_out_grad.astype(jnp.bfloat16), "dp").astype(jnp.float32),
        lax.psum(up_grad.astype(jnp.bfloat16), "dp").astype(jnp.float32),
        lax.psum(down_grad.astype(jnp.bfloat16), "dp").astype(jnp.float32),
    )
    gain_total, bias_total = lax.psum(
        (jnp.stack([gain_one, gain_two, gain_three]), jnp.stack([bias_one, bias_two, bias_three])),
        ("dp", "tensor"),
    )
    return (
        result.astype(jnp.bfloat16),
        target_grad.astype(jnp.bfloat16),
        memory_grad.astype(jnp.bfloat16),
        self_qkv_total,
        self_out_total,
        cross_query_total,
        cross_kv_total,
        cross_out_total,
        up_total,
        down_total,
        gain_total,
        bias_total,
    )


BLK = 256
f32 = jnp.float32
bf16 = jnp.bfloat16
NN = (((1,), (0,)), ((), ()))
NT = (((1,), (1,)), ((), ()))
TN = (((0,), (0,)), ((), ()))


def dot(a, b, dims=NN):
    return lax.dot_general(a, b, dims, preferred_element_type=f32)


def lanes(rows):
    return lax.broadcasted_iota(jnp.int32, (rows, 128), 1)


def place3(x, rows):
    hi = x.astype(bf16)
    rest = x - hi.astype(f32)
    mid = rest.astype(bf16)
    lo = (rest - mid.astype(f32)).astype(bf16)
    at = lanes(rows) % 64
    return jnp.where(at == 0, hi, jnp.where(at == 1, mid, jnp.where(at == 2, lo, jnp.zeros_like(hi))))


def fwd_kernel(causal, len_ref, q_ref, k_ref, v_ref, c_ref, lse_ref, kaug, vaug):
    k2, v2 = k_ref[...], v_ref[...]
    seq = k2.shape[0]
    lane = lanes(seq)
    zero = jnp.zeros_like(k2)
    if not causal:
        pos = lax.broadcasted_iota(jnp.int32, (seq, 128), 0)
        bias = jnp.where((pos >= len_ref[0]) & (lane == 0), -1e30, 0.0).astype(bf16)
    for h in range(2):
        own = (lane // 64) == h
        kaug[h, :, :128] = jnp.where(own, k2, zero)
        if not causal:
            kaug[h, :, 128:] = bias
        vaug[h, :, :128] = jnp.where(own, v2, zero)
        vaug[h, :, 128:] = jnp.where(own, jnp.ones_like(v2), zero)
    lb = lanes(BLK)
    for i in range(seq // BLK):
        rows = slice(i * BLK, (i + 1) * BLK)
        q = q_ref[rows, :] * jnp.asarray(HD**-0.5, bf16)
        if not causal:
            q = jnp.concatenate([q, jnp.where(lb == 0, 1.0, 0.0).astype(bf16)], axis=1)
        nk = (i + 1) * BLK if causal else seq
        acc = None
        ms = []
        for h in range(2):
            s = dot(q, kaug[h, :nk, :128] if causal else kaug[h], NT)
            if causal:
                a = lax.broadcasted_iota(jnp.int32, (BLK, BLK), 0)
                b = lax.broadcasted_iota(jnp.int32, (BLK, BLK), 1)
                d = jnp.where(b <= a, s[:, nk - BLK :], mask_fill)
                s = d if nk == BLK else jnp.concatenate([s[:, : nk - BLK], d], axis=1)
            m = jnp.max(s, axis=1, keepdims=True)
            p = jnp.exp(s - m).astype(bf16)
            o = dot(p, vaug[h, :nk])
            acc = o if acc is None else acc + o
            ms.append(m)
        total = acc[:, 128:]
        c_ref[rows, :] = (acc[:, :128] / total).astype(bf16)
        lse_ref[rows, :] = place3(-(jnp.where(lb < 64, ms[0], ms[1]) + jnp.log(total)), BLK)


def cost(matmuls, blocks, seq, causal):
    area = seq * seq * blocks * 2 * (0.625 if causal else 1)
    return pl.CostEstimate(
        flops=int(matmuls * area * 2 * 256), bytes_accessed=16 * seq * 128 * blocks, transcendentals=int(area)
    )


def attend_fwd(q, k, v, length, causal):
    seq, width = q.shape
    spec = pl.BlockSpec((seq, 128), lambda i: (0, i))
    return pl.pallas_call(
        functools.partial(fwd_kernel, causal),
        grid=(width // 128,),
        in_specs=[pl.BlockSpec(memory_space=pltpu.SMEM)] + [spec] * 3,
        out_specs=[spec] * 2,
        out_shape=[jax.ShapeDtypeStruct((seq, width), bf16)] * 2,
        scratch_shapes=[pltpu.VMEM((2, seq, 256), bf16)] * 2,
        compiler_params=pltpu.CompilerParams(vmem_limit_bytes=48 * 2**20),
        cost_estimate=cost(2, width // 128, seq, causal),
        name="attend_causal" if causal else "attend_memory",
    )(length, q, k, v)


def back_scratch(seq):
    vmem = pltpu.VMEM
    return [
        vmem((seq, 256), bf16),
        vmem((2, seq, 128), bf16),
        vmem((2, seq, 256), bf16),
        vmem((seq, 256), bf16),
        vmem((2, seq, 128), bf16),
        vmem((2, seq, 256), bf16),
        vmem((128, seq), f32),
        vmem((2, 128, seq), bf16),
    ]


def back_pair(causal, length, q2, k2, v2, c2, aug, g2, grads, member, scratch, tick):
    qs, qm, ka, gs, gm, va, dqa, kt = scratch
    seq = k2.shape[0]
    lane = lanes(seq)
    l64 = lane % 64
    zero = jnp.zeros_like(k2)
    one = jnp.ones_like(k2)
    scale = jnp.asarray(HD**-0.5, bf16)
    prod = c2.astype(f32) * g2.astype(f32)
    d0 = jnp.sum(jnp.where(lane < 64, prod, 0.0), axis=1, keepdims=True)
    d1 = jnp.sum(jnp.where(lane < 64, 0.0, prod), axis=1, keepdims=True)
    qs[:, :128] = q2 * scale
    if not causal:
        aug = jnp.where(l64 == 3, one, aug)
        pos = lax.broadcasted_iota(jnp.int32, (seq, 128), 0)
        bias = jnp.where(pos >= length, -1e30, 0.0).astype(bf16)
    qs[:, 128:] = aug
    gs[:, :128] = g2
    gs[:, 128:] = place3(-jnp.where(lane < 64, d0, d1), seq)
    for h in range(2):
        own = (lane // 64) == h
        sel = own & (l64 < 3)
        qm[h] = jnp.where(own, q2 * scale, zero)
        gm[h] = jnp.where(own, g2, zero)
        ka[h, :, :128] = jnp.where(own, k2, zero)
        ko = jnp.where(sel, one, zero)
        if not causal:
            ko = jnp.where(own & (l64 == 3), bias, ko)
        ka[h, :, 128:] = ko
        va[h, :, :128] = jnp.where(own, v2, zero)
        va[h, :, 128:] = jnp.where(sel, one, zero)
        kt[h] = ka[h, :, :128].T
    dqa[...] = jnp.zeros_like(dqa)
    grads[:, member(3)] = c2
    for j in range(seq // BLK):
        rows = slice(j * BLK, (j + 1) * BLK)
        q0 = j * BLK if causal else 0
        dk = None
        dv = None
        dq = None
        for h in range(2):
            p = jnp.exp(dot(ka[h, rows, :], qs[q0:, :], NT))
            if causal:
                a = lax.broadcasted_iota(jnp.int32, (BLK, BLK), 0)
                b = lax.broadcasted_iota(jnp.int32, (BLK, BLK), 1)
                d = jnp.where(a <= b, p[:, :BLK], 0.0)
                p = d if q0 + BLK == seq else jnp.concatenate([d, p[:, BLK:]], axis=1)
            dp = dot(va[h, rows, :], gs[q0:, :], NT)
            ds = (p * dp).astype(bf16)
            p = p.astype(bf16)
            a = dot(p, gm[h, q0:, :])
            b = dot(ds, qm[h, q0:, :])
            c = dot(kt[h, :, rows], ds)
            dv = a if dv is None else dv + a
            dk = b if dk is None else dk + b
            dq = c if dq is None else dq + c
        dqa[:, q0:] += dq
        grads[rows, member(1)] = dk.astype(bf16)
        grads[rows, member(2)] = dv.astype(bf16)
        tick(j)
    grads[:, member(0)] = (dqa[...] * HD**-0.5).T.astype(bf16)


BOTH = (0, 1)
X, CORE, Y, Z1, Z2 = range(5)
DELAY = 2
SLOTS = 2 * DELAY
CHUNK = 64
SUBS = 4
QUADS = 4
WIDTH = 512
LEAD = 5
LINKS = (CORE, X, Y, Z1, Z2, Y, CORE, CORE)
CHUNKS = 4 * QUADS * SUBS
TICKS = CHUNKS + LEAD + 7 * DELAY
STEPS = 2 * QUADS
FEED_TICKS, CROSS_TICKS, SELF_TICKS, NORM_TICKS = 2, 3, 2, 4
CROSS_AT = STEPS * FEED_TICKS + NORM_TICKS
SELF_AT = CROSS_AT + STEPS * CROSS_TICKS + NORM_TICKS
DRAIN_AT = SELF_AT + STEPS * SELF_TICKS
TILE = 256
NORM_TILE = 128
dma_sem = pltpu.SemaphoreType.DMA


def partner(bit):
    d = lax.axis_index("dp")
    t = lax.axis_index("tensor")
    if bit == 0:
        return (d, 1 - t)
    size = 2 ** (bit - 1)
    return (d + size * (1 - 2 * ((d // size) % 2)), t)


def greet():
    barrier = pltpu.get_barrier_semaphore()
    for bit in range(5):
        pl.semaphore_signal(barrier, inc=1, device_id=partner(bit), device_id_type=pl.DeviceIdType.MESH)
    pl.semaphore_wait(barrier, 5)


def remote_copy(src, dst, send, recv, bit):
    return pltpu.make_async_remote_copy(
        src_ref=src,
        dst_ref=dst,
        send_sem=send,
        recv_sem=recv,
        device_id=partner(bit),
        device_id_type=pl.DeviceIdType.MESH,
    )


def stream_scratch():
    return [
        pltpu.VMEM((2, SLOTS, 2, 2, CHUNK, WIDTH), bf16),
        pltpu.VMEM((3, SLOTS, 2, CHUNK, WIDTH), bf16),
        pltpu.VMEM((6, SLOTS, CHUNK, WIDTH), bf16),
        dma_sem((8, SLOTS)),
        dma_sem((8, SLOTS)),
        dma_sem((2, SLOTS)),
    ]


def stream_stage(stage, c, queue, out, pairs, wide, narrow, send, recv, local):
    d = lax.axis_index("dp")
    core = d % 2
    y = (d // 2) % 2
    slot = lax.rem(c, SLOTS)
    block = c // SUBS
    sub = lax.rem(c, SUBS)
    away, came, own = [wide.at[i, slot] for i in range(3)]
    got_y, s3, got_z, s4, got_zz, s5 = [narrow.at[i, slot] for i in range(6)]

    def remote(k):
        src, dst = (
            (queue.at[block, :, 1 - core, :, sub], pairs.at[0, slot]),
            (away, came),
            (own.at[1 - y], got_y),
            (s3, got_z),
            (s4, got_zz),
            (s5, out.at[block, core, y, sub]),
            (s5, out.at[block, core, y, sub]),
            (out.at[block, core, 1 - y, sub], out.at[block, core, 1 - y, sub]),
        )[k]
        return remote_copy(src, dst, send.at[k, slot], recv.at[k, slot], LINKS[k])

    def load():
        return pltpu.make_async_copy(queue.at[block, :, core, :, sub], pairs.at[1, slot], local.at[0, slot])

    def keep():
        return pltpu.make_async_copy(s5, out.at[block, core, y, sub], local.at[1, slot])

    if stage == 0:
        remote(0).start()
        load().start()
    elif stage == 1:
        remote(0).wait()
        load().wait()
        away[...] = pairs[1, slot, 1] + pairs[0, slot, 1]
        remote(1).start()
        own[...] = pairs[1, slot, 0] + pairs[0, slot, 0]
    elif stage == 2:
        remote(1).wait()
        own[...] = own[...] + came[...]
        remote(2).start()
    elif stage == 3:
        remote(2).wait()
        s3[...] = wide[2, slot, y] + got_y[...]
        remote(3).start()
    elif stage == 4:
        remote(3).wait()
        s4[...] = s3[...] + got_z[...]
        remote(4).start()
    elif stage == 5:
        remote(4).wait()
        s5[...] = s4[...] + got_zz[...]
        remote(5).start()
        remote(6).start()
        keep().start()
    elif stage == 6:
        remote(5).wait()
        remote(6).wait()
        keep().wait()
        remote(7).start()
    else:
        remote(7).wait()


def small_scratch(shape):
    return [pltpu.VMEM((6,) + shape, f32), pltpu.VMEM((5,) + shape, f32), dma_sem((5,)), dma_sem((5,))]


def small_stage(k, out, acc, got, send, recv):
    def remote(i):
        return remote_copy(acc.at[i], got.at[i], send.at[i], recv.at[i], i)

    if k > 0:
        remote(k - 1).wait()
        acc[k] = acc[k - 1] + got[k - 1]
    if k < 5:
        remote(k).start()
    else:
        out[...] = acc[5]


def norm_step(index, more, weights, gain_ref, sum_ref, total, dc, left, acc, zt, sems, tick):
    def fetch_tile(a):
        slot = lax.rem(a, 2)
        rows = pl.ds(pl.multiple_of(a * NORM_TILE, NORM_TILE), NORM_TILE)
        return pltpu.make_async_copy(sum_ref.at[rows], zt.at[slot], sems.at[slot])

    tiles = total.shape[0] // NORM_TILE
    fetch_tile(0).start()

    @pl.loop(0, tiles)
    def _(a):
        rows = pl.ds(pl.multiple_of(a * NORM_TILE, NORM_TILE), NORM_TILE)
        fetch_tile(a).wait()

        @pl.when(a + 1 < tiles)
        def _():
            fetch_tile(a + 1).start()

        z = zt[lax.rem(a, 2)]
        dh = total[rows, :]
        for x, w in more:
            dh = dh + dot(x[rows, :], w[...], NT)
        centered = z - jnp.mean(z, axis=1, keepdims=True)
        r = lax.rsqrt(jnp.mean(centered * centered, axis=1, keepdims=True) + norm_eps)
        n = centered * r
        acc[0, index : index + 1, :] = acc[0, index : index + 1, :] + jnp.sum(dh * n, axis=0, keepdims=True)
        acc[0, 3 + index : 4 + index, :] = acc[0, 3 + index : 4 + index, :] + jnp.sum(dh, axis=0, keepdims=True)
        e = dh * gain_ref[index : index + 1, :]
        dz = r * (e - jnp.mean(e, axis=1, keepdims=True) - n * jnp.mean(e * n, axis=1, keepdims=True))
        total[rows, :] = alpha_res * dz
        g = dz.astype(bf16)
        left[:, rows] = g.T
        for i in BOTH:
            dc[i, rows, :] = dot(g, weights[i][...], NT).astype(bf16)
        pl.when(lax.rem(a, 2) == 1)(lambda: tick(a // 2))


def back_kernel(*refs):
    refs = list(refs)
    take = lambda n: [refs.pop(0) for _ in range(n)]
    (len_ref,) = take(1)
    cross_in = [take(5) for _ in BOTH]
    self_in = [take(5) for _ in BOTH]
    co = take(2)
    gain_ref, small_ref = take(2)
    feed_in = [take(4) for _ in BOTH]
    g3_ref, g3t_ref, h2t_ref, h1t_ref, memt_ref, tart_ref, base_ref, sum2_ref, sum1_ref = take(9)
    cq_in, so_in, kv_in, qkv_in = take(2), take(2), take(2), take(2)
    dmem_ref, dtar_ref, out, queue, small_out = take(5)
    grads, *scratch = take(9)
    stream = [queue, out] + take(6)
    small_refs = [small_out] + take(4)
    acc = small_refs[1]
    lefts, tall, flat, total, ends, dc, zt, staged = take(8)
    left_sems, feed_sems, zt_sems, staged_sems, base_sem = take(5)
    step = pl.program_id(0)
    half = lax.rem(step, 2)
    pair = lax.rem(step // 2, QUADS)

    def tick(t):
        for stage in range(7, -1, -1):
            c = t - LEAD - DELAY * stage
            pl.when((c >= 0) & (c < CHUNKS))(functools.partial(stream_stage, stage, c, *stream))

    def load_left(i, ref):
        return pltpu.make_async_copy(ref, lefts.at[i], left_sems.at[i])

    def load_feed(i, j):
        cols_j = pl.ds(pl.multiple_of(j * WIDTH, WIDTH), WIDTH)
        act, slope, up, down = feed_in[i]
        return [
            pltpu.make_async_copy(act.at[:, cols_j], tall.at[0, i], feed_sems.at[0, i]),
            pltpu.make_async_copy(slope.at[:, cols_j], tall.at[1, i], feed_sems.at[1, i]),
            pltpu.make_async_copy(up.at[:, cols_j], tall.at[2, i], feed_sems.at[2, i]),
            pltpu.make_async_copy(down.at[cols_j], flat.at[i], feed_sems.at[3, i]),
        ]

    def load_late():
        return [
            copy
            for i in BOTH
            for copy in (
                pltpu.make_async_copy(kv_in[i].at[0], tall.at[0, i], feed_sems.at[0, i]),
                pltpu.make_async_copy(kv_in[i].at[1], tall.at[1, i], feed_sems.at[1, i]),
                pltpu.make_async_copy(cq_in[i], tall.at[2, i], feed_sems.at[2, i]),
                pltpu.make_async_copy(so_in[i], flat.at[i], feed_sems.at[3, i]),
            )
        ]

    def load_last():
        return [pltpu.make_async_copy(qkv_in[i].at[m], tall.at[m, i], feed_sems.at[m, i]) for i in BOTH for m in range(3)]

    def input_grad(rows, members, start):
        for m in range(members):
            for i in BOTH:
                term = dot(ends[m, i, rows, :], tall[m, i], NT)
                start = term if start is None else start + term
        lefts[1, rows, :] = start.astype(bf16)

    def send_grad(ref):
        return pltpu.make_async_copy(lefts.at[1], ref, base_sem)

    def post(slot, block, i):
        return pltpu.make_async_copy(staged.at[slot], queue.at[block, i], staged_sems.at[slot])

    def posted():
        for slot in range(2):
            post(slot, 0, 0).wait()

    def feed_product(slot, block, left, right):
        result = dot(lefts[left], right[:, :WIDTH])
        staged[slot] = result.astype(bf16).reshape(2, 2, SUBS, CHUNK, WIDTH)
        post(slot, block, half).start()

    def pair_products(block, spans):
        for left, first, last in spans:
            result = dot(lefts[left], grads[:, 256 * first : 256 * last]).astype(bf16)
            for m in range(first, last):
                for i in BOTH:
                    at = 256 * (m - first) + 128 * i
                    piece = result[:, at : at + 128].reshape(2, 2, SUBS, CHUNK, 128)
                    staged[i, :, :, :, :, 128 * m : 128 * (m + 1)] = piece
        for i in BOTH:
            post(i, block, i).start()

    @pl.when(step == 0)
    def _():
        for copy in load_feed(0, 0) + [load_left(i, r) for i, r in enumerate((g3t_ref, h2t_ref, g3_ref))]:
            copy.start()
        base = pltpu.make_async_copy(base_ref, total, base_sem)
        base.start()
        acc[0] = small_ref[...]
        greet()
        for copy in [load_left(i, r) for i, r in enumerate((g3t_ref, h2t_ref, g3_ref))]:
            copy.wait()
        base.wait()

    @pl.when(step < STEPS)
    def _():
        t = step * FEED_TICKS
        for i in BOTH:

            @pl.when(half == i)
            def _(i=i):
                for copy in load_feed(i, pair):
                    copy.wait()

                @pl.when(step < STEPS - 1)
                def _():
                    for copy in load_feed(1 - i, pair + i):
                        copy.start()

        du = dot(lefts[2], flat[half], NT) * tall[1, half].astype(f32)
        grads[:, :WIDTH] = du.astype(bf16)
        @pl.when(step > 0)
        def _():
            post(0, 0, 0).wait()

        feed_product(0, 2 * pair, 0, tall.at[0, half])
        tick(t)
        for a in range(2):
            rows = slice(2 * a * TILE, 2 * (a + 1) * TILE)
            total[rows, :] += dot(grads[rows, :WIDTH], tall[2, half], NT)

        @pl.when(step > 0)
        def _():
            post(1, 0, 0).wait()

        feed_product(1, 2 * pair + 1, 1, grads)
        tick(t + 1)

    @pl.when(step == STEPS)
    def _():
        fetch = [load_left(0, h1t_ref), load_left(1, memt_ref)]
        for copy in fetch + load_late():
            copy.start()
        norm_step(
            1, [], co, gain_ref, sum2_ref, total, dc, lefts.at[2], acc, zt, zt_sems, lambda k: tick(STEPS * FEED_TICKS + k)
        )
        for copy in fetch:
            copy.wait()
        posted()

    at = pl.ds(pl.multiple_of(pair * 128, 128), 128)

    def member(m):
        return pl.ds(pl.multiple_of(256 * m + 128 * half, 128), 128)


    @pl.when((step >= STEPS) & (step < 2 * STEPS))
    def _():
        t = CROSS_AT + (step - STEPS) * CROSS_TICKS
        q2, k2, v2, c2, aug = [jnp.where(half == 0, a[...], b[...]) for a, b in zip(*cross_in)]

        def ticks(j):
            if j % 2 == 1:
                tick(t + j // 2)

        back_pair(False, len_ref[0], q2, k2, v2, c2, aug, dc[half, :, at], grads, member, scratch, ticks)
        for m, k in ((0, 2), (1, 0), (2, 1)):
            ends[k, half, :, at] = grads[:, member(m)]

        @pl.when((half == 0) & (step > STEPS))
        def _():
            posted()

        @pl.when(half == 1)
        def _():
            pair_products(2 * QUADS + pair, ((0, 0, 1), (1, 1, 3), (2, 3, 4)))

        tick(t + 2)

    @pl.when(step == 2 * STEPS)
    def _():
        fetch = load_left(0, tart_ref)
        fetch.start()
        for copy in load_late():
            copy.wait()
        more = [(ends.at[2, i], tall.at[2, i]) for i in BOTH]
        so = [flat.at[i] for i in BOTH]
        norm_step(
            0, more, so, gain_ref, sum1_ref, total, dc, lefts.at[2], acc, zt, zt_sems, lambda k: tick(SELF_AT - NORM_TICKS + k)
        )
        fetch.wait()

        @pl.loop(0, 4)
        def _(a):
            input_grad(pl.ds(pl.multiple_of(a * TILE, TILE), TILE), 2, None)

        send_grad(dmem_ref).start()
        for copy in load_last():
            copy.start()

    @pl.when(step >= 2 * STEPS)
    def _():
        t = SELF_AT + (step - 2 * STEPS) * SELF_TICKS
        q2, k2, v2, c2, aug = [jnp.where(half == 0, a[...], b[...]) for a, b in zip(*self_in)]
        def ticks(j):
            if j == 0:
                tick(t)

        back_pair(True, 0, q2, k2, v2, c2, aug, dc[half, :, at], grads, member, scratch, ticks)
        for m in range(3):
            ends[m, half, :, at] = grads[:, member(m)]

        @pl.when(half == 0)
        def _():
            posted()

        @pl.when(half == 1)
        def _():
            pair_products(3 * QUADS + pair, ((0, 0, 3), (2, 3, 4)))

        tick(t + 1)
        for k in range(5, -1, -1):
            pl.when(step == 2 * STEPS + 1 + k)(functools.partial(small_stage, k, *small_refs))

    @pl.when(step == 3 * STEPS - 1)
    def _():
        posted()
        send_grad(dmem_ref).wait()
        for copy in load_last():
            copy.wait()

        @pl.loop(0, 4)
        def _(a):
            tick(DRAIN_AT + a)
            rows = pl.ds(pl.multiple_of(a * TILE, TILE), TILE)
            input_grad(rows, 3, total[rows, :])

        send_grad(dtar_ref).start()
        pl.loop(DRAIN_AT + 4, TICKS)(tick)
        send_grad(dtar_ref).wait()


def layer_back(length, cross_in, self_in, weights, gain, small, feed_in, rest):
    seq, width = cross_in[0][0].shape
    model = gain.shape[1]
    early = lambda s: jnp.clip(s - STEPS, 0, STEPS - 1)
    late = lambda s: jnp.clip(s - 2 * STEPS, 0, STEPS - 1)
    cross_spec = pl.BlockSpec((seq, 128), lambda s: (0, early(s) // 2))
    self_spec = pl.BlockSpec((seq, 128), lambda s: (0, late(s) // 2))
    anywhere = pl.BlockSpec(memory_space=pl.ANY)
    full = lambda x: pl.BlockSpec(x.shape, lambda s: (0, 0), pipeline_mode=pl.Buffered(1))
    shape = jax.ShapeDtypeStruct
    vmem = pltpu.VMEM
    blocks = 4 * QUADS
    return pl.pallas_call(
        back_kernel,
        grid=(3 * STEPS,),
        in_specs=[pl.BlockSpec(memory_space=pltpu.SMEM)]
        + [cross_spec] * 10
        + [self_spec] * 10
        + [full(x) for x in (*weights, gain, small)]
        + [anywhere] * 25,
        out_specs=[anywhere] * 4 + [full(small)],
        out_shape=[shape((seq, model), bf16)] * 2
        + [
            shape((blocks, 2, 2, SUBS, CHUNK, WIDTH), bf16),
            shape((blocks, 2, 2, 2, SUBS, CHUNK, WIDTH), bf16),
            shape(small.shape, f32),
        ],
        scratch_shapes=[vmem((seq, 2 * WIDTH), bf16)]
        + back_scratch(seq)
        + stream_scratch()
        + small_scratch(small.shape)
        + [
            vmem((3, model, seq), bf16),
            vmem((3, 2, seq, WIDTH), bf16),
            vmem((2, WIDTH, model), bf16),
            vmem((seq, model), f32),
            vmem((3, 2, seq, width), bf16),
            vmem((2, seq, width), bf16),
            vmem((2, NORM_TILE, model), f32),
            vmem((2, 2, 2, SUBS, CHUNK, WIDTH), bf16),
            dma_sem((3,)),
            dma_sem((4, 2)),
            dma_sem((2,)),
            dma_sem((2,)),
            dma_sem,
        ],
        compiler_params=pltpu.CompilerParams(
            collective_id=1, has_side_effects=True, vmem_limit_bytes=62 * 2**20
        ),
        cost_estimate=cost(16, 8, seq, False),
        name="layer_back",
    )(length, *cross_in[0], *cross_in[1], *self_in[0], *self_in[1], *weights, gain, small, *feed_in[0], *feed_in[1], *rest)


ALL = ("dp", "tensor")
DEVICES = 32


def swap(x, flip):
    return lax.ppermute(x, ALL, [(i, i ^ flip) for i in range(DEVICES)])


def swap_tensor(x):
    return swap(x, 1)


def swap_core(x):
    return swap(x, 2)


def swap_y(x):
    return swap(x, 4)


def my_block():
    d = lax.axis_index("dp")
    return 2 * (d % 2) + (d // 2) % 2


def add_low(*terms):
    return sum(t.astype(f32) for t in terms).astype(bf16)


def blocks_of(own, axis):
    size = own.shape[axis] // 4
    return [lax.dynamic_slice_in_dim(own, (my_block() ^ j) * size, size, axis) for j in range(4)]


def swap_pieces(x, move):
    return [move(p) for p in x] if isinstance(x, (list, tuple)) else move(x)


def tie(*xs):
    return lax.optimization_barrier(xs)


class Pipe:
    def __init__(self):
        self.live = []

    def put(self, gen):
        wait, arrays = next(gen)
        self.live.append([gen, wait, arrays])

    def step(self, due, landed):
        done = 0
        for item in due:
            arrays = landed[done : done + len(item[2])]
            done += len(item[2])
            try:
                item[1], item[2] = item[0].send(arrays)
            except StopIteration:
                self.live.remove(item)

    def cut(self, *xs):
        due = []
        for item in self.live:
            item[1] -= 1
            if item[1] <= 0:
                due.append(item)
        tied = tie(*xs, *[a for item in due for a in item[2]])
        self.step(due, tied[len(xs) :])
        return tied[: len(xs)] if len(xs) > 1 else tied[0]

    def drain(self):
        while self.live:
            self.step(list(self.live), [a for item in self.live for a in item[2]])


def fetch(out, key, block, waits):
    far = swap_tensor(block)
    (far,) = yield waits[0], [far]
    side = swap_y(far)
    near = swap_core(far)
    side, near = yield waits[1], [side, near]
    out[key] = [far, side, near, swap_core(side)]
    return


def ffn_kernel(h_ref, up_ref, down_ref, a_ref, d_ref, b_ref):
    h = h_ref[...]
    size = 512
    total = None
    for j in range(4):
        cols = slice(j * size, (j + 1) * size)
        u = dot(h, up_ref[:, cols])
        cdf = 0.5 + 0.5 * lax.erf(u * (0.5**0.5))
        slope = cdf + u * (jnp.exp(-0.5 * u * u) * 0.3989422804014327)
        act = (u * cdf).astype(bf16)
        a_ref[:, cols] = act
        d_ref[:, cols] = slope.astype(bf16)
        term = dot(act, down_ref[cols, :])
        total = term if total is None else total + term
    b_ref[...] = total


def whole(x):
    return pl.BlockSpec(x.shape, lambda r: (0, 0))


ROWS = 512


def ffn_forward(h, up, down):
    seq, width = h.shape
    units = up.shape[1]
    rows = lambda w: pl.BlockSpec((ROWS, w), lambda r: (r, 0))
    return pl.pallas_call(
        ffn_kernel,
        grid=(seq // ROWS,),
        in_specs=[rows(width)] + [whole(up), whole(down)],
        out_specs=[rows(units), rows(units), rows(width)],
        out_shape=[jax.ShapeDtypeStruct((seq, units), bf16)] * 2 + [jax.ShapeDtypeStruct((seq, width), f32)],
        compiler_params=pltpu.CompilerParams(vmem_limit_bytes=50 * 2**20),
        cost_estimate=pl.CostEstimate(flops=4 * seq * width * units, bytes_accessed=22 * 2**20, transcendentals=2 * seq * units),
        name="feed_forward",
    )(h, up, down)


def arrange_kernel(me_ref, *refs):
    for j in range(4):

        @pl.when(pl.program_id(0) == j)
        def _(j=j):
            refs[4][...] = refs[j][...]


def arrange(slabs):
    members, rows, width = slabs[0].shape
    return pl.pallas_call(
        arrange_kernel,
        grid_spec=pltpu.PrefetchScalarGridSpec(
            num_scalar_prefetch=1,
            grid=(4,),
            in_specs=[pl.BlockSpec((members, rows, width), lambda j, me: (0, 0, 0))] * 4,
            out_specs=pl.BlockSpec((members, rows, width), lambda j, me: (0, j ^ me[0], 0)),
        ),
        out_shape=jax.ShapeDtypeStruct((members, 4 * rows, width), bf16),
        compiler_params=pltpu.CompilerParams(vmem_limit_bytes=40 * 2**20),
        cost_estimate=pl.CostEstimate(flops=0, bytes_accessed=16 * members * rows * width, transcendentals=0),
        name="arrange",
    )(my_block().reshape(1), *slabs)


def slab_of(own):
    rows = own.shape[1] // 4
    return lax.dynamic_slice_in_dim(own, my_block() * rows, rows, 1)


def spread_kernel(spans, x_ref, *out_refs):
    for lo, hi, k, m in spans:
        x = x_ref[:, lo:hi].astype(f32)
        if m is None:
            out_refs[k][...] = x.T
        else:
            out_refs[k][m] = x


def spread(pairs, first, spans, outs):
    _, rows, width = pairs.shape
    tile = 512
    specs = []
    shapes = []
    for members in outs:
        if members is None:
            specs.append(pl.BlockSpec((128, tile), lambda p, t: (p, t)))
            shapes.append(jax.ShapeDtypeStruct((512, rows), f32))
        else:
            specs.append(pl.BlockSpec((members, tile, 128), lambda p, t: (0, t, p)))
            shapes.append(jax.ShapeDtypeStruct((members, rows, 512), f32))
    return pl.pallas_call(
        functools.partial(spread_kernel, spans),
        grid=(4, rows // tile),
        in_specs=[pl.BlockSpec((None, tile, width), lambda p, t: (p + first, t, 0))],
        out_specs=specs,
        out_shape=shapes,
        compiler_params=pltpu.CompilerParams(vmem_limit_bytes=40 * 2**20),
        cost_estimate=pl.CostEstimate(flops=0, bytes_accessed=24 * rows * width, transcendentals=0),
        name="spread",
    )(pairs)


def flip_kernel(x_ref, out_ref):
    out_ref[...] = x_ref[...].T


def flip(x):
    rows, width = x.shape
    return pl.pallas_call(
        flip_kernel,
        grid=(4,),
        in_specs=[pl.BlockSpec((rows // 4, width), lambda i: (i, 0))],
        out_specs=pl.BlockSpec((width, rows // 4), lambda i: (0, i)),
        out_shape=jax.ShapeDtypeStruct((width, rows), x.dtype),
        cost_estimate=pl.CostEstimate(flops=0, bytes_accessed=4 * rows * width, transcendentals=0),
        name="flip",
    )(x)


def spread_feed_kernel(x_ref, down_ref, up_ref):
    even = lax.rem(pl.program_id(0), 2) == 0

    @pl.when(even)
    def _():
        down_ref[...] = x_ref[...].astype(f32).T

    @pl.when(jnp.logical_not(even))
    def _():
        up_ref[...] = x_ref[...].astype(f32)


def spread_feed(blocks):
    _, rows, width = blocks.shape
    return pl.pallas_call(
        spread_feed_kernel,
        grid=(8,),
        in_specs=[pl.BlockSpec((None, rows, width), lambda b: (b, 0, 0))],
        out_specs=[
            pl.BlockSpec((width, rows), lambda b: (b // 2, 0)),
            pl.BlockSpec((rows, width), lambda b: (0, b // 2)),
        ],
        out_shape=[jax.ShapeDtypeStruct((4 * width, rows), f32), jax.ShapeDtypeStruct((rows, 4 * width), f32)],
        compiler_params=pltpu.CompilerParams(vmem_limit_bytes=40 * 2**20),
        cost_estimate=pl.CostEstimate(flops=0, bytes_accessed=48 * rows * width, transcendentals=0),
        name="spread_feed",
    )(blocks)


def one_pair_each(
    target,
    memory,
    mem_len,
    grad_out,
    self_qkv,
    self_out,
    cross_query,
    cross_kv,
    cross_out,
    ffn_up,
    ffn_down,
    ln_gain,
    ln_bias,
):
    length = lax.dynamic_slice_in_dim(mem_len, lax.axis_index("tensor"), 1)
    pipe = Pipe()
    got = {}
    so3, cq3, co3 = self_out[None], cross_query[None], cross_out[None]

    pipe.put(fetch(got, "qkv", slab_of(self_qkv), (1, 1)))
    q1 = [[dot(target, self_qkv[m]).astype(bf16) for m in range(3)], None]
    at1 = [attend_fwd(*q1[0], length, True), None]
    so_s, cq_s, kv_s, co_s = [slab_of(x) for x in (so3, cq3, cross_kv, co3)]
    mem, so_s, cq_s, kv_s, _ = pipe.cut(memory, so_s, cq_s, kv_s, at1[0][0])
    pipe.put(fetch(got, "so", so_s, (1, 1)))
    pipe.put(fetch(got, "cq", cq_s, (1, 1)))
    pipe.put(fetch(got, "kv", kv_s, (1, 1)))
    kv = [[dot(mem, cross_kv[m]).astype(bf16) for m in range(2)], None]
    up_s, down_s = slab_of(ffn_up[None]), slab_of(ffn_down[None])
    target_t = flip(target)
    memory_t = flip(mem)
    kv[0][0], up_s, co_s, target_t, memory_t = tie(kv[0][0], up_s, co_s, target_t, memory_t)
    tar, kv[0][0], kv[0][1], target_t, memory_t = pipe.cut(target, *kv[0], target_t, memory_t)
    qkv_oth = arrange(got["qkv"])
    q1[1] = [dot(tar, qkv_oth[m]).astype(bf16) for m in range(3)]
    pipe.put(fetch(got, "co", co_s, (1, 1)))
    q1[1][0], up_s = tie(q1[1][0], up_s)
    pipe.put(fetch(got, "up", up_s, (2, 1)))
    at1[1] = attend_fwd(*q1[1], length, True)
    at1[1], _ = tie(at1[1], at1[1][0])
    c1_oth = pipe.cut(at1[1][0])
    c1 = [at1[0][0], c1_oth]
    so_oth = arrange(got["so"])[0]
    b1 = dot(c1[0], self_out) + dot(c1[1], so_oth)
    sum1 = alpha_res * target.astype(f32) + b1
    h1 = norm_rows(sum1, ln_gain[0], ln_bias[0])
    h1_low = h1.astype(bf16)
    cq_oth = arrange(got["cq"])[0]
    kv_oth = arrange(got["kv"])
    q2 = [dot(h1_low, cross_query).astype(bf16), dot(h1_low, cq_oth).astype(bf16)]
    kv[1] = [dot(memory, kv_oth[m]).astype(bf16) for m in range(2)]
    q2[0], kv[1][0], down_s = pipe.cut(q2[0], kv[1][0], down_s)
    pipe.put(fetch(got, "down", down_s, (1, 1)))
    at2 = [attend_fwd(q2[0], *kv[0], length, False), None]
    h1_again, _ = tie(h1_low, at2[0][0])
    h1_t = flip(h1_again)
    q2[1], h1_t, _ = pipe.cut(q2[1], h1_t, at2[0][0])
    at2[1] = attend_fwd(q2[1], *kv[1], length, False)
    co_oth = arrange(got["co"])[0]
    c2 = [at2[0][0], at2[1][0]]
    c2[1] = pipe.cut(c2[1])
    b2 = dot(c2[0], cross_out) + dot(c2[1], co_oth)
    sum2 = alpha_res * h1 + b2
    h2 = norm_rows(sum2, ln_gain[1], ln_bias[1])
    h2_low = h2.astype(bf16)
    act0, slope0, b3 = ffn_forward(h2_low, ffn_up, ffn_down)
    h2_t = flip(h2_low)
    while "up" not in got or "down" not in got:
        act0 = pipe.cut(act0)
    h2_again, h1_t, h2_t, _ = tie(h2_low, h1_t, h2_t, act0)
    up_oth, down_oth = arrange(got["up"])[0], arrange(got["down"])[0]
    act1, slope1, b3b = ffn_forward(h2_again, up_oth, down_oth)
    result, back3 = jax.vjp(norm_rows, alpha_res * h2 + b3 + b3b, ln_gain[2], ln_bias[2])
    dz3, gain3, bias3 = back3(grad_out.astype(f32))
    g3 = dz3.astype(bf16)
    none = jnp.zeros_like(gain3)
    small = jnp.stack([none, none, gain3, none, none, bias3, none, none])
    dmem, dtar, blocks, _, small = layer_back(
        length,
        [[q2[i], *kv[i], c2[i], at2[i][1]] for i in BOTH],
        [[*q1[i], c1[i], at1[i][1]] for i in BOTH],
        (cross_out, co_oth),
        ln_gain,
        small,
        [(act0, slope0, ffn_up, ffn_down), (act1, slope1, up_oth, down_oth)],
        (g3, flip(g3), h2_t, h1_t, memory_t, target_t, alpha_res * dz3, sum2, sum1)
        + (cross_query, cq_oth, self_out, so_oth, cross_kv, kv_oth, self_qkv, qkv_oth),
    )
    blocks = blocks.reshape(16, 1024, 512)
    cq_total, kv_total, co_total = spread(
        blocks,
        8,
        ((0, 128, 0, 0), (128, 256, 1, 0), (256, 384, 1, 1), (384, 512, 2, None)),
        (1, 2, None),
    )
    qkv_total, so_total = spread(
        blocks,
        12,
        ((0, 128, 0, 0), (128, 256, 0, 1), (256, 384, 0, 2), (384, 512, 1, None)),
        (3, None),
    )
    down_total, up_total = spread_feed(blocks)
    return (
        result.astype(bf16),
        dtar,
        dmem,
        qkv_total,
        so_total,
        cq_total[0],
        kv_total,
        co_total,
        up_total,
        down_total,
        small[:3],
        small[3:6],
    )


def solution(mesh):
    placed = (
        P(("dp", "tensor"), None),
        P(("dp", "tensor"), None),
        P("dp"),
        P(("dp", "tensor"), None),
        P(None, None, "tensor"),
        P("tensor", None),
        P(None, "tensor"),
        P(None, None, "tensor"),
        P("tensor", None),
        P(None, "tensor"),
        P("tensor", None),
        P(),
        P(),
    )
    body = one_pair_each if mesh.shape["tensor"] == 2 and mesh.shape["dp"] == 16 else on_device
    return jax.shard_map(
        body,
        mesh=mesh,
        in_specs=placed,
        out_specs=(
            P(("dp", "tensor"), None),
            P(("dp", "tensor"), None),
            P(("dp", "tensor"), None),
            P(None, None, "tensor"),
            P("tensor", None),
            P(None, "tensor"),
            P(None, None, "tensor"),
            P("tensor", None),
            P(None, "tensor"),
            P("tensor", None),
            P(),
            P(),
        ),
        check_vma=False,
    )
```

```python
import functools

import jax
import jax.numpy as jnp
from jax import lax
from jax.experimental import pallas as pl
from jax.experimental.pallas import tpu as pltpu
from jax.sharding import PartitionSpec as P

HD = 64


alpha_res = 300.0**0.25
norm_eps = 1e-05
mask_fill = -1e30
contract_rows = (((0,), (0,)), ((), ()))
contract_cols = (((1,), (1,)), ((), ()))


def norm_rows(resid, gain_vec, bias_vec):
    average = jnp.mean(resid, axis=-1, keepdims=True)
    centered = resid - average
    variance = jnp.mean(centered * centered, axis=-1, keepdims=True)
    return centered * lax.rsqrt(variance + norm_eps) * gain_vec + bias_vec


def exact_gelu(values_in):
    return jax.nn.gelu(values_in, approximate=False)


def gather_rows(local_rows):
    return lax.all_gather(local_rows, "tensor", axis=0, tiled=True)


def gather_grads(local_rows):
    return lax.all_gather(local_rows, "tensor", axis=0, tiled=True)


def scatter_branch(left_mat, right_mat, row_count):

    def partial_term(offset, num_rows):
        return jnp.dot(left_mat, right_mat, preferred_element_type=jnp.float32)

    return lax.psum_scatter(
        partial_term(jnp.int32(0), row_count * lax.axis_size("tensor")),
        "tensor",
        scatter_dimension=0,
        tiled=True,
    )


def project_context(context, weight_local, row_count):
    return scatter_branch(context, weight_local, row_count)


def scatter_inputs(factor_pairs, row_count):

    def partial_term(offset, num_rows):
        terms = [
            lax.dot_general(grad_mat, weight_mat, contract_cols, preferred_element_type=jnp.float32)
            for grad_mat, weight_mat in factor_pairs
        ]
        return sum(terms)

    return lax.psum_scatter(
        partial_term(jnp.int32(0), row_count * lax.axis_size("tensor")).astype(jnp.bfloat16),
        "tensor",
        scatter_dimension=0,
        tiled=True,
    ).astype(jnp.float32)


def block_view(flat, pair_count, block_rows):
    tok_count, col_count = flat.shape
    seq_len = tok_count // pair_count
    return flat.reshape(pair_count, seq_len // block_rows, block_rows, col_count // HD, HD)


def pair_view(flat, pair_count):
    tok_count, col_count = flat.shape
    return flat.reshape(pair_count, tok_count // pair_count, col_count // HD, HD)


def block_scores(query_blk, key_pair, start_row, key_len, causal):
    block_rows = query_blk.shape[0]
    seq_len = key_pair.shape[0]
    products = jnp.einsum(
        "qhd,khd->hqk", query_blk, key_pair, preferred_element_type=jnp.float32
    ) * HD ** (-0.5)
    key_pos = lax.broadcasted_iota(jnp.int32, (block_rows, seq_len), 1)
    query_pos = start_row + lax.broadcasted_iota(jnp.int32, (block_rows, seq_len), 0)
    allowed = key_pos < key_len
    if causal:
        allowed = allowed & (key_pos <= query_pos)
    return jnp.where(allowed[None], products, mask_fill)


def attend_forward(queries, key_rows, value_rows, key_lens, causal):
    pair_count = key_lens.shape[0]
    seq_len = queries.shape[0] // pair_count
    block_rows = min(512, seq_len)
    starts = lax.iota(jnp.int32, seq_len // block_rows) * block_rows

    def one_pair(packed):
        query_pair, key_pair, value_pair, key_len = packed

        def one_block(inner):
            query_blk, start_row = inner
            scores = block_scores(query_blk, key_pair, start_row, key_len, causal)
            row_max = jnp.max(scores, axis=-1, keepdims=True)
            shifted = jnp.exp(scores - row_max)
            row_total = jnp.sum(shifted, axis=-1, keepdims=True)
            attn_prob = (shifted / row_total).astype(jnp.bfloat16)
            context = jnp.einsum(
                "hqk,khd->qhd", attn_prob, value_pair, preferred_element_type=jnp.float32
            )
            return (context.astype(jnp.bfloat16), (row_max + jnp.log(row_total))[..., 0])

        return lax.map(one_block, (query_pair, starts))

    context, log_total = lax.map(
        one_pair,
        (
            block_view(queries, pair_count, block_rows),
            pair_view(key_rows, pair_count),
            pair_view(value_rows, pair_count),
            key_lens,
        ),
    )
    return (context.reshape(queries.shape), log_total)


def attend_backward(queries, key_rows, value_rows, key_lens, causal, log_total, grad_context):
    pair_count = key_lens.shape[0]
    seq_len = queries.shape[0] // pair_count
    block_rows = min(512, seq_len)
    starts = lax.iota(jnp.int32, seq_len // block_rows) * block_rows
    score_scale = HD ** (-0.5)

    def one_pair(packed):
        query_pair, key_pair, value_pair, key_len, total_pair, grad_pair = packed

        def one_block(carry, inner):
            key_grad, value_grad = carry
            query_blk, start_row, total_blk, grad_blk = inner
            scores = block_scores(query_blk, key_pair, start_row, key_len, causal)
            attn_prob = jnp.exp(scores - total_blk[..., None])
            value_grad = value_grad + jnp.einsum(
                "hqk,qhd->khd",
                attn_prob.astype(jnp.bfloat16),
                grad_blk,
                preferred_element_type=jnp.float32,
            )
            prob_grad = jnp.einsum(
                "qhd,khd->hqk", grad_blk, value_pair, preferred_element_type=jnp.float32
            )
            score_grad = (
                attn_prob * (prob_grad - jnp.sum(attn_prob * prob_grad, axis=-1, keepdims=True))
            ).astype(jnp.bfloat16)
            query_grad = (
                jnp.einsum("hqk,khd->qhd", score_grad, key_pair, preferred_element_type=jnp.float32)
                * score_scale
            )
            key_grad = (
                key_grad
                + jnp.einsum(
                    "hqk,qhd->khd", score_grad, query_blk, preferred_element_type=jnp.float32
                )
                * score_scale
            )
            return ((key_grad, value_grad), query_grad.astype(jnp.bfloat16))

        zeros = jnp.zeros(key_pair.shape, jnp.float32)
        (key_grad, value_grad), query_grad = lax.scan(
            one_block, (zeros, zeros), (query_pair, starts, total_pair, grad_pair)
        )
        return (query_grad, key_grad.astype(jnp.bfloat16), value_grad.astype(jnp.bfloat16))

    query_grad, key_grad, value_grad = lax.map(
        one_pair,
        (
            block_view(queries, pair_count, block_rows),
            pair_view(key_rows, pair_count),
            pair_view(value_rows, pair_count),
            key_lens,
            log_total,
            block_view(grad_context, pair_count, block_rows),
        ),
    )
    return (
        query_grad.reshape(queries.shape),
        key_grad.reshape(queries.shape),
        value_grad.reshape(queries.shape),
    )


def on_device(
    target,
    memory,
    mem_len,
    grad_out,
    self_qkv,
    self_out,
    cross_query,
    cross_kv,
    cross_out,
    ffn_up,
    ffn_down,
    ln_gain,
    ln_bias,
):
    row_count = target.shape[0]
    pair_count = mem_len.shape[0]
    seq_len = row_count * lax.axis_size("tensor") // pair_count
    full_lens = jnp.full((pair_count,), seq_len, jnp.int32)
    target_all = gather_rows(target)
    qkv_rows = jnp.einsum(
        "td,ide->ite", target_all, self_qkv, preferred_element_type=jnp.float32
    ).astype(jnp.bfloat16)
    context_one, total_one = attend_forward(qkv_rows[0], qkv_rows[1], qkv_rows[2], full_lens, True)
    branch_one = project_context(context_one, self_out, row_count)
    normed_one, norm_back_one = jax.vjp(
        norm_rows, alpha_res * target.astype(jnp.float32) + branch_one, ln_gain[0], ln_bias[0]
    )
    normed_one_all = gather_rows(normed_one.astype(jnp.bfloat16))
    memory_all = gather_rows(memory)
    query_two = jnp.dot(normed_one_all, cross_query, preferred_element_type=jnp.float32).astype(
        jnp.bfloat16
    )
    kv_two = jnp.einsum(
        "td,ide->ite", memory_all, cross_kv, preferred_element_type=jnp.float32
    ).astype(jnp.bfloat16)
    context_two, total_two = attend_forward(query_two, kv_two[0], kv_two[1], mem_len, False)
    branch_two = project_context(context_two, cross_out, row_count)
    normed_two, norm_back_two = jax.vjp(
        norm_rows, alpha_res * normed_one + branch_two, ln_gain[1], ln_bias[1]
    )
    normed_two_low = normed_two.astype(jnp.bfloat16)
    normed_two_all = gather_rows(normed_two_low)
    hidden = jnp.dot(normed_two_all, ffn_up, preferred_element_type=jnp.float32)
    activated, gelu_back = jax.vjp(exact_gelu, hidden)
    activated_low = activated.astype(jnp.bfloat16)
    branch_three = scatter_branch(activated_low, ffn_down, row_count)
    result, norm_back_three = jax.vjp(
        norm_rows, alpha_res * normed_two + branch_three, ln_gain[2], ln_bias[2]
    )
    grad_sum_three, gain_three, bias_three = norm_back_three(grad_out.astype(jnp.float32))
    branch_grad_three = gather_grads(grad_sum_three.astype(jnp.bfloat16))
    down_grad = lax.dot_general(
        activated_low, branch_grad_three, contract_rows, preferred_element_type=jnp.float32
    )
    act_grad = lax.dot_general(
        branch_grad_three, ffn_down, contract_cols, preferred_element_type=jnp.float32
    )
    hidden_grad = gelu_back(act_grad)[0].astype(jnp.bfloat16)
    up_grad = lax.dot_general(
        normed_two_all, hidden_grad, contract_rows, preferred_element_type=jnp.float32
    )
    normed_two_grad = alpha_res * grad_sum_three + scatter_inputs(
        ((hidden_grad, ffn_up),), row_count
    )
    grad_sum_two, gain_two, bias_two = norm_back_two(normed_two_grad)
    branch_grad_two = gather_grads(grad_sum_two.astype(jnp.bfloat16))
    cross_out_grad = lax.dot_general(
        context_two, branch_grad_two, contract_rows, preferred_element_type=jnp.float32
    )
    context_grad_two = lax.dot_general(
        branch_grad_two, cross_out, contract_cols, preferred_element_type=jnp.float32
    ).astype(jnp.bfloat16)
    query_grad_two, key_grad_two, value_grad_two = attend_backward(
        query_two, kv_two[0], kv_two[1], mem_len, False, total_two, context_grad_two
    )
    cross_query_grad = lax.dot_general(
        normed_one_all, query_grad_two, contract_rows, preferred_element_type=jnp.float32
    )
    cross_kv_grad = jnp.einsum(
        "td,ite->ide",
        memory_all,
        jnp.stack([key_grad_two, value_grad_two]),
        preferred_element_type=jnp.float32,
    )
    memory_grad = scatter_inputs(
        ((key_grad_two, cross_kv[0]), (value_grad_two, cross_kv[1])), row_count
    )
    normed_one_grad = alpha_res * grad_sum_two + scatter_inputs(
        ((query_grad_two, cross_query),), row_count
    )
    grad_sum_one, gain_one, bias_one = norm_back_one(normed_one_grad)
    branch_grad_one = gather_grads(grad_sum_one.astype(jnp.bfloat16))
    self_out_grad = lax.dot_general(
        context_one, branch_grad_one, contract_rows, preferred_element_type=jnp.float32
    )
    context_grad_one = lax.dot_general(
        branch_grad_one, self_out, contract_cols, preferred_element_type=jnp.float32
    ).astype(jnp.bfloat16)
    query_grad_one, key_grad_one, value_grad_one = attend_backward(
        qkv_rows[0], qkv_rows[1], qkv_rows[2], full_lens, True, total_one, context_grad_one
    )
    self_qkv_grad = jnp.einsum(
        "td,ite->ide",
        target_all,
        jnp.stack([query_grad_one, key_grad_one, value_grad_one]),
        preferred_element_type=jnp.float32,
    )
    target_grad = alpha_res * grad_sum_one + scatter_inputs(
        ((query_grad_one, self_qkv[0]), (key_grad_one, self_qkv[1]), (value_grad_one, self_qkv[2])),
        row_count,
    )
    (
        self_qkv_total,
        self_out_total,
        cross_query_total,
        cross_kv_total,
        cross_out_total,
        up_total,
        down_total,
    ) = (
        lax.psum(self_qkv_grad.astype(jnp.bfloat16), "dp").astype(jnp.float32),
        lax.psum(self_out_grad.astype(jnp.bfloat16), "dp").astype(jnp.float32),
        lax.psum(cross_query_grad.astype(jnp.bfloat16), "dp").astype(jnp.float32),
        lax.psum(cross_kv_grad.astype(jnp.bfloat16), "dp").astype(jnp.float32),
        lax.psum(cross_out_grad.astype(jnp.bfloat16), "dp").astype(jnp.float32),
        lax.psum(up_grad.astype(jnp.bfloat16), "dp").astype(jnp.float32),
        lax.psum(down_grad.astype(jnp.bfloat16), "dp").astype(jnp.float32),
    )
    gain_total, bias_total = lax.psum(
        (jnp.stack([gain_one, gain_two, gain_three]), jnp.stack([bias_one, bias_two, bias_three])),
        ("dp", "tensor"),
    )
    return (
        result.astype(jnp.bfloat16),
        target_grad.astype(jnp.bfloat16),
        memory_grad.astype(jnp.bfloat16),
        self_qkv_total,
        self_out_total,
        cross_query_total,
        cross_kv_total,
        cross_out_total,
        up_total,
        down_total,
        gain_total,
        bias_total,
    )


BLK = 256
f32 = jnp.float32
bf16 = jnp.bfloat16
NN = (((1,), (0,)), ((), ()))
NT = (((1,), (1,)), ((), ()))
TN = (((0,), (0,)), ((), ()))


def dot(a, b, dims=NN):
    return lax.dot_general(a, b, dims, preferred_element_type=f32)


def lanes(rows):
    return lax.broadcasted_iota(jnp.int32, (rows, 128), 1)


def place3(x, rows):
    hi = x.astype(bf16)
    rest = x - hi.astype(f32)
    mid = rest.astype(bf16)
    lo = (rest - mid.astype(f32)).astype(bf16)
    at = lanes(rows) % 64
    return jnp.where(at == 0, hi, jnp.where(at == 1, mid, jnp.where(at == 2, lo, jnp.zeros_like(hi))))


def fwd_kernel(causal, len_ref, q_ref, k_ref, v_ref, c_ref, lse_ref, kaug, vaug):
    k2, v2 = k_ref[...], v_ref[...]
    seq = k2.shape[0]
    lane = lanes(seq)
    zero = jnp.zeros_like(k2)
    if not causal:
        pos = lax.broadcasted_iota(jnp.int32, (seq, 128), 0)
        bias = jnp.where((pos >= len_ref[0]) & (lane == 0), -1e30, 0.0).astype(bf16)
    for h in range(2):
        own = (lane // 64) == h
        kaug[h, :, :128] = jnp.where(own, k2, zero)
        if not causal:
            kaug[h, :, 128:] = bias
        vaug[h, :, :128] = jnp.where(own, v2, zero)
        vaug[h, :, 128:] = jnp.where(own, jnp.ones_like(v2), zero)
    lb = lanes(BLK)
    for i in range(seq // BLK):
        rows = slice(i * BLK, (i + 1) * BLK)
        q = q_ref[rows, :] * jnp.asarray(HD**-0.5, bf16)
        if not causal:
            q = jnp.concatenate([q, jnp.where(lb == 0, 1.0, 0.0).astype(bf16)], axis=1)
        nk = (i + 1) * BLK if causal else seq
        acc = None
        ms = []
        for h in range(2):
            s = dot(q, kaug[h, :nk, :128] if causal else kaug[h], NT)
            if causal:
                a = lax.broadcasted_iota(jnp.int32, (BLK, BLK), 0)
                b = lax.broadcasted_iota(jnp.int32, (BLK, BLK), 1)
                d = jnp.where(b <= a, s[:, nk - BLK :], mask_fill)
                s = d if nk == BLK else jnp.concatenate([s[:, : nk - BLK], d], axis=1)
            m = jnp.max(s, axis=1, keepdims=True)
            p = jnp.exp(s - m).astype(bf16)
            o = dot(p, vaug[h, :nk])
            acc = o if acc is None else acc + o
            ms.append(m)
        total = acc[:, 128:]
        c_ref[rows, :] = (acc[:, :128] / total).astype(bf16)
        lse_ref[rows, :] = place3(-(jnp.where(lb < 64, ms[0], ms[1]) + jnp.log(total)), BLK)


def cost(matmuls, blocks, seq, causal):
    area = seq * seq * blocks * 2 * (0.625 if causal else 1)
    return pl.CostEstimate(
        flops=int(matmuls * area * 2 * 256), bytes_accessed=16 * seq * 128 * blocks, transcendentals=int(area)
    )


def attend_fwd(q, k, v, length, causal):
    seq, width = q.shape
    spec = pl.BlockSpec((seq, 128), lambda i: (0, i))
    return pl.pallas_call(
        functools.partial(fwd_kernel, causal),
        grid=(width // 128,),
        in_specs=[pl.BlockSpec(memory_space=pltpu.SMEM)] + [spec] * 3,
        out_specs=[spec] * 2,
        out_shape=[jax.ShapeDtypeStruct((seq, width), bf16)] * 2,
        scratch_shapes=[pltpu.VMEM((2, seq, 256), bf16)] * 2,
        compiler_params=pltpu.CompilerParams(vmem_limit_bytes=48 * 2**20),
        cost_estimate=cost(2, width // 128, seq, causal),
        name="attend_causal" if causal else "attend_memory",
    )(length, q, k, v)


def back_scratch(seq):
    vmem = pltpu.VMEM
    return [
        vmem((seq, 256), bf16),
        vmem((2, seq, 128), bf16),
        vmem((2, seq, 256), bf16),
        vmem((seq, 256), bf16),
        vmem((2, seq, 128), bf16),
        vmem((2, seq, 256), bf16),
        vmem((128, seq), f32),
        vmem((2, 128, seq), bf16),
    ]


def back_pair(causal, length, q2, k2, v2, c2, aug, g2, grads, member, scratch, tick):
    qs, qm, ka, gs, gm, va, dqa, kt = scratch
    seq = k2.shape[0]
    lane = lanes(seq)
    l64 = lane % 64
    zero = jnp.zeros_like(k2)
    one = jnp.ones_like(k2)
    scale = jnp.asarray(HD**-0.5, bf16)
    prod = c2.astype(f32) * g2.astype(f32)
    d0 = jnp.sum(jnp.where(lane < 64, prod, 0.0), axis=1, keepdims=True)
    d1 = jnp.sum(jnp.where(lane < 64, 0.0, prod), axis=1, keepdims=True)
    qs[:, :128] = q2 * scale
    if not causal:
        aug = jnp.where(l64 == 3, one, aug)
        pos = lax.broadcasted_iota(jnp.int32, (seq, 128), 0)
        bias = jnp.where(pos >= length, -1e30, 0.0).astype(bf16)
    qs[:, 128:] = aug
    gs[:, :128] = g2
    gs[:, 128:] = place3(-jnp.where(lane < 64, d0, d1), seq)
    for h in range(2):
        own = (lane // 64) == h
        sel = own & (l64 < 3)
        qm[h] = jnp.where(own, q2 * scale, zero)
        gm[h] = jnp.where(own, g2, zero)
        ka[h, :, :128] = jnp.where(own, k2, zero)
        ko = jnp.where(sel, one, zero)
        if not causal:
            ko = jnp.where(own & (l64 == 3), bias, ko)
        ka[h, :, 128:] = ko
        va[h, :, :128] = jnp.where(own, v2, zero)
        va[h, :, 128:] = jnp.where(sel, one, zero)
        kt[h] = ka[h, :, :128].T
    dqa[...] = jnp.zeros_like(dqa)
    grads[:, member(3)] = c2
    for j in range(seq // BLK):
        rows = slice(j * BLK, (j + 1) * BLK)
        q0 = j * BLK if causal else 0
        dk = None
        dv = None
        dq = None
        for h in range(2):
            p = jnp.exp(dot(ka[h, rows, :], qs[q0:, :], NT))
            if causal:
                a = lax.broadcasted_iota(jnp.int32, (BLK, BLK), 0)
                b = lax.broadcasted_iota(jnp.int32, (BLK, BLK), 1)
                d = jnp.where(a <= b, p[:, :BLK], 0.0)
                p = d if q0 + BLK == seq else jnp.concatenate([d, p[:, BLK:]], axis=1)
            dp = dot(va[h, rows, :], gs[q0:, :], NT)
            ds = (p * dp).astype(bf16)
            p = p.astype(bf16)
            a = dot(p, gm[h, q0:, :])
            b = dot(ds, qm[h, q0:, :])
            c = dot(kt[h, :, rows], ds)
            dv = a if dv is None else dv + a
            dk = b if dk is None else dk + b
            dq = c if dq is None else dq + c
        dqa[:, q0:] += dq
        grads[rows, member(1)] = dk.astype(bf16)
        grads[rows, member(2)] = dv.astype(bf16)
        tick(j)
    grads[:, member(0)] = (dqa[...] * HD**-0.5).T.astype(bf16)


BOTH = (0, 1)
X, CORE, Y, Z1, Z2 = range(5)
DELAY = 2
SLOTS = 2 * DELAY
CHUNK = 64
SUBS = 4
QUADS = 4
WIDTH = 512
LEAD = 5
LINKS = (CORE, X, Y, Z1, Z2, Y, CORE, CORE)
CHUNKS = 4 * QUADS * SUBS
TICKS = CHUNKS + LEAD + 7 * DELAY
STEPS = 2 * QUADS
FEED_TICKS, CROSS_TICKS, SELF_TICKS, NORM_TICKS = 2, 3, 2, 4
CROSS_AT = STEPS * FEED_TICKS + NORM_TICKS
SELF_AT = CROSS_AT + STEPS * CROSS_TICKS + NORM_TICKS
DRAIN_AT = SELF_AT + STEPS * SELF_TICKS
TILE = 256
NORM_TILE = 128
dma_sem = pltpu.SemaphoreType.DMA


def partner(bit):
    d = lax.axis_index("dp")
    t = lax.axis_index("tensor")
    if bit == 0:
        return (d, 1 - t)
    size = 2 ** (bit - 1)
    return (d + size * (1 - 2 * ((d // size) % 2)), t)


def greet():
    barrier = pltpu.get_barrier_semaphore()
    for bit in range(5):
        pl.semaphore_signal(barrier, inc=1, device_id=partner(bit), device_id_type=pl.DeviceIdType.MESH)
    pl.semaphore_wait(barrier, 5)


def remote_copy(src, dst, send, recv, bit):
    return pltpu.make_async_remote_copy(
        src_ref=src,
        dst_ref=dst,
        send_sem=send,
        recv_sem=recv,
        device_id=partner(bit),
        device_id_type=pl.DeviceIdType.MESH,
    )


def stream_scratch():
    return [
        pltpu.VMEM((2, SLOTS, 2, 2, CHUNK, WIDTH), bf16),
        pltpu.VMEM((3, SLOTS, 2, CHUNK, WIDTH), bf16),
        pltpu.VMEM((6, SLOTS, CHUNK, WIDTH), bf16),
        dma_sem((8, SLOTS)),
        dma_sem((8, SLOTS)),
        dma_sem((2, SLOTS)),
    ]


def stream_stage(stage, c, queue, out, pairs, wide, narrow, send, recv, local):
    d = lax.axis_index("dp")
    core = d % 2
    y = (d // 2) % 2
    slot = lax.rem(c, SLOTS)
    block = c // SUBS
    sub = lax.rem(c, SUBS)
    away, came, own = [wide.at[i, slot] for i in range(3)]
    got_y, s3, got_z, s4, got_zz, s5 = [narrow.at[i, slot] for i in range(6)]

    def remote(k):
        src, dst = (
            (queue.at[block, :, 1 - core, :, sub], pairs.at[0, slot]),
            (away, came),
            (own.at[1 - y], got_y),
            (s3, got_z),
            (s4, got_zz),
            (s5, out.at[block, core, y, sub]),
            (s5, out.at[block, core, y, sub]),
            (out.at[block, core, 1 - y, sub], out.at[block, core, 1 - y, sub]),
        )[k]
        return remote_copy(src, dst, send.at[k, slot], recv.at[k, slot], LINKS[k])

    def load():
        return pltpu.make_async_copy(queue.at[block, :, core, :, sub], pairs.at[1, slot], local.at[0, slot])

    def keep():
        return pltpu.make_async_copy(s5, out.at[block, core, y, sub], local.at[1, slot])

    if stage == 0:
        remote(0).start()
        load().start()
    elif stage == 1:
        remote(0).wait()
        load().wait()
        away[...] = pairs[1, slot, 1] + pairs[0, slot, 1]
        remote(1).start()
        own[...] = pairs[1, slot, 0] + pairs[0, slot, 0]
    elif stage == 2:
        remote(1).wait()
        own[...] = own[...] + came[...]
        remote(2).start()
    elif stage == 3:
        remote(2).wait()
        s3[...] = wide[2, slot, y] + got_y[...]
        remote(3).start()
    elif stage == 4:
        remote(3).wait()
        s4[...] = s3[...] + got_z[...]
        remote(4).start()
    elif stage == 5:
        remote(4).wait()
        s5[...] = s4[...] + got_zz[...]
        remote(5).start()
        remote(6).start()
        keep().start()
    elif stage == 6:
        remote(5).wait()
        remote(6).wait()
        keep().wait()
        remote(7).start()
    else:
        remote(7).wait()


def small_scratch(shape):
    return [pltpu.VMEM((6,) + shape, f32), pltpu.VMEM((5,) + shape, f32), dma_sem((5,)), dma_sem((5,))]


def small_stage(k, out, acc, got, send, recv):
    def remote(i):
        return remote_copy(acc.at[i], got.at[i], send.at[i], recv.at[i], i)

    if k > 0:
        remote(k - 1).wait()
        acc[k] = acc[k - 1] + got[k - 1]
    if k < 5:
        remote(k).start()
    else:
        out[...] = acc[5]


def norm_step(index, more, weights, gain_ref, sum_ref, total, dc, left, acc, zt, sems, tick):
    def fetch_tile(a):
        slot = lax.rem(a, 2)
        rows = pl.ds(pl.multiple_of(a * NORM_TILE, NORM_TILE), NORM_TILE)
        return pltpu.make_async_copy(sum_ref.at[rows], zt.at[slot], sems.at[slot])

    tiles = total.shape[0] // NORM_TILE
    fetch_tile(0).start()

    @pl.loop(0, tiles)
    def _(a):
        rows = pl.ds(pl.multiple_of(a * NORM_TILE, NORM_TILE), NORM_TILE)
        fetch_tile(a).wait()

        @pl.when(a + 1 < tiles)
        def _():
            fetch_tile(a + 1).start()

        z = zt[lax.rem(a, 2)]
        dh = total[rows, :]
        for x, w in more:
            dh = dh + dot(x[rows, :], w[...], NT)
        centered = z - jnp.mean(z, axis=1, keepdims=True)
        r = lax.rsqrt(jnp.mean(centered * centered, axis=1, keepdims=True) + norm_eps)
        n = centered * r
        acc[0, index : index + 1, :] = acc[0, index : index + 1, :] + jnp.sum(dh * n, axis=0, keepdims=True)
        acc[0, 3 + index : 4 + index, :] = acc[0, 3 + index : 4 + index, :] + jnp.sum(dh, axis=0, keepdims=True)
        e = dh * gain_ref[index : index + 1, :]
        dz = r * (e - jnp.mean(e, axis=1, keepdims=True) - n * jnp.mean(e * n, axis=1, keepdims=True))
        total[rows, :] = alpha_res * dz
        g = dz.astype(bf16)
        left[:, rows] = g.T
        for i in BOTH:
            dc[i, rows, :] = dot(g, weights[i][...], NT).astype(bf16)
        pl.when(lax.rem(a, 2) == 1)(lambda: tick(a // 2))


def back_kernel(*refs):
    refs = list(refs)
    take = lambda n: [refs.pop(0) for _ in range(n)]
    (len_ref,) = take(1)
    cross_in = [take(5) for _ in BOTH]
    self_in = [take(5) for _ in BOTH]
    co = take(2)
    gain_ref, small_ref = take(2)
    feed_in = [take(4) for _ in BOTH]
    g3_ref, g3t_ref, h2t_ref, h1t_ref, memt_ref, tart_ref, base_ref, sum2_ref, sum1_ref = take(9)
    cq_in, so_in, kv_in, qkv_in = take(2), take(2), take(2), take(2)
    dmem_ref, dtar_ref, out, queue, small_out = take(5)
    grads, *scratch = take(9)
    stream = [queue, out] + take(6)
    small_refs = [small_out] + take(4)
    acc = small_refs[1]
    lefts, tall, flat, total, ends, dc, zt, staged = take(8)
    left_sems, feed_sems, zt_sems, staged_sems, base_sem = take(5)
    step = pl.program_id(0)
    half = lax.rem(step, 2)
    pair = lax.rem(step // 2, QUADS)

    def tick(t):
        for stage in range(7, -1, -1):
            c = t - LEAD - DELAY * stage
            pl.when((c >= 0) & (c < CHUNKS))(functools.partial(stream_stage, stage, c, *stream))

    def load_left(i, ref):
        return pltpu.make_async_copy(ref, lefts.at[i], left_sems.at[i])

    def load_feed(i, j):
        cols_j = pl.ds(pl.multiple_of(j * WIDTH, WIDTH), WIDTH)
        act, slope, up, down = feed_in[i]
        return [
            pltpu.make_async_copy(act.at[:, cols_j], tall.at[0, i], feed_sems.at[0, i]),
            pltpu.make_async_copy(slope.at[:, cols_j], tall.at[1, i], feed_sems.at[1, i]),
            pltpu.make_async_copy(up.at[:, cols_j], tall.at[2, i], feed_sems.at[2, i]),
            pltpu.make_async_copy(down.at[cols_j], flat.at[i], feed_sems.at[3, i]),
        ]

    def load_late():
        return [
            copy
            for i in BOTH
            for copy in (
                pltpu.make_async_copy(kv_in[i].at[0], tall.at[0, i], feed_sems.at[0, i]),
                pltpu.make_async_copy(kv_in[i].at[1], tall.at[1, i], feed_sems.at[1, i]),
                pltpu.make_async_copy(cq_in[i], tall.at[2, i], feed_sems.at[2, i]),
                pltpu.make_async_copy(so_in[i], flat.at[i], feed_sems.at[3, i]),
            )
        ]

    def load_last():
        return [pltpu.make_async_copy(qkv_in[i].at[m], tall.at[m, i], feed_sems.at[m, i]) for i in BOTH for m in range(3)]

    def input_grad(rows, members, start):
        for m in range(members):
            for i in BOTH:
                term = dot(ends[m, i, rows, :], tall[m, i], NT)
                start = term if start is None else start + term
        lefts[1, rows, :] = start.astype(bf16)

    def send_grad(ref):
        return pltpu.make_async_copy(lefts.at[1], ref, base_sem)

    def post(slot, block, i):
        return pltpu.make_async_copy(staged.at[slot], queue.at[block, i], staged_sems.at[slot])

    def posted():
        for slot in range(2):
            post(slot, 0, 0).wait()

    def feed_product(slot, block, left, right):
        result = dot(lefts[left], right[:, :WIDTH])
        staged[slot] = result.astype(bf16).reshape(2, 2, SUBS, CHUNK, WIDTH)
        post(slot, block, half).start()

    def pair_products(block, spans):
        for left, first, last in spans:
            result = dot(lefts[left], grads[:, 256 * first : 256 * last]).astype(bf16)
            for m in range(first, last):
                for i in BOTH:
                    at = 256 * (m - first) + 128 * i
                    piece = result[:, at : at + 128].reshape(2, 2, SUBS, CHUNK, 128)
                    staged[i, :, :, :, :, 128 * m : 128 * (m + 1)] = piece
        for i in BOTH:
            post(i, block, i).start()

    @pl.when(step == 0)
    def _():
        for copy in load_feed(0, 0) + [load_left(i, r) for i, r in enumerate((g3t_ref, h2t_ref, g3_ref))]:
            copy.start()
        base = pltpu.make_async_copy(base_ref, total, base_sem)
        base.start()
        acc[0] = small_ref[...]
        greet()
        for copy in [load_left(i, r) for i, r in enumerate((g3t_ref, h2t_ref, g3_ref))]:
            copy.wait()
        base.wait()

    @pl.when(step < STEPS)
    def _():
        t = step * FEED_TICKS
        for i in BOTH:

            @pl.when(half == i)
            def _(i=i):
                for copy in load_feed(i, pair):
                    copy.wait()

                @pl.when(step < STEPS - 1)
                def _():
                    for copy in load_feed(1 - i, pair + i):
                        copy.start()

        du = dot(lefts[2], flat[half], NT) * tall[1, half].astype(f32)
        grads[:, :WIDTH] = du.astype(bf16)
        @pl.when(step > 0)
        def _():
            post(0, 0, 0).wait()

        feed_product(0, 2 * pair, 0, tall.at[0, half])
        tick(t)
        for a in range(2):
            rows = slice(2 * a * TILE, 2 * (a + 1) * TILE)
            total[rows, :] += dot(grads[rows, :WIDTH], tall[2, half], NT)

        @pl.when(step > 0)
        def _():
            post(1, 0, 0).wait()

        feed_product(1, 2 * pair + 1, 1, grads)
        tick(t + 1)

    @pl.when(step == STEPS)
    def _():
        fetch = [load_left(0, h1t_ref), load_left(1, memt_ref)]
        for copy in fetch + load_late():
            copy.start()
        norm_step(
            1, [], co, gain_ref, sum2_ref, total, dc, lefts.at[2], acc, zt, zt_sems, lambda k: tick(STEPS * FEED_TICKS + k)
        )
        for copy in fetch:
            copy.wait()
        posted()

    at = pl.ds(pl.multiple_of(pair * 128, 128), 128)

    def member(m):
        return pl.ds(pl.multiple_of(256 * m + 128 * half, 128), 128)


    @pl.when((step >= STEPS) & (step < 2 * STEPS))
    def _():
        t = CROSS_AT + (step - STEPS) * CROSS_TICKS
        q2, k2, v2, c2, aug = [jnp.where(half == 0, a[...], b[...]) for a, b in zip(*cross_in)]

        def ticks(j):
            if j % 2 == 1:
                tick(t + j // 2)

        back_pair(False, len_ref[0], q2, k2, v2, c2, aug, dc[half, :, at], grads, member, scratch, ticks)
        for m, k in ((0, 2), (1, 0), (2, 1)):
            ends[k, half, :, at] = grads[:, member(m)]

        @pl.when((half == 0) & (step > STEPS))
        def _():
            posted()

        @pl.when(half == 1)
        def _():
            pair_products(2 * QUADS + pair, ((0, 0, 1), (1, 1, 3), (2, 3, 4)))

        tick(t + 2)

    @pl.when(step == 2 * STEPS)
    def _():
        fetch = load_left(0, tart_ref)
        fetch.start()
        for copy in load_late():
            copy.wait()
        more = [(ends.at[2, i], tall.at[2, i]) for i in BOTH]
        so = [flat.at[i] for i in BOTH]
        norm_step(
            0, more, so, gain_ref, sum1_ref, total, dc, lefts.at[2], acc, zt, zt_sems, lambda k: tick(SELF_AT - NORM_TICKS + k)
        )
        fetch.wait()

        @pl.loop(0, 4)
        def _(a):
            input_grad(pl.ds(pl.multiple_of(a * TILE, TILE), TILE), 2, None)

        send_grad(dmem_ref).start()
        for copy in load_last():
            copy.start()

    @pl.when(step >= 2 * STEPS)
    def _():
        t = SELF_AT + (step - 2 * STEPS) * SELF_TICKS
        q2, k2, v2, c2, aug = [jnp.where(half == 0, a[...], b[...]) for a, b in zip(*self_in)]
        def ticks(j):
            if j == 0:
                tick(t)

        back_pair(True, 0, q2, k2, v2, c2, aug, dc[half, :, at], grads, member, scratch, ticks)
        for m in range(3):
            ends[m, half, :, at] = grads[:, member(m)]

        @pl.when(half == 0)
        def _():
            posted()

        @pl.when(half == 1)
        def _():
            pair_products(3 * QUADS + pair, ((0, 0, 3), (2, 3, 4)))

        tick(t + 1)
        for k in range(5, -1, -1):
            pl.when(step == 2 * STEPS + 1 + k)(functools.partial(small_stage, k, *small_refs))

    @pl.when(step == 3 * STEPS - 1)
    def _():
        posted()
        send_grad(dmem_ref).wait()
        for copy in load_last():
            copy.wait()

        @pl.loop(0, 4)
        def _(a):
            tick(DRAIN_AT + a)
            rows = pl.ds(pl.multiple_of(a * TILE, TILE), TILE)
            input_grad(rows, 3, total[rows, :])

        send_grad(dtar_ref).start()
        pl.loop(DRAIN_AT + 4, TICKS)(tick)
        send_grad(dtar_ref).wait()


def layer_back(length, cross_in, self_in, weights, gain, small, feed_in, rest):
    seq, width = cross_in[0][0].shape
    model = gain.shape[1]
    early = lambda s: jnp.clip(s - STEPS, 0, STEPS - 1)
    late = lambda s: jnp.clip(s - 2 * STEPS, 0, STEPS - 1)
    cross_spec = pl.BlockSpec((seq, 128), lambda s: (0, early(s) // 2))
    self_spec = pl.BlockSpec((seq, 128), lambda s: (0, late(s) // 2))
    anywhere = pl.BlockSpec(memory_space=pl.ANY)
    full = lambda x: pl.BlockSpec(x.shape, lambda s: (0, 0), pipeline_mode=pl.Buffered(1))
    shape = jax.ShapeDtypeStruct
    vmem = pltpu.VMEM
    blocks = 4 * QUADS
    return pl.pallas_call(
        back_kernel,
        grid=(3 * STEPS,),
        in_specs=[pl.BlockSpec(memory_space=pltpu.SMEM)]
        + [cross_spec] * 10
        + [self_spec] * 10
        + [full(x) for x in (*weights, gain, small)]
        + [anywhere] * 25,
        out_specs=[anywhere] * 4 + [full(small)],
        out_shape=[shape((seq, model), bf16)] * 2
        + [
            shape((blocks, 2, 2, SUBS, CHUNK, WIDTH), bf16),
            shape((blocks, 2, 2, 2, SUBS, CHUNK, WIDTH), bf16),
            shape(small.shape, f32),
        ],
        scratch_shapes=[vmem((seq, 2 * WIDTH), bf16)]
        + back_scratch(seq)
        + stream_scratch()
        + small_scratch(small.shape)
        + [
            vmem((3, model, seq), bf16),
            vmem((3, 2, seq, WIDTH), bf16),
            vmem((2, WIDTH, model), bf16),
            vmem((seq, model), f32),
            vmem((3, 2, seq, width), bf16),
            vmem((2, seq, width), bf16),
            vmem((2, NORM_TILE, model), f32),
            vmem((2, 2, 2, SUBS, CHUNK, WIDTH), bf16),
            dma_sem((3,)),
            dma_sem((4, 2)),
            dma_sem((2,)),
            dma_sem((2,)),
            dma_sem,
        ],
        compiler_params=pltpu.CompilerParams(
            collective_id=1, has_side_effects=True, vmem_limit_bytes=62 * 2**20
        ),
        cost_estimate=cost(16, 8, seq, False),
        name="layer_back",
    )(length, *cross_in[0], *cross_in[1], *self_in[0], *self_in[1], *weights, gain, small, *feed_in[0], *feed_in[1], *rest)


ALL = ("dp", "tensor")
DEVICES = 32


def swap(x, flip):
    return lax.ppermute(x, ALL, [(i, i ^ flip) for i in range(DEVICES)])


def swap_tensor(x):
    return swap(x, 1)


def swap_core(x):
    return swap(x, 2)


def swap_y(x):
    return swap(x, 4)


def my_block():
    d = lax.axis_index("dp")
    return 2 * (d % 2) + (d // 2) % 2


def add_low(*terms):
    return sum(t.astype(f32) for t in terms).astype(bf16)


def blocks_of(own, axis):
    size = own.shape[axis] // 4
    return [lax.dynamic_slice_in_dim(own, (my_block() ^ j) * size, size, axis) for j in range(4)]


def swap_pieces(x, move):
    return [move(p) for p in x] if isinstance(x, (list, tuple)) else move(x)


def tie(*xs):
    return lax.optimization_barrier(xs)


class Pipe:
    def __init__(self):
        self.live = []

    def put(self, gen):
        wait, arrays = next(gen)
        self.live.append([gen, wait, arrays])

    def step(self, due, landed):
        done = 0
        for item in due:
            arrays = landed[done : done + len(item[2])]
            done += len(item[2])
            try:
                item[1], item[2] = item[0].send(arrays)
            except StopIteration:
                self.live.remove(item)

    def cut(self, *xs):
        due = []
        for item in self.live:
            item[1] -= 1
            if item[1] <= 0:
                due.append(item)
        tied = tie(*xs, *[a for item in due for a in item[2]])
        self.step(due, tied[len(xs) :])
        return tied[: len(xs)] if len(xs) > 1 else tied[0]

    def drain(self):
        while self.live:
            self.step(list(self.live), [a for item in self.live for a in item[2]])


def fetch(out, key, block, waits):
    far = swap_tensor(block)
    (far,) = yield waits[0], [far]
    side = swap_y(far)
    near = swap_core(far)
    side, near = yield waits[1], [side, near]
    out[key] = [far, side, near, swap_core(side)]
    return


def ffn_kernel(h_ref, up_ref, down_ref, a_ref, d_ref, b_ref):
    h = h_ref[...]
    size = 512
    total = None
    for j in range(4):
        cols = slice(j * size, (j + 1) * size)
        u = dot(h, up_ref[:, cols])
        cdf = 0.5 + 0.5 * lax.erf(u * (0.5**0.5))
        slope = cdf + u * (jnp.exp(-0.5 * u * u) * 0.3989422804014327)
        act = (u * cdf).astype(bf16)
        a_ref[:, cols] = act
        d_ref[:, cols] = slope.astype(bf16)
        term = dot(act, down_ref[cols, :])
        total = term if total is None else total + term
    b_ref[...] = total


def whole(x):
    return pl.BlockSpec(x.shape, lambda r: (0, 0))


ROWS = 512


def ffn_forward(h, up, down):
    seq, width = h.shape
    units = up.shape[1]
    rows = lambda w: pl.BlockSpec((ROWS, w), lambda r: (r, 0))
    return pl.pallas_call(
        ffn_kernel,
        grid=(seq // ROWS,),
        in_specs=[rows(width)] + [whole(up), whole(down)],
        out_specs=[rows(units), rows(units), rows(width)],
        out_shape=[jax.ShapeDtypeStruct((seq, units), bf16)] * 2 + [jax.ShapeDtypeStruct((seq, width), f32)],
        compiler_params=pltpu.CompilerParams(vmem_limit_bytes=50 * 2**20),
        cost_estimate=pl.CostEstimate(flops=4 * seq * width * units, bytes_accessed=22 * 2**20, transcendentals=2 * seq * units),
        name="feed_forward",
    )(h, up, down)


def arrange_kernel(me_ref, *refs):
    for j in range(4):

        @pl.when(pl.program_id(0) == j)
        def _(j=j):
            refs[4][...] = refs[j][...]


def arrange(slabs):
    members, rows, width = slabs[0].shape
    return pl.pallas_call(
        arrange_kernel,
        grid_spec=pltpu.PrefetchScalarGridSpec(
            num_scalar_prefetch=1,
            grid=(4,),
            in_specs=[pl.BlockSpec((members, rows, width), lambda j, me: (0, 0, 0))] * 4,
            out_specs=pl.BlockSpec((members, rows, width), lambda j, me: (0, j ^ me[0], 0)),
        ),
        out_shape=jax.ShapeDtypeStruct((members, 4 * rows, width), bf16),
        compiler_params=pltpu.CompilerParams(vmem_limit_bytes=40 * 2**20),
        cost_estimate=pl.CostEstimate(flops=0, bytes_accessed=16 * members * rows * width, transcendentals=0),
        name="arrange",
    )(my_block().reshape(1), *slabs)


def slab_of(own):
    rows = own.shape[1] // 4
    return lax.dynamic_slice_in_dim(own, my_block() * rows, rows, 1)


def spread_kernel(spans, x_ref, *out_refs):
    for lo, hi, k, m in spans:
        x = x_ref[:, lo:hi].astype(f32)
        if m is None:
            out_refs[k][...] = x.T
        else:
            out_refs[k][m] = x


def spread(pairs, first, spans, outs):
    _, rows, width = pairs.shape
    tile = 512
    specs = []
    shapes = []
    for members in outs:
        if members is None:
            specs.append(pl.BlockSpec((128, tile), lambda p, t: (p, t)))
            shapes.append(jax.ShapeDtypeStruct((512, rows), f32))
        else:
            specs.append(pl.BlockSpec((members, tile, 128), lambda p, t: (0, t, p)))
            shapes.append(jax.ShapeDtypeStruct((members, rows, 512), f32))
    return pl.pallas_call(
        functools.partial(spread_kernel, spans),
        grid=(4, rows // tile),
        in_specs=[pl.BlockSpec((None, tile, width), lambda p, t: (p + first, t, 0))],
        out_specs=specs,
        out_shape=shapes,
        compiler_params=pltpu.CompilerParams(vmem_limit_bytes=40 * 2**20),
        cost_estimate=pl.CostEstimate(flops=0, bytes_accessed=24 * rows * width, transcendentals=0),
        name="spread",
    )(pairs)


def flip_kernel(x_ref, out_ref):
    out_ref[...] = x_ref[...].T


def flip(x):
    rows, width = x.shape
    return pl.pallas_call(
        flip_kernel,
        grid=(4,),
        in_specs=[pl.BlockSpec((rows // 4, width), lambda i: (i, 0))],
        out_specs=pl.BlockSpec((width, rows // 4), lambda i: (0, i)),
        out_shape=jax.ShapeDtypeStruct((width, rows), x.dtype),
        cost_estimate=pl.CostEstimate(flops=0, bytes_accessed=4 * rows * width, transcendentals=0),
        name="flip",
    )(x)


def spread_feed_kernel(x_ref, down_ref, up_ref):
    even = lax.rem(pl.program_id(0), 2) == 0

    @pl.when(even)
    def _():
        down_ref[...] = x_ref[...].astype(f32).T

    @pl.when(jnp.logical_not(even))
    def _():
        up_ref[...] = x_ref[...].astype(f32)


def spread_feed(blocks):
    _, rows, width = blocks.shape
    return pl.pallas_call(
        spread_feed_kernel,
        grid=(8,),
        in_specs=[pl.BlockSpec((None, rows, width), lambda b: (b, 0, 0))],
        out_specs=[
            pl.BlockSpec((width, rows), lambda b: (b // 2, 0)),
            pl.BlockSpec((rows, width), lambda b: (0, b // 2)),
        ],
        out_shape=[jax.ShapeDtypeStruct((4 * width, rows), f32), jax.ShapeDtypeStruct((rows, 4 * width), f32)],
        compiler_params=pltpu.CompilerParams(vmem_limit_bytes=40 * 2**20),
        cost_estimate=pl.CostEstimate(flops=0, bytes_accessed=48 * rows * width, transcendentals=0),
        name="spread_feed",
    )(blocks)


def one_pair_each(
    target,
    memory,
    mem_len,
    grad_out,
    self_qkv,
    self_out,
    cross_query,
    cross_kv,
    cross_out,
    ffn_up,
    ffn_down,
    ln_gain,
    ln_bias,
):
    length = lax.dynamic_slice_in_dim(mem_len, lax.axis_index("tensor"), 1)
    pipe = Pipe()
    got = {}
    so3, cq3, co3 = self_out[None], cross_query[None], cross_out[None]

    pipe.put(fetch(got, "qkv", slab_of(self_qkv), (1, 1)))
    q1 = [[dot(target, self_qkv[m]).astype(bf16) for m in range(3)], None]
    at1 = [attend_fwd(*q1[0], length, True), None]
    so_s, cq_s, kv_s, co_s = [slab_of(x) for x in (so3, cq3, cross_kv, co3)]
    mem, so_s, cq_s, kv_s, _ = pipe.cut(memory, so_s, cq_s, kv_s, at1[0][0])
    pipe.put(fetch(got, "so", so_s, (1, 1)))
    pipe.put(fetch(got, "kv", jnp.concatenate([kv_s, cq_s]), (1, 1)))
    kv = [[dot(mem, cross_kv[m]).astype(bf16) for m in range(2)], None]
    up_s, down_s = slab_of(ffn_up[None]), slab_of(ffn_down[None])
    target_t = flip(target)
    memory_t = flip(mem)
    kv[0][0], up_s, co_s, target_t, memory_t = tie(kv[0][0], up_s, co_s, target_t, memory_t)
    tar, kv[0][0], kv[0][1], target_t, memory_t = pipe.cut(target, *kv[0], target_t, memory_t)
    qkv_oth = arrange(got["qkv"])
    q1[1] = [dot(tar, qkv_oth[m]).astype(bf16) for m in range(3)]
    pipe.put(fetch(got, "co", co_s, (1, 1)))
    q1[1][0], up_s = tie(q1[1][0], up_s)
    pipe.put(fetch(got, "up", up_s, (2, 1)))
    at1[1] = attend_fwd(*q1[1], length, True)
    at1[1], _ = tie(at1[1], at1[1][0])
    c1_oth = pipe.cut(at1[1][0])
    c1 = [at1[0][0], c1_oth]
    so_oth = arrange(got["so"])[0]
    b1 = dot(c1[0], self_out) + dot(c1[1], so_oth)
    sum1 = alpha_res * target.astype(f32) + b1
    h1 = norm_rows(sum1, ln_gain[0], ln_bias[0])
    h1_low = h1.astype(bf16)
    kv_oth = arrange(got["kv"])
    cq_oth = kv_oth[2]
    q2 = [dot(h1_low, cross_query).astype(bf16), dot(h1_low, cq_oth).astype(bf16)]
    kv[1] = [dot(memory, kv_oth[m]).astype(bf16) for m in range(2)]
    q2[0], kv[1][0], down_s = pipe.cut(q2[0], kv[1][0], down_s)
    pipe.put(fetch(got, "down", down_s, (1, 1)))
    at2 = [attend_fwd(q2[0], *kv[0], length, False), None]
    h1_again, _ = tie(h1_low, at2[0][0])
    h1_t = flip(h1_again)
    q2[1], h1_t, _ = pipe.cut(q2[1], h1_t, at2[0][0])
    at2[1] = attend_fwd(q2[1], *kv[1], length, False)
    co_oth = arrange(got["co"])[0]
    c2 = [at2[0][0], at2[1][0]]
    c2[1] = pipe.cut(c2[1])
    b2 = dot(c2[0], cross_out) + dot(c2[1], co_oth)
    sum2 = alpha_res * h1 + b2
    h2 = norm_rows(sum2, ln_gain[1], ln_bias[1])
    h2_low = h2.astype(bf16)
    act0, slope0, b3 = ffn_forward(h2_low, ffn_up, ffn_down)
    h2_t = flip(h2_low)
    while "up" not in got or "down" not in got:
        act0 = pipe.cut(act0)
    h2_again, h1_t, h2_t, _ = tie(h2_low, h1_t, h2_t, act0)
    up_oth, down_oth = arrange(got["up"])[0], arrange(got["down"])[0]
    act1, slope1, b3b = ffn_forward(h2_again, up_oth, down_oth)
    result, back3 = jax.vjp(norm_rows, alpha_res * h2 + b3 + b3b, ln_gain[2], ln_bias[2])
    dz3, gain3, bias3 = back3(grad_out.astype(f32))
    g3 = dz3.astype(bf16)
    none = jnp.zeros_like(gain3)
    small = jnp.stack([none, none, gain3, none, none, bias3, none, none])
    dmem, dtar, blocks, _, small = layer_back(
        length,
        [[q2[i], *kv[i], c2[i], at2[i][1]] for i in BOTH],
        [[*q1[i], c1[i], at1[i][1]] for i in BOTH],
        (cross_out, co_oth),
        ln_gain,
        small,
        [(act0, slope0, ffn_up, ffn_down), (act1, slope1, up_oth, down_oth)],
        (g3, flip(g3), h2_t, h1_t, memory_t, target_t, alpha_res * dz3, sum2, sum1)
        + (cross_query, cq_oth, self_out, so_oth, cross_kv, kv_oth, self_qkv, qkv_oth),
    )
    blocks = blocks.reshape(16, 1024, 512)
    cq_total, kv_total, co_total = spread(
        blocks,
        8,
        ((0, 128, 0, 0), (128, 256, 1, 0), (256, 384, 1, 1), (384, 512, 2, None)),
        (1, 2, None),
    )
    qkv_total, so_total = spread(
        blocks,
        12,
        ((0, 128, 0, 0), (128, 256, 0, 1), (256, 384, 0, 2), (384, 512, 1, None)),
        (3, None),
    )
    down_total, up_total = spread_feed(blocks)
    return (
        result.astype(bf16),
        dtar,
        dmem,
        qkv_total,
        so_total,
        cq_total[0],
        kv_total,
        co_total,
        up_total,
        down_total,
        small[:3],
        small[3:6],
    )


def solution(mesh):
    placed = (
        P(("dp", "tensor"), None),
        P(("dp", "tensor"), None),
        P("dp"),
        P(("dp", "tensor"), None),
        P(None, None, "tensor"),
        P("tensor", None),
        P(None, "tensor"),
        P(None, None, "tensor"),
        P("tensor", None),
        P(None, "tensor"),
        P("tensor", None),
        P(),
        P(),
    )
    body = one_pair_each if mesh.shape["tensor"] == 2 and mesh.shape["dp"] == 16 else on_device
    return jax.shard_map(
        body,
        mesh=mesh,
        in_specs=placed,
        out_specs=(
            P(("dp", "tensor"), None),
            P(("dp", "tensor"), None),
            P(("dp", "tensor"), None),
            P(None, None, "tensor"),
            P("tensor", None),
            P(None, "tensor"),
            P(None, None, "tensor"),
            P("tensor", None),
            P(None, "tensor"),
            P("tensor", None),
            P(),
            P(),
        ),
        check_vma=False,
    )
```
